32 devices in a mesh: sx: 4 (over y, core), sy: 8 (over z, x).
Axes of the slice: x: 2, y: 2, z: 4, core: 2. Of those that a mesh axis runs over, the one named last changes fastest.
Arguments:
- loads: float32 [4, 8, 1536, 256], P('sx', 'sy')
- schur_flex: float32 [4, 8, 1536, 1536], P('sx', 'sy'), as said below
- dirichlet: float32 [4, 8, 1536, 1536], P('sx', 'sy'), as said below
- coupling: float32 [4, 8, 16, 1536], P('sx', 'sy'), may hold values from -0.3125 to 0.3125
- corner_index: int32 [4, 8, 16], P('sx', 'sy'), may hold values from 0 to 128, as said below
- face_lists: int32 [4, 8, 4, 384], P('sx', 'sy'), may hold values from 0 to 383, as said below
- coarse_inverse: float32 [128, 128], P(('sx', 'sy')), as said below
Outputs:
- multipliers: float32 [4, 8, 1536, 256], P('sx', 'sy')
- residual: float32 [4, 8, 1536, 256], P('sx', 'sy')
The draws below stay inside these ranges and needn't reach their ends.
Inputs may be any that keep to these rules, and one draw needn't show every extreme that they name: `corner_index`: each subdomain lists 4 coarse dofs for each of its four corners; 128 marks a corner on the clamped edges of the panel, which has no coarse dof; every coarse dof below 128 is named by some subdomain. `face_lists`: each face's list is a permutation of the 384 dofs of the facing face; the facing lists of two neighbouring subdomains are inverse permutations. `schur_flex`: symmetric positive definite for every subdomain. `dirichlet`: symmetric positive definite for every subdomain. `coarse_inverse`: symmetric positive definite.
All inputs are finite; a program needn't handle non-finite values.
Results may differ from the reference program's by a relative error of at most 0.00017.
Values sent between devices are 32-bit elements; how exact they have to be, the bound alone decides.
No kernel may reach another device: no remote copies, remote signals or barrier semaphores. Data moves between devices by JAX's collectives and lax.ppermute only.
A program may use at most 128 MiB of HBM per device.

```python
import math
import jax
import jax.numpy as jnp
from jax import lax

NI = 1536
LOADS = 256
CDOF = 4
ITERS = 2
FACE = 384
NCL = 16
GLOBAL_SYS_SIZE = 128
N_SX = 4
N_SY = 8


def spd_block(key, order):
    first, second = jax.random.split(key, 2)
    offdiag = jax.random.uniform(first, (order, order), jnp.float32, -1.0, 1.0) / math.sqrt(order)
    symmetric = 0.5 * (offdiag + offdiag.T)
    identity = jnp.eye(order, dtype=jnp.float32)
    diagonal = jax.random.uniform(second, (order,), jnp.float32, 1.05, 2.0)
    matrix = symmetric * (1.0 - identity) + identity * diagonal[:, None]
    return matrix


def interface_block(key):
    return spd_block(key, NI)


def spd_stack(key, salt):
    keys = jax.random.split(jax.random.fold_in(key, salt), N_SX * N_SY)
    return lax.map(interface_block, keys).reshape(N_SX, N_SY, NI, NI)


def draw_schur_flex(key, part):
    return spd_stack(key, 101)


def draw_dirichlet(key, part):
    return spd_stack(key, 202)


def draw_coarse_inverse(key, part):
    return spd_block(jax.random.fold_in(key, 303), GLOBAL_SYS_SIZE)


def draw_loads(key, part):
    first = jax.random.fold_in(jax.random.fold_in(key, 404), 0)
    devices = N_SX * N_SY
    position = jnp.arange(devices, dtype=jnp.float32).reshape(N_SX, N_SY, 1, 1) / (devices - 1)
    values = jax.random.normal(first, (N_SX, N_SY, NI, LOADS), jnp.float32)
    return values * (1.0 + 2.0 * position)


def inverse_perm(perm):
    return jnp.zeros(perm.shape, jnp.int32).at[perm].set(jnp.arange(perm.shape[0], dtype=jnp.int32))


def face_perm(key):
    return jax.random.permutation(key, FACE).astype(jnp.int32)


def draw_face_lists(key, part):
    keys = jax.random.split(jax.random.fold_in(key, 505), 2 * N_SX * N_SY)
    along_x = jax.vmap(face_perm)(keys[:N_SX * N_SY]).reshape(N_SX, N_SY, FACE)
    along_y = jax.vmap(face_perm)(keys[N_SX * N_SY:]).reshape(N_SX, N_SY, FACE)
    invert = jax.vmap(jax.vmap(inverse_perm))
    face_zero = invert(jnp.roll(along_x, 1, axis=0))
    face_two = invert(jnp.roll(along_y, 1, axis=1))
    return jnp.stack([face_zero, along_x, face_two, along_y], axis=2).astype(jnp.int32)


def draw_corner_index(key, part):
    relabel_unknowns = jax.random.permutation(jax.random.fold_in(key, 606), GLOBAL_SYS_SIZE).astype(jnp.int32)
    index_a = jnp.arange(N_SX, dtype=jnp.int32)[:, None, None]
    index_b = jnp.arange(N_SY, dtype=jnp.int32)[None, :, None]
    local = jnp.arange(NCL, dtype=jnp.int32)[None, None, :]
    junction_point = local // CDOF
    component = local % CDOF
    vertex_a = index_a + junction_point // 2
    vertex_b = index_b + junction_point % 2
    genuine_elements = (vertex_a < N_SX) & (vertex_b < N_SY)
    grid_node = (vertex_a * N_SY + vertex_b) * CDOF + component
    grid_node = jnp.minimum(grid_node, GLOBAL_SYS_SIZE - 1)
    return jnp.where(genuine_elements, relabel_unknowns[grid_node], GLOBAL_SYS_SIZE).astype(jnp.int32)


def steps_of(own_key, shape, pieces, low, top_value):
    gain = 1.0
    for axis_at, shards_of in pieces:
        heights = jax.random.uniform(jax.random.fold_in(jax.random.fold_in(own_key, 6), axis_at), (shards_of,), jnp.float32, low / len(pieces), top_value / len(pieces))
        gain = gain * jnp.repeat(jnp.exp(heights), shape[axis_at] // shards_of).reshape((-1,) + (1,) * (len(shape) - 1 - axis_at))
    return gain


def centred(stream_key, extent, scale, bound, pieces=(), kind=jnp.bfloat16):
    gain = steps_of(stream_key, extent, pieces, -0.22, 0.18) if pieces else 1.0
    drawn = jax.random.normal(stream_key, extent, jnp.float32) * scale * gain
    return jnp.minimum(jnp.maximum(drawn, -bound), bound).astype(kind)


def setup_inputs(seed: int = 0) -> dict:
    seeds = jax.random.split(jax.random.key(seed), 8)
    loads = draw_loads(jax.random.fold_in(seeds[7], 71), 0)
    schur_flex = draw_schur_flex(jax.random.fold_in(seeds[7], 71), 0)
    dirichlet = draw_dirichlet(jax.random.fold_in(seeds[7], 71), 0)
    coupling = centred(seeds[3], (N_SX, N_SY, NCL, NI), (NI // 4) ** -0.5, 0.3125, ((0, 4), (1, 8)), jnp.float32)
    corner_index = draw_corner_index(jax.random.fold_in(seeds[7], 71), 0)
    face_lists = draw_face_lists(jax.random.fold_in(seeds[7], 71), 0)
    coarse_inverse = draw_coarse_inverse(jax.random.fold_in(seeds[7], 71), 0)
    return dict(loads=loads, schur_flex=schur_flex, dirichlet=dirichlet, coupling=coupling, corner_index=corner_index, face_lists=face_lists, coarse_inverse=coarse_inverse)


def subdomain_product(pair):
    return jnp.dot(pair[0], pair[1], precision=lax.Precision.HIGHEST)


def batched_product(matrices, vectors):
    size = matrices.shape[2]
    final_result = lax.map(subdomain_product, (matrices.reshape(-1, size, size), vectors.reshape(-1, size, LOADS)))
    return final_result.reshape(N_SX, N_SY, size, LOADS)


def jump(field, face_lists):
    face_rows = field.reshape(N_SX, N_SY, 4, FACE, LOADS)
    zero_x = jnp.zeros((1, N_SY, FACE, LOADS), field.dtype)
    zero_y = jnp.zeros((N_SX, 1, FACE, LOADS), field.dtype)
    from_low_x = jnp.concatenate([zero_x, face_rows[:-1, :, 1]], axis=0)
    from_high_x = jnp.concatenate([face_rows[1:, :, 0], zero_x], axis=0)
    from_low_y = jnp.concatenate([zero_y, face_rows[:, :-1, 3]], axis=1)
    from_high_y = jnp.concatenate([face_rows[:, 1:, 2], zero_y], axis=1)
    received = jnp.stack([from_low_x, from_high_x, from_low_y, from_high_y], axis=2)
    index_a = jnp.arange(N_SX, dtype=jnp.int32)[:, None, None, None]
    index_b = jnp.arange(N_SY, dtype=jnp.int32)[None, :, None, None]
    index_f = jnp.arange(4, dtype=jnp.int32)[None, None, :, None]
    matched = received[index_a, index_b, index_f, face_lists]
    return (face_rows - matched).reshape(N_SX, N_SY, NI, LOADS)


def apply_dual(dual_vector, schur_flex, coupling, corner_index, face_lists, coarse_inverse):
    highest = lax.Precision.HIGHEST
    spread = jump(dual_vector, face_lists)
    fine_part = batched_product(schur_flex, spread)
    local_load = jnp.einsum("abki,abir->abkr", coupling, spread, precision=highest)
    coarse_rhs = jnp.zeros((GLOBAL_SYS_SIZE, LOADS), jnp.float32).at[corner_index.reshape(-1)].add(local_load.reshape(-1, LOADS), mode="drop")
    coarse_sol = jnp.dot(coarse_inverse, coarse_rhs, precision=highest)
    filled_out = jnp.concatenate([coarse_sol, jnp.zeros((1, LOADS), jnp.float32)], axis=0)
    picked = filled_out[corner_index]
    correction = jnp.einsum("abki,abkr->abir", coupling, picked, precision=highest)
    return jump(fine_part + correction, face_lists)


def precondition(dual_vector, dirichlet, face_lists):
    spread = jump(dual_vector, face_lists)
    operator_applied = batched_product(dirichlet, spread)
    return 0.5 * jump(operator_applied, face_lists)


def inner(first, second):
    return jnp.sum(first * second, axis=(0, 1, 2))


def reference(loads, schur_flex, dirichlet, coupling, corner_index, face_lists, coarse_inverse):
    force_discontinuity = jump(loads, face_lists)
    multipliers = jnp.zeros_like(force_discontinuity)
    residual = force_discontinuity
    precond = precondition(residual, dirichlet, face_lists)
    direction = precond
    residual_inner = inner(residual, precond)
    for iteration in range(ITERS):
        image = apply_dual(direction, schur_flex, coupling, corner_index, face_lists, coarse_inverse)
        step_size = residual_inner / inner(direction, image)
        multipliers = multipliers + step_size * direction
        residual = residual - step_size * image
        if iteration + 1 < ITERS:
            precond = precondition(residual, dirichlet, face_lists)
            new_dot = inner(residual, precond)
            direction = precond + (new_dot / residual_inner) * direction
            residual_inner = new_dot
    return multipliers, residual
```

```python
import jax
import jax.numpy as jnp
from jax import lax
from jax.sharding import PartitionSpec as P

AXES = ("sx", "sy")
HIGHEST = lax.Precision.HIGHEST
HIGH = lax.Precision.HIGH


def shifted(block, axis, distance):
    devices = range(lax.axis_size(axis))
    route = [(i - distance, i) for i in devices if i - distance in devices]
    return lax.ppermute(block, axis, route)


def facing(face_rows):
    return [
        shifted(face_rows[1], "sx", 1),
        shifted(face_rows[0], "sx", -1),
        shifted(face_rows[3], "sy", 1),
        shifted(face_rows[2], "sy", -1),
    ]


def parts_of(x):
    high = lax.reduce_precision(x, 8, 7)
    mid = lax.reduce_precision(x - high, 8, 7)
    low = x - high - mid
    return [part.astype(jnp.bfloat16) for part in (high, mid, low)]


def reorder(select, rows):
    out = None
    for part in parts_of(rows)[::-1]:
        term = jnp.dot(select, part, preferred_element_type=jnp.float32)
        out = term if out is None else out + term
    return out


def from_all(rows):
    count = lax.axis_size("sx") * lax.axis_size("sy")
    copies = jnp.broadcast_to(rows[None], (count,) + rows.shape)
    return lax.all_to_all(copies, AXES, 0, 0, tiled=True)


def shards(loads, schur_flex, dirichlet, coupling, corner_index, face_lists, coarse_inverse):
    flex_mat = schur_flex[0, 0]
    prec_mat = dirichlet[0, 0]
    coupling_mat = coupling[0, 0]
    corners = corner_index[0, 0]
    face_index = face_lists[0, 0]
    load = loads[0, 0]
    ncoarse = coarse_inverse.shape[1]
    ncl, ni = coupling_mat.shape
    width = load.shape[1]
    face = ni // 4
    n_sx, n_sy = lax.axis_size("sx"), lax.axis_size("sy")
    at_x, at_y = lax.axis_index("sx"), lax.axis_index("sy")

    has = jnp.stack([at_x > 0, at_x < n_sx - 1, at_y > 0, at_y < n_sy - 1])
    scale = jnp.repeat(jnp.where(has, 2.0, 1.0).astype(jnp.float32), face)[:, None]
    select = (face_index[:, :, None] == jnp.arange(face, dtype=jnp.int32)).astype(jnp.bfloat16)

    def jump(field):
        received = facing(field.reshape(4, face, width))
        matched = jnp.concatenate([reorder(select[f], received[f]) for f in range(4)], axis=0)
        return field - matched

    force_jump = jump(load)

    listed = jnp.zeros((1, ncoarse), jnp.float32).at[0, :ncl].set(corners.astype(jnp.float32))
    table = from_all(jnp.concatenate([coarse_inverse, listed], axis=0))
    matrix_all = table[:, :-1].reshape(ncoarse, ncoarse)
    corners_all = table[:, -1, :ncl].astype(jnp.int32)
    coarse_ids = jnp.arange(ncoarse, dtype=jnp.int32)
    gather_all = (corners_all.reshape(1, -1) == coarse_ids[:, None]).astype(jnp.float32)

    coupling_faces = coupling_mat.reshape(ncl, 4, face).transpose(1, 2, 0)
    coupling_near = facing(coupling_faces)
    me = at_x * n_sy + at_y
    near = [me - n_sy, me + n_sy, me - 1, me + 1]
    both_sides, both_corners = [], []
    for f in range(4):
        there = jnp.clip(near[f], 0, n_sx * n_sy - 1)
        theirs = -reorder(select[f], coupling_near[f])
        both_sides.append(jnp.concatenate([coupling_faces[f], theirs], axis=1))
        ids = jnp.concatenate([corners, corners_all[there]])
        both_corners.append((ids[:, None] == coarse_ids[None, :]).astype(jnp.float32))

    def correction(coarse_sol):
        return jnp.concatenate(
            [
                jnp.dot(both_sides[f], jnp.dot(both_corners[f], coarse_sol, precision=HIGHEST), precision=HIGHEST)
                for f in range(4)
            ],
            axis=0,
        )

    def inner(first, second):
        return jnp.sum(first * second, axis=0, keepdims=True)

    def reduced(coarse_part, dots):
        gathered = from_all(jnp.concatenate([coarse_part] + dots, axis=0))
        rhs = jnp.dot(gather_all, gathered[:, :ncl].reshape(-1, width), precision=HIGHEST)
        sol = jnp.dot(matrix_all, rhs, precision=HIGHEST)
        return rhs, sol, jnp.sum(gathered[:, ncl:], axis=0)

    residual = force_jump
    spread = scale * residual
    applied = jnp.dot(prec_mat, spread, precision=HIGH)
    rho0 = 0.5 * inner(spread, applied)
    direction = 0.5 * jump(applied)

    spread = scale * direction
    fine0 = jnp.dot(flex_mat, spread, precision=HIGH)
    coarse_part = jnp.dot(coupling_mat, spread, precision=HIGHEST)
    rhs0, sol0, dots = reduced(coarse_part, [rho0, inner(spread, fine0)])
    rho0, fine_dot0 = dots[0:1], dots[1:2]
    jump0 = jump(fine0)
    image = jump0 + correction(sol0)
    step0 = rho0 / (fine_dot0 + inner(rhs0, sol0))
    multipliers = step0 * direction
    residual = residual - step0 * image
    spread = scale * residual
    applied = jnp.dot(prec_mat, spread, precision=HIGH)
    rho1 = 0.5 * inner(spread, applied)
    precond = 0.5 * jump(applied)

    spread = scale * precond
    fine1 = jnp.dot(flex_mat, spread, precision=HIGH)
    coarse_part = jnp.dot(coupling_mat, spread, precision=HIGHEST)
    rhs1, sol1, dots = reduced(coarse_part, [rho1, inner(spread, fine1), inner(spread, fine0)])
    rho1, dot11, dot10 = dots[0:1], dots[1:2], dots[2:3]
    beta = rho1 / rho0
    rhs1 = rhs1 + beta * rhs0
    sol1 = sol1 + beta * sol0
    curve = dot11 + 2.0 * beta * dot10 + beta * beta * fine_dot0 + inner(rhs1, sol1)
    step1 = rho1 / curve
    image = jump(fine1) + beta * jump0 + correction(sol1)
    multipliers = multipliers + step1 * (precond + beta * direction)
    residual = residual - step1 * image
    return (multipliers[None, None], residual[None, None])


def solution(mesh):
    return jax.shard_map(
        shards,
        mesh=mesh,
        in_specs=(
            P("sx", "sy", None, None),
            P("sx", "sy", None, None),
            P("sx", "sy", None, None),
            P("sx", "sy", None, None),
            P("sx", "sy", None),
            P("sx", "sy", None, None),
            P(("sx", "sy"), None),
        ),
        out_specs=(P("sx", "sy", None, None), P("sx", "sy", None, None)),
        check_vma=False,
    )
```

```python
import jax
import jax.numpy as jnp
from jax import lax
from jax.sharding import PartitionSpec as P

HIGHEST = lax.Precision.HIGHEST
HIGH = lax.Precision.HIGH


def shifted(block, axis, distance):
    devices = range(lax.axis_size(axis))
    route = [(i - distance, i) for i in devices if i - distance in devices]
    return lax.ppermute(block, axis, route)


def facing(rows, axis):
    return [shifted(rows[1], axis, 1), shifted(rows[0], axis, -1)]


def parts_of(x):
    high = lax.reduce_precision(x, 8, 7)
    mid = lax.reduce_precision(x - high, 8, 7)
    low = x - high - mid
    return [part.astype(jnp.bfloat16) for part in (high, mid, low)]


def reorder(select, rows):
    out = None
    for part in parts_of(rows)[::-1]:
        term = jnp.dot(select, part, preferred_element_type=jnp.float32)
        out = term if out is None else out + term
    return out


def from_all(rows, axes):
    count = 1
    for axis in axes:
        count *= lax.axis_size(axis)
    copies = jnp.broadcast_to(rows[None], (count,) + rows.shape)
    return lax.all_to_all(copies, axes, 0, 0, tiled=True)


def inner(first, second):
    return sum(jnp.sum(a * b, axis=0, keepdims=True) for a, b in zip(first, second))


def shards(loads, schur_flex, dirichlet, coupling, corner_index, face_lists, coarse_inverse):
    flex_mat = schur_flex[0, 0]
    prec_mat = dirichlet[0, 0]
    coupling_mat = coupling[0, 0]
    corners = corner_index[0, 0]
    face_index = face_lists[0, 0]
    load = loads[0, 0]
    ncoarse = coarse_inverse.shape[1]
    ncl, ni = coupling_mat.shape
    width = load.shape[1]
    face, half = ni // 4, ni // 2
    n_sx, n_sy = lax.axis_size("sx"), lax.axis_size("sy")
    at_x, at_y = lax.axis_index("sx"), lax.axis_index("sy")

    has = jnp.stack([at_x > 0, at_x < n_sx - 1, at_y > 0, at_y < n_sy - 1])
    scale = jnp.repeat(jnp.where(has, 2.0, 1.0).astype(jnp.float32), face)[:, None]
    scales = (scale[:half], scale[half:])
    select = (face_index[:, :, None] == jnp.arange(face, dtype=jnp.int32)).astype(jnp.bfloat16)

    def received(rows, at, axis):
        both = facing((rows[:face], rows[face:]), axis)
        return jnp.concatenate([reorder(select[at + f], both[f]) for f in range(2)], axis=0)

    def jump(field):
        far = received(field[1], 2, "sy")
        close = received(field[0], 0, "sx")
        return field[0] - close, field[1] - far

    def scaled(field):
        return scales[0] * field[0], scales[1] * field[1]

    def product(matrix, spread, extra=None):
        early = jnp.dot(matrix[:, :half], spread[0], precision=HIGH)
        out_y = early[half:] + jnp.dot(matrix[half:, half:], spread[1], precision=HIGH)
        if extra is not None:
            out_y = out_y + extra[half:]
        late, out_y = lax.optimization_barrier((spread[1], out_y))
        out_x = early[:half] + jnp.dot(matrix[:half, half:], late, precision=HIGH)
        if extra is not None:
            out_x = out_x + extra[:half]
        return out_x, out_y

    def both(fn, *fields):
        return tuple(fn(*pair) for pair in zip(*fields))

    residual0 = jump((load[:half], load[half:]))

    listed = jnp.zeros((1, ncoarse), jnp.float32).at[0, :ncl].set(corners.astype(jnp.float32))
    table = from_all(jnp.concatenate([coarse_inverse, listed], axis=0), ("sx", "sy"))
    matrix_all = table[:, :-1].reshape(ncoarse, ncoarse)
    corners_all = table[:, -1, :ncl].astype(jnp.int32)
    coarse_ids = jnp.arange(ncoarse, dtype=jnp.int32)

    rows = [coupling_mat[:, f * face : (f + 1) * face] for f in range(4)]
    coupling_near = facing(rows[:2], "sx") + facing(rows[2:], "sy")
    me = at_x * n_sy + at_y
    near = [me - n_sy, me + n_sy, me - 1, me + 1]
    own_pick = (corners[:, None] == coarse_ids[None, :]).astype(jnp.float32)
    lift = []
    for f in range(4):
        there = jnp.clip(near[f], 0, n_sx * n_sy - 1)
        near_pick = (corners_all[there][:, None] == coarse_ids[None, :]).astype(jnp.float32)
        theirs = reorder(select[f], coupling_near[f].T)
        lift.append(
            jnp.dot(rows[f].T, own_pick, precision=HIGHEST) - jnp.dot(theirs, near_pick, precision=HIGHEST)
        )
    lift = (jnp.concatenate(lift[:2], axis=0), jnp.concatenate(lift[2:], axis=0))
    lift_applied = jnp.dot(prec_mat, jnp.concatenate(scaled(lift), axis=0), precision=HIGH)
    gather_row = (
        lax.dynamic_slice_in_dim(corners_all, at_x * n_sy, n_sy, axis=0).reshape(1, -1) == coarse_ids[:, None]
    ).astype(jnp.float32)

    def reduced(spread, dots):
        coarse_part = jnp.dot(coupling_mat, jnp.concatenate(spread, axis=0), precision=HIGHEST)
        gathered = from_all(jnp.concatenate([coarse_part] + dots, axis=0), ("sy",))
        rhs = jnp.dot(gather_row, gathered[:, :ncl].reshape(-1, width), precision=HIGHEST)
        sums = jnp.sum(gathered[:, ncl:], axis=0)
        total = jnp.sum(from_all(jnp.concatenate([rhs, sums], axis=0), ("sx",)), axis=0)
        sol = jnp.dot(matrix_all, total[:ncoarse], precision=HIGHEST)
        return total[:ncoarse], sol, total[ncoarse:]

    def lifted(sol):
        return both(lambda part: jnp.dot(part, sol, precision=HIGHEST), lift)

    spread = scaled(residual0)
    applied0 = product(prec_mat, spread)
    rho0 = 0.5 * inner(spread, applied0)
    direction0 = both(lambda x: 0.5 * x, jump(applied0))

    spread = scaled(direction0)
    fine0 = product(flex_mat, spread)
    rhs0, sol0, dots = reduced(spread, [rho0, inner(spread, fine0)])
    jump0 = jump(fine0)
    image_applied = product(prec_mat, scaled(jump0), jnp.dot(lift_applied, sol0, precision=HIGH))
    image_jump = jump(image_applied)
    rho0, fine_dot0 = dots[0:1], dots[1:2]
    step0 = rho0 / (fine_dot0 + inner([rhs0], [sol0]))
    residual1 = both(lambda r, j, c: r - step0 * (j + c), residual0, jump0, lifted(sol0))
    applied1 = both(lambda z, y: z - step0 * y, applied0, image_applied)
    rho1 = 0.5 * inner(scaled(residual1), applied1)
    precond = both(lambda p, y: p - (0.5 * step0) * y, direction0, image_jump)

    spread = scaled(precond)
    fine1 = product(flex_mat, spread)
    rhs1, sol1, dots = reduced(spread, [rho1, inner(spread, fine1), inner(spread, fine0)])
    rho1, dot11, dot10 = dots[0:1], dots[1:2], dots[2:3]
    beta = rho1 / rho0
    rhs1 = rhs1 + beta * rhs0
    sol1 = sol1 + beta * sol0
    curve = dot11 + 2.0 * beta * dot10 + beta * beta * fine_dot0 + inner([rhs1], [sol1])
    step1 = rho1 / curve
    jump1 = jump(fine1)
    residual2 = both(
        lambda r, j, k, c: r - step1 * (j + beta * k + c), residual1, jump1, jump0, lifted(sol1)
    )
    multipliers = both(lambda d, p: (step0 + step1 * beta) * d + step1 * p, direction0, precond)
    return tuple(jnp.concatenate(out, axis=0)[None, None] for out in (multipliers, residual2))


def solution(mesh):
    return jax.shard_map(
        shards,
        mesh=mesh,
        in_specs=(
            P("sx", "sy", None, None),
            P("sx", "sy", None, None),
            P("sx", "sy", None, None),
            P("sx", "sy", None, None),
            P("sx", "sy", None),
            P("sx", "sy", None, None),
            P(("sx", "sy"), None),
        ),
        out_specs=(P("sx", "sy", None, None), P("sx", "sy", None, None)),
        check_vma=False,
    )
```

```python
import functools

import jax
import jax.numpy as jnp
from jax import lax
from jax.experimental import pallas as pl
from jax.experimental.pallas import tpu as pltpu
from jax.sharding import PartitionSpec as P

HIGHEST = lax.Precision.HIGHEST
HIGH = lax.Precision.HIGH
F32 = jnp.float32
BF16 = jnp.bfloat16
LIMIT = 40 * 1024 * 1024


def shifted(block, axis, distance):
    devices = range(lax.axis_size(axis))
    route = [(i - distance, i) for i in devices if i - distance in devices]
    return lax.ppermute(block, axis, route)


def facing(low, high, axis):
    return shifted(high, axis, 1), shifted(low, axis, -1)


def from_all(rows):
    count = lax.axis_size("sx") * lax.axis_size("sy")
    copies = jnp.broadcast_to(rows[None], (count,) + rows.shape)
    return lax.all_to_all(copies, ("sx", "sy"), 0, 0, tiled=True)


def split(x):
    high = x.astype(BF16)
    return high, (x - high.astype(F32)).astype(BF16)


def dot(a, b):
    return jnp.dot(a, b, preferred_element_type=F32)


def product(a, b_high, b_low):
    a_high, a_low = split(a)
    return dot(a_high, b_high) + (dot(a_high, b_low) + dot(a_low, b_high))


def permuted(select, rows):
    high = rows.astype(BF16)
    rest = rows - high.astype(F32)
    mid = rest.astype(BF16)
    low = (rest - mid.astype(F32)).astype(BF16)
    return dot(select, high) + (dot(select, mid) + dot(select, low))


def spread_into(at, refs, select, scale, coef, bases, outs, high, low):
    owns, nears = refs
    size = owns[0].shape[0]
    for f in range(2):
        value = coef[...] * (owns[f][...] - permuted(select[f], nears[f][:size]))
        if bases:
            value = bases[f][...] + value
        outs[f][...] = value
        high[f * size : (f + 1) * size], low[f * size : (f + 1) * size] = split(scale[at + f] * value)


def early_kernel(based, *refs):
    scale, mat, own0, own1, near0, near1, select, coef = refs[:8]
    bases, (out0, out1, partial, high, low) = refs[8 : 8 + 2 * based], refs[8 + 2 * based :]

    @pl.when(pl.program_id(0) == 0)
    def _():
        spread_into(0, ((own0, own1), (near0, near1)), select, scale, coef, bases, (out0, out1), high, low)

    partial[...] = product(mat[...], high[...], low[...])


def crit_kernel(based, extended, *refs):
    scale, mat, own2, own3, near2, near3, select, coef, partial = refs[:9]
    rest = refs[9:]
    bases, rest = rest[: 2 * based], rest[2 * based :]
    extra, rest = rest[:extended], rest[extended:]
    out2, out3, applied2, applied3, high, low = rest

    @pl.when(pl.program_id(0) == 0)
    def _():
        spread_into(2, ((own2, own3), (near2, near3)), select, scale, coef, bases, (out2, out3), high, low)

    value = partial[...] + product(mat[...], high[...], low[...])
    if extended:
        value = value + extra[0][...]
    for at, ref in enumerate((applied2, applied3)):

        @pl.when(pl.program_id(0) == at)
        def _(ref=ref):
            ref[...] = value


def late_kernel(extended, *refs):
    scale, mat, value2, value3, partial = refs[:5]
    extra, rest = refs[5 : 5 + extended], refs[5 + extended :]
    applied0, applied1, high, low = rest
    size = value2.shape[0]

    @pl.when(pl.program_id(0) == 0)
    def _():
        for f, ref in enumerate((value2, value3)):
            high[f * size : (f + 1) * size], low[f * size : (f + 1) * size] = split(scale[2 + f] * ref[...])

    value = partial[...] + product(mat[...], high[...], low[...])
    if extended:
        value = value + extra[0][...]
    for at, ref in enumerate((applied0, applied1)):

        @pl.when(pl.program_id(0) == at)
        def _(ref=ref):
            ref[...] = value


def tail_kernel(*refs):
    owns, nears, bases = refs[:4], refs[4:8], refs[8:12]
    select, coef, out = refs[12:]
    size = out.shape[0]
    for f in range(4):

        @pl.when(pl.program_id(0) == f)
        def _(f=f):
            out[...] = bases[f][...] + coef[...] * (owns[f][...] - permuted(select[0], nears[f][:size]))


def weighted_kernel(*refs):
    firsts, seconds = refs[:4], refs[4:8]
    first_coef, second_coef, out = refs[8:]
    for f in range(4):

        @pl.when(pl.program_id(0) == f)
        def _(f=f):
            out[...] = first_coef[...] * firsts[f][...] + second_coef[...] * seconds[f][...]


def whole(array):
    return pl.BlockSpec(array.shape, lambda i, n=array.ndim: (0,) * n)


def call(kernel, grid, operands, outs, scratch, flops):
    arrays = [a for a, _ in operands]
    moved = sum(a.size * a.dtype.itemsize for a in arrays)
    return pl.pallas_call(
        kernel,
        grid=(grid,),
        in_specs=[s for _, s in operands],
        out_specs=[s for _, s in outs],
        out_shape=[jax.ShapeDtypeStruct(s, F32) for s, _ in outs],
        scratch_shapes=scratch,
        compiler_params=pltpu.CompilerParams(vmem_limit_bytes=LIMIT),
        cost_estimate=pl.CostEstimate(flops=flops, bytes_accessed=moved, transcendentals=0),
    )(*arrays)


def shards(loads, schur_flex, dirichlet, coupling, corner_index, face_lists, coarse_inverse):
    flex_mat = schur_flex[0, 0]
    prec_mat = dirichlet[0, 0]
    coupling_mat = coupling[0, 0]
    corners = corner_index[0, 0]
    face_index = face_lists[0, 0]
    load = loads[0, 0]
    ncoarse = coarse_inverse.shape[1]
    ncl, ni = coupling_mat.shape
    width = load.shape[1]
    face, half = ni // 4, ni // 2
    n_sx, n_sy = lax.axis_size("sx"), lax.axis_size("sy")
    at_x, at_y = lax.axis_index("sx"), lax.axis_index("sy")

    has = jnp.stack([at_x > 0, at_x < n_sx - 1, at_y > 0, at_y < n_sy - 1])
    scale = jnp.where(has, 2.0, 1.0).astype(F32)
    select = (face_index[:, :, None] == jnp.arange(face, dtype=jnp.int32)).astype(BF16)
    one = jnp.ones((1, width), F32)
    smem = pl.BlockSpec(memory_space=pltpu.SMEM)

    one_face = jax.ShapeDtypeStruct((face, width), F32)
    face_out = ((face, width), whole(one_face))
    parts = [pltpu.VMEM((half, width), BF16), pltpu.VMEM((half, width), BF16)]
    part_flops = 6 * half * half * width

    def exchange_y(faces):
        return facing(faces[2], faces[3], "sy")

    def exchange_x(faces):
        return facing(faces[0], faces[1], "sx")

    def with_whole(arrays):
        return [(a, whole(a)) for a in arrays]

    def early(matrix, owns, nears, coef, bases=()):
        operands = [(scale, smem), (matrix, pl.BlockSpec((face, half), lambda i: (i, 0)))]
        operands += with_whole([*owns, *nears])
        operands += [(select, pl.BlockSpec((2, face, face), lambda i: (0, 0, 0))), (coef, whole(coef))]
        operands += with_whole(bases)
        outs = [face_out, face_out, ((ni, width), pl.BlockSpec((face, width), lambda i: (i, 0)))]
        return call(functools.partial(early_kernel, bool(bases)), 4, operands, outs, parts, 2 * part_flops)

    def crit(matrix, owns, nears, coef, partial, bases=(), extra=()):
        operands = [(scale, smem), (matrix, pl.BlockSpec((face, half), lambda i: (i + 2, 1)))]
        operands += with_whole([*owns, *nears])
        operands += [(select, pl.BlockSpec((2, face, face), lambda i: (1, 0, 0))), (coef, whole(coef))]
        operands += [(partial, pl.BlockSpec((face, width), lambda i: (i + 2, 0)))]
        operands += with_whole(bases)
        operands += [(a, pl.BlockSpec((face, width), lambda i: (i + 2, 0))) for a in extra]
        kernel = functools.partial(crit_kernel, bool(bases), len(extra))
        return call(kernel, 2, operands, [face_out] * 4, parts, part_flops)

    def late(matrix, values, partial, extra=()):
        operands = [(scale, smem), (matrix, pl.BlockSpec((face, half), lambda i: (i, 1)))]
        operands += with_whole(values)
        operands += [(partial, pl.BlockSpec((face, width), lambda i: (i, 0)))]
        operands += [(a, pl.BlockSpec((face, width), lambda i: (i, 0))) for a in extra]
        return call(functools.partial(late_kernel, len(extra)), 2, operands, [face_out] * 2, parts, part_flops)

    def applied(matrix, owns, nears, coef, bases=(), extra=()):
        v0, v1, partial = early(matrix, owns[:2], nears[:2], coef, bases[:2])
        v2, v3, a2, a3 = crit(matrix, owns[2:], nears[2:], coef, partial, bases[2:], extra)
        a0, a1 = late(matrix, (v2, v3), partial, extra)
        return (v0, v1, v2, v3), (a0, a1, a2, a3)

    def exchanged(faces):
        far = exchange_y(faces)
        return (*exchange_x(faces), *far)

    def inner(first, second):
        return sum(jnp.sum(scale[f] * first[f] * second[f], axis=0, keepdims=True) for f in range(4))

    def rows_of(array):
        return [array[f * face : (f + 1) * face] for f in range(4)]

    load_faces = rows_of(load)
    sent = []
    for f in range(4):
        columns = jnp.pad(coupling_mat[:, f * face : (f + 1) * face], ((0, 0), (0, -face % width)))
        blocks = [columns[:, at : at + width] for at in range(0, columns.shape[1], width)]
        sent.append(jnp.concatenate([load_faces[f], *blocks], axis=0))
    near = exchanged(sent)

    listed = jnp.zeros((1, ncoarse), F32).at[0, :ncl].set(corners.astype(F32))
    table = from_all(jnp.concatenate([coarse_inverse, listed], axis=0))
    matrix_all = table[:, :-1].reshape(ncoarse, ncoarse)
    corners_all = table[:, -1, :ncl].astype(jnp.int32)
    coarse_ids = jnp.arange(ncoarse, dtype=jnp.int32)[:, None]

    me = at_x * n_sy + at_y
    there = [me - n_sy, me + n_sy, me - 1, me + 1]
    lift = []
    for f in range(4):
        columns = jnp.concatenate(
            [near[f][at : at + ncl] for at in range(face, near[f].shape[0], ncl)], axis=1
        )[:, :face]
        theirs = lax.dot_general(columns, select[f].astype(F32), (((1,), (1,)), ((), ())), precision=HIGHEST)
        ids = jnp.concatenate([corners, corners_all[jnp.clip(there[f], 0, n_sx * n_sy - 1)]])
        values = jnp.concatenate([coupling_mat[:, f * face : (f + 1) * face], -theirs], axis=0)
        lift.append(jnp.dot((coarse_ids == ids[None, :]).astype(F32), values, precision=HIGHEST))
    lift = jnp.concatenate(lift, axis=1)
    lift_spread = lift * jnp.repeat(scale, face)[None, :]

    def coarse_sum(faces):
        local = sum(
            jnp.dot(lift_spread[:, f * face : (f + 1) * face], faces[f], precision=HIGH) for f in range(4)
        )
        return lax.psum(lax.psum(0.5 * local, "sx"), "sy")

    def lifted(sol):
        full = lax.dot_general(lift, sol, (((0,), (0,)), ((), ())), precision=HIGH)
        return rows_of(full)

    def dots_sum(dots):
        return jnp.sum(from_all(jnp.concatenate(dots, axis=0)), axis=0)

    residual0, applied0 = applied(prec_mat, load_faces, near, one)
    near = exchanged(applied0)
    rho0 = 0.5 * inner(residual0, applied0)
    rhs0 = coarse_sum(applied0)
    lift_applied = lax.dot_general(prec_mat, lift_spread, (((1,), (1,)), ((), ())), precision=HIGH)

    direction0, fine0 = applied(flex_mat, applied0, near, 0.5 * one)
    near = exchanged(fine0)
    dots0 = dots_sum([rho0, inner(direction0, fine0)])
    sol0 = jnp.dot(matrix_all, rhs0, precision=HIGHEST)
    lift_sol = jnp.dot(lift_applied, sol0, precision=HIGH)
    jump0, image_applied = applied(prec_mat, fine0, near, one, (), (lift_sol,))
    near = exchanged(image_applied)
    rho0, fine_dot0 = dots0[0:1], dots0[1:2]
    step0 = rho0 / (fine_dot0 + jnp.sum(rhs0 * sol0, axis=0, keepdims=True))
    rhs1 = rhs0 - step0 * coarse_sum(image_applied)
    lift0 = lifted(sol0)
    residual1 = [r - step0 * (j + c) for r, j, c in zip(residual0, jump0, lift0)]
    applied1 = [z - step0 * y for z, y in zip(applied0, image_applied)]
    rho1 = 0.5 * inner(residual1, applied1)

    precond, fine1 = applied(flex_mat, image_applied, near, -0.5 * step0, direction0)
    near = exchanged(fine1)
    dots1 = dots_sum([rho1, inner(precond, fine1), inner(precond, fine0)])
    rho1, dot11, dot10 = dots1[0:1], dots1[1:2], dots1[2:3]
    beta = rho1 / rho0
    rhs1 = rhs1 + beta * rhs0
    sol1 = jnp.dot(matrix_all, rhs1, precision=HIGHEST)
    curve = dot11 + 2.0 * beta * dot10 + beta * beta * fine_dot0 + jnp.sum(rhs1 * sol1, axis=0, keepdims=True)
    step1 = rho1 / curve
    lift1 = lifted(sol1)
    bases = [r - step1 * (beta * j + c) for r, j, c in zip(residual1, jump0, lift1)]
    block = pl.BlockSpec((face, width), lambda i: (i, 0))
    (multipliers,) = call(
        weighted_kernel,
        4,
        with_whole([*direction0, *precond, step0 + step1 * beta, step1]),
        [((ni, width), block)],
        [],
        4 * ni * width,
    )
    operands = with_whole([*fine1, *near, *bases])
    operands += [(select, pl.BlockSpec((1, face, face), lambda i: (i, 0, 0)))] + with_whole([-step1])
    (residual2,) = call(tail_kernel, 4, operands, [((ni, width), block)], [], 6 * ni * face * width)
    return multipliers[None, None], residual2[None, None]


def solution(mesh):
    return jax.shard_map(
        shards,
        mesh=mesh,
        in_specs=(
            P("sx", "sy", None, None),
            P("sx", "sy", None, None),
            P("sx", "sy", None, None),
            P("sx", "sy", None, None),
            P("sx", "sy", None),
            P("sx", "sy", None, None),
            P(("sx", "sy"), None),
        ),
        out_specs=(P("sx", "sy", None, None), P("sx", "sy", None, None)),
        check_vma=False,
    )
```

```python
import functools

import jax
import jax.numpy as jnp
from jax import lax
from jax.experimental import pallas as pl
from jax.experimental.pallas import tpu as pltpu
from jax.sharding import PartitionSpec as P

HIGHEST = lax.Precision.HIGHEST
F32 = jnp.float32
BF16 = jnp.bfloat16
LIMIT = 56 * 1024 * 1024


def shifted(block, axis, distance):
    devices = range(lax.axis_size(axis))
    route = [(i - distance, i) for i in devices if i - distance in devices]
    return lax.ppermute(block, axis, route)


def facing(low, high, axis):
    return shifted(high, axis, 1), shifted(low, axis, -1)


def from_all(rows):
    count = lax.axis_size("sx") * lax.axis_size("sy")
    copies = jnp.broadcast_to(rows[None], (count,) + rows.shape)
    return lax.all_to_all(copies, ("sx", "sy"), 0, 0, tiled=True)


def split(x):
    high = x.astype(BF16)
    return high, (x - high.astype(F32)).astype(BF16)


def dot(a, b):
    return jnp.dot(a, b, preferred_element_type=F32)


def product(a, b_high, b_low):
    a_high, a_low = split(a)
    return dot(a_high, b_high) + (dot(a_high, b_low) + dot(a_low, b_high))


def permuted(select, rows):
    high = rows.astype(BF16)
    rest = rows - high.astype(F32)
    mid = rest.astype(BF16)
    low = (rest - mid.astype(F32)).astype(BF16)
    return dot(select, high) + (dot(select, mid) + dot(select, low))


def pack_kernel(load, coupling, *outs):
    face = load.shape[0] // len(outs)
    width = load.shape[1]
    ncl = coupling.shape[0]
    for f, out in enumerate(outs):
        out[:face] = load[f * face : (f + 1) * face]
        for block, at in enumerate(range(0, face, width)):
            rows = slice(face + block * ncl, face + (block + 1) * ncl)
            wide = min(width, face - at)
            if wide < width:
                out[rows] = jnp.zeros((ncl, width), F32)
            out[rows, :wide] = coupling[:, f * face + at : f * face + at + wide]


def lift_kernel(near0, near1, near2, near3, select, coupling, picks, out):
    face = out.shape[0]
    ncl = coupling.shape[0]
    for f, near in enumerate((near0, near1, near2, near3)):

        @pl.when(pl.program_id(0) == f)
        def _(near=near):
            columns = jnp.concatenate([near[at : at + ncl] for at in range(0, near.shape[0], ncl)], axis=1)
            own = jnp.dot(coupling[...].T, picks[0, :ncl], precision=HIGHEST)
            theirs = jnp.dot(columns[:, :face].T, picks[0, ncl:], precision=HIGHEST)
            out[...] = own - permuted(select[0], theirs)


def field_into(at, faces, select, scale, coef, bases, lifts, outs, images, high, low):
    size = outs[0].shape[0]
    if lifts:
        lift, sol = lifts
        corrections = product(lift[...], *split(sol[...]))
    for f in range(2):
        own, near = faces[f]
        image = own[:size] - permuted(select[f], near[:size])
        rows = slice(f * size, (f + 1) * size)
        if lifts:
            image = image + corrections[rows]
        if images:
            images[f][...] = image
        value = coef[...] * image
        if bases:
            value = bases[f][...] + value
        outs[f][...] = value
        high[rows], low[rows] = split(scale[at + f] * value)


def take(refs, *counts):
    groups = []
    for count in counts:
        groups.append(refs[:count])
        refs = refs[count:]
    return (*groups, refs)


def early_kernel(based, lifted, *refs):
    (scale, mat, own0, own1, near0, near1, select, coef), bases, lifts, outs, images, rest = take(
        refs, 8, 2 * based, 2 * lifted, 2, 2 * lifted
    )
    partial, high, low = rest

    @pl.when(pl.program_id(0) == 0)
    def _():
        faces = ((own0, near0), (own1, near1))
        field_into(0, faces, select, scale, coef, bases, lifts, outs, images, high, low)

    partial[...] = product(mat[...], high[...], low[...])


def crit_kernel(based, lifted, *refs):
    (scale, mat, own2, own3, near2, near3, select, coef, partial), bases, lifts, outs, images, rest = take(
        refs, 9, 2 * based, 2 * lifted, 2, 2 * lifted
    )
    *applied, high, low = rest

    @pl.when(pl.program_id(0) == 0)
    def _():
        faces = ((own2, near2), (own3, near3))
        field_into(2, faces, select, scale, coef, bases, lifts, outs, images, high, low)

    value = partial[...] + product(mat[...], high[...], low[...])
    for at, ref in enumerate(applied):

        @pl.when(pl.program_id(0) == at)
        def _(ref=ref):
            ref[...] = value


def late_kernel(others, *refs):
    (scale, mat, coupling), values, applied, other, rest = take(refs, 3, 4, 2, 4 * others)
    partial, carried, out0, out1, sums, high, low = rest
    size = out0.shape[0]
    ncl = coupling.shape[0]

    def inner(f, with_ref):
        return jnp.sum(scale[f] * values[f][...] * with_ref, axis=0, keepdims=True)

    @pl.when(pl.program_id(0) == 0)
    def _():
        coarse = None
        for f in (0, 1, 2, 3):
            parts = split(scale[f] * values[f][...])
            if f >= 2:
                rows = slice((f - 2) * size, (f - 1) * size)
                high[rows], low[rows] = parts
            term = product(coupling[:, f * size : (f + 1) * size], *parts)
            coarse = term if coarse is None else coarse + term
        sums[:ncl] = coarse
        sums[ncl : ncl + 1] = inner(2, applied[0][...]) + inner(3, applied[1][...])
        sums[ncl + 1 : ncl + 2] = carried[ncl : ncl + 1]
        if others:
            sums[ncl + 2 : ncl + 3] = sum(inner(f, other[f][...]) for f in range(4))

    value = partial[...] + product(mat[...], high[...], low[...])
    for at, ref in enumerate((out0, out1)):

        @pl.when(pl.program_id(0) == at)
        def _(at=at, ref=ref):
            ref[...] = value
            sums[ncl : ncl + 1] += inner(at, value)


def gathered_sums(table, pick, ncl, stacked):
    for d in range(table.shape[0]):
        stacked[d * ncl : (d + 1) * ncl] = table[d, :ncl]
    rhs = permuted(pick[...], stacked[...])
    return rhs, [jnp.sum(table[:, row], axis=0, keepdims=True) for row in range(ncl, table.shape[1])]


def first_step_kernel(ncl, table, pick, matrix, rhs_out, sol_out, steps, stacked):
    rhs, (fine_dot, rho) = gathered_sums(table, pick, ncl, stacked)
    sol = jnp.dot(matrix[...], rhs, precision=HIGHEST)
    rho = 0.5 * rho
    curve = fine_dot + jnp.sum(rhs * sol, axis=0, keepdims=True)
    rhs_out[...] = rhs
    sol_out[...] = sol
    steps[0:1] = rho / curve
    steps[1:2] = rho
    steps[2:3] = fine_dot
    steps[3:] = jnp.zeros((steps.shape[0] - 3, steps.shape[1]), F32)


def second_step_kernel(ncl, table, pick, matrix, rhs0, sol0, steps0, sol_out, steps, stacked):
    rhs, (dot11, rho1, dot10) = gathered_sums(table, pick, ncl, stacked)
    sol = jnp.dot(matrix[...], rhs, precision=HIGHEST)
    step0, rho0, dot00 = (steps0[row : row + 1] for row in range(3))
    rho1 = 0.5 * rho1
    beta = rho1 / rho0
    coarse = jnp.sum((rhs + beta * rhs0[...]) * (sol + beta * sol0[...]), axis=0, keepdims=True)
    step1 = rho1 / (dot11 + 2.0 * beta * dot10 + beta * beta * dot00 + coarse)
    sol_out[...] = sol
    steps[0:1] = -step1
    steps[1:2] = -step1 * beta
    steps[2:3] = step0 + step1 * beta
    steps[3:4] = step1
    steps[4:] = jnp.zeros((steps.shape[0] - 4, steps.shape[1]), F32)


def tail_kernel(*refs):
    owns, nears, residuals, images, rest = take(refs, 4, 4, 4, 4)
    select, lift, sol, steps, out = rest
    size = out.shape[0]
    for f in range(4):

        @pl.when(pl.program_id(0) == f)
        def _(f=f):
            image = owns[f][...] - permuted(select[0], nears[f][:size])
            image = image + product(lift[...], *split(sol[...]))
            out[...] = residuals[f][...] + steps[0:1] * image + steps[1:2] * images[f][...]


def weighted_kernel(*refs):
    firsts, seconds, (steps, out) = take(refs, 4, 4)
    for f in range(4):

        @pl.when(pl.program_id(0) == f)
        def _(f=f):
            out[...] = steps[2:3] * firsts[f][...] + steps[3:4] * seconds[f][...]


def whole(array):
    return pl.BlockSpec(array.shape, lambda i, n=len(array.shape): (0,) * n)


def with_whole(arrays):
    return [(a, whole(a)) for a in arrays]


def call(kernel, grid, operands, outs, scratch=()):
    return pl.pallas_call(
        kernel,
        grid=(grid,),
        in_specs=[s for _, s in operands],
        out_specs=[s for _, s in outs],
        out_shape=[jax.ShapeDtypeStruct(s, F32) for s, _ in outs],
        scratch_shapes=list(scratch),
        compiler_params=pltpu.CompilerParams(vmem_limit_bytes=LIMIT),
        cost_estimate=pl.CostEstimate(flops=1024, bytes_accessed=1024, transcendentals=0),
    )(*[a for a, _ in operands])


def out_whole(*shape):
    return shape, whole(jax.ShapeDtypeStruct(shape, F32))


def shards(loads, schur_flex, dirichlet, coupling, corner_index, face_lists, coarse_inverse):
    flex_mat = schur_flex[0, 0]
    prec_mat = dirichlet[0, 0]
    coupling_mat = coupling[0, 0]
    corners = corner_index[0, 0]
    face_index = face_lists[0, 0]
    load = loads[0, 0]
    ncoarse = coarse_inverse.shape[1]
    ncl, ni = coupling_mat.shape
    width = load.shape[1]
    face, half = ni // 4, ni // 2
    n_sx, n_sy = lax.axis_size("sx"), lax.axis_size("sy")
    at_x, at_y = lax.axis_index("sx"), lax.axis_index("sy")

    has = jnp.stack([at_x > 0, at_x < n_sx - 1, at_y > 0, at_y < n_sy - 1])
    scale = jnp.where(has, 2.0, 1.0).astype(F32)
    select = (face_index[:, :, None] == jnp.arange(face, dtype=jnp.int32)).astype(BF16)
    one = jnp.ones((1, width), F32)
    smem = pl.BlockSpec(memory_space=pltpu.SMEM)
    face_out = out_whole(face, width)
    parts = [pltpu.VMEM((half, width), BF16), pltpu.VMEM((half, width), BF16)]

    def lift_specs(lifts, at):
        if not lifts:
            return []
        lift, sol = lifts
        return [(lift, pl.BlockSpec((half, ncoarse), lambda i: (at, 0))), (sol, whole(sol))]

    def early(matrix, owns, nears, coef, bases, lifts):
        operands = [(scale, smem), (matrix, pl.BlockSpec((face, half), lambda i: (i, 0)))]
        operands += with_whole([*owns, *nears])
        operands += [(select, pl.BlockSpec((2, face, face), lambda i: (0, 0, 0))), (coef, whole(coef))]
        operands += with_whole(bases) + lift_specs(lifts, 0)
        outs = [face_out] * (4 if lifts else 2)
        outs += [((ni, width), pl.BlockSpec((face, width), lambda i: (i, 0)))]
        *fields, partial = call(functools.partial(early_kernel, bool(bases), bool(lifts)), 4, operands, outs, parts)
        return fields[:2], fields[2:], partial

    def crit(matrix, owns, nears, coef, partial, bases, lifts):
        operands = [(scale, smem), (matrix, pl.BlockSpec((face, half), lambda i: (i + 2, 1)))]
        operands += with_whole([*owns, *nears])
        operands += [(select, pl.BlockSpec((2, face, face), lambda i: (1, 0, 0))), (coef, whole(coef))]
        operands += [(partial, pl.BlockSpec((face, width), lambda i: (i + 2, 0)))]
        operands += with_whole(bases) + lift_specs(lifts, 1)
        outs = [face_out] * (6 if lifts else 4)
        *fields, a2, a3 = call(functools.partial(crit_kernel, bool(bases), bool(lifts)), 2, operands, outs, parts)
        return fields[:2], fields[2:], (a2, a3)

    def late(matrix, values, applied, partial, carried, other):
        operands = [(scale, smem), (matrix, pl.BlockSpec((face, half), lambda i: (i, 1)))]
        operands += with_whole([coupling_mat, *values, *applied, *other])
        operands += [(partial, pl.BlockSpec((face, width), lambda i: (i, 0))), (carried, whole(carried))]
        outs = [face_out, face_out, out_whole(ncl + 2 + bool(other), width)]
        return call(functools.partial(late_kernel, int(bool(other))), 2, operands, outs, parts)

    def applied(matrix, owns, nears, coef, bases=(), lifts=(), carried=None, other=()):
        v01, q01, partial = early(matrix, owns[:2], nears[:2], coef, bases[:2], lifts)
        v23, q23, a23 = crit(matrix, owns[2:], nears[2:], coef, partial, bases[2:], lifts)
        values = (*v01, *v23)
        if carried is None:
            carried = jnp.zeros((ncl + 1, width), F32)
        a0, a1, sums = late(matrix, values, a23, partial, carried, other)
        return values, (*q01, *q23), (a0, a1, *a23), sums

    def exchanged(faces):
        far = facing(faces[2], faces[3], "sy")
        return (*facing(faces[0], faces[1], "sx"), *far)

    extra = -(-face // width) * ncl
    sent = call(pack_kernel, 1, with_whole([load, coupling_mat]), [out_whole(face + extra, width)] * 4)
    near = exchanged(sent)

    listed = jnp.zeros((1, ncoarse), F32).at[0, :ncl].set(corners.astype(F32))
    own_rows, _ = lax.optimization_barrier((jnp.concatenate([coarse_inverse, listed], axis=0), sent[0]))
    table = from_all(own_rows)
    matrix_all = table[:, :-1].reshape(ncoarse, ncoarse)
    corners_all = table[:, -1, :ncl].astype(jnp.int32)
    coarse_ids = jnp.arange(ncoarse, dtype=jnp.int32)
    pick_all = (corners_all.reshape(1, -1) == coarse_ids[:, None]).astype(BF16)
    me = at_x * n_sy + at_y
    there = jnp.clip(jnp.stack([me - n_sy, me + n_sy, me - 1, me + 1]), 0, n_sx * n_sy - 1)
    ids = jnp.concatenate([jnp.broadcast_to(corners, (4, ncl)), corners_all[there]], axis=1)
    picks = (ids[:, :, None] == coarse_ids).astype(F32)

    residual0, _, applied0, sums = applied(prec_mat, sent, near, one)
    operands = [(n, pl.BlockSpec((extra, width), lambda i: (face // extra, 0))) for n in near]
    operands += [
        (select, pl.BlockSpec((1, face, face), lambda i: (i, 0, 0))),
        (coupling_mat, pl.BlockSpec((ncl, face), lambda i: (0, i))),
        (picks, pl.BlockSpec((1, 2 * ncl, ncoarse), lambda i: (i, 0, 0))),
    ]
    (lift,) = call(lift_kernel, 4, operands, [((ni, ncoarse), pl.BlockSpec((face, ncoarse), lambda i: (i, 0)))])
    near = exchanged(applied0)

    stacked = [pltpu.VMEM((n_sx * n_sy * ncl, width), F32)]
    coarse_out, steps_out = out_whole(ncoarse, width), out_whole(8, width)
    direction0, _, fine0, sums = applied(flex_mat, applied0, near, 0.5 * one, carried=sums)
    near = exchanged(fine0)
    rhs0, sol0, steps0 = call(
        functools.partial(first_step_kernel, ncl),
        1,
        with_whole([from_all(sums), pick_all, matrix_all]),
        [coarse_out, coarse_out, steps_out],
        stacked,
    )
    residual1, image0, applied1, sums = applied(prec_mat, fine0, near, -steps0[0:1], residual0, (lift, sol0))
    near = exchanged(applied1)

    precond, _, fine1, sums = applied(flex_mat, applied1, near, 0.5 * one, carried=sums, other=fine0)
    near = exchanged(fine1)
    sol1, steps1 = call(
        functools.partial(second_step_kernel, ncl),
        1,
        with_whole([from_all(sums), pick_all, matrix_all, rhs0, sol0, steps0]),
        [coarse_out, steps_out],
        stacked,
    )
    out = [((ni, width), pl.BlockSpec((face, width), lambda i: (i, 0)))]
    (multipliers,) = call(weighted_kernel, 4, with_whole([*direction0, *precond, steps1]), out)
    operands = with_whole([*fine1, *near, *residual1, *image0])
    operands += [
        (select, pl.BlockSpec((1, face, face), lambda i: (i, 0, 0))),
        (lift, pl.BlockSpec((face, ncoarse), lambda i: (i, 0))),
    ]
    (residual2,) = call(tail_kernel, 4, operands + with_whole([sol1, steps1]), out)
    return multipliers[None, None], residual2[None, None]


def solution(mesh):
    return jax.shard_map(
        shards,
        mesh=mesh,
        in_specs=(
            P("sx", "sy", None, None),
            P("sx", "sy", None, None),
            P("sx", "sy", None, None),
            P("sx", "sy", None, None),
            P("sx", "sy", None),
            P("sx", "sy", None, None),
            P(("sx", "sy"), None),
        ),
        out_specs=(P("sx", "sy", None, None), P("sx", "sy", None, None)),
        check_vma=False,
    )
```

```python
import functools

import jax
import jax.numpy as jnp
from jax import lax
from jax.experimental import pallas as pl
from jax.experimental.pallas import tpu as pltpu
from jax.sharding import PartitionSpec as P

HIGHEST = lax.Precision.HIGHEST
F32 = jnp.float32
BF16 = jnp.bfloat16
LIMIT = 24 * 1024 * 1024


def shifted(block, axis, distance):
    devices = range(lax.axis_size(axis))
    route = [(i - distance, i) for i in devices if i - distance in devices]
    return lax.ppermute(block, axis, route)


def facing(low, high, axis):
    return shifted(high, axis, 1), shifted(low, axis, -1)


def from_all(rows):
    count = lax.axis_size("sx") * lax.axis_size("sy")
    copies = jnp.broadcast_to(rows[None], (count,) + rows.shape)
    return lax.all_to_all(copies, ("sx", "sy"), 0, 0, tiled=True)


def split(x):
    high = x.astype(BF16)
    return high, (x - high.astype(F32)).astype(BF16)


def dot(a, b):
    return jnp.dot(a, b, preferred_element_type=F32)


def product(a, b_high, b_low):
    a_high, a_low = split(a)
    return dot(a_high, b_high) + (dot(a_high, b_low) + dot(a_low, b_high))


def permuted(select, rows):
    high = rows.astype(BF16)
    rest = rows - high.astype(F32)
    mid = rest.astype(BF16)
    low = (rest - mid.astype(F32)).astype(BF16)
    return dot(select, high) + (dot(select, mid) + dot(select, low))


def pack_kernel(load, coupling, *outs):
    face = load.shape[0] // len(outs)
    width = load.shape[1]
    ncl = coupling.shape[0]
    for f, out in enumerate(outs):
        out[:face] = load[f * face : (f + 1) * face]
        for block, at in enumerate(range(0, face, width)):
            rows = slice(face + block * ncl, face + (block + 1) * ncl)
            wide = min(width, face - at)
            if wide < width:
                out[rows] = jnp.zeros((ncl, width), F32)
            out[rows, :wide] = coupling[:, f * face + at : f * face + at + wide]


def lift_kernel(near0, near1, near2, near3, select, coupling, picks, out):
    face = out.shape[0] // 4
    ncl = coupling.shape[0]
    for f, near in enumerate((near0, near1, near2, near3)):
        columns = jnp.concatenate([near[at : at + ncl] for at in range(face, near.shape[0], ncl)], axis=1)
        own = jnp.dot(coupling[:, f * face : (f + 1) * face].T, picks[f, :ncl], precision=HIGHEST)
        theirs = jnp.dot(columns[:, :face].T, picks[f, ncl:], precision=HIGHEST)
        out[f * face : (f + 1) * face] = own - permuted(select[f], theirs)


def field_into(at, faces, select, scale, coef, bases, lifts, outs, images, high, low):
    size = outs[0].shape[0]
    if lifts:
        lift, sol = lifts
        corrections = product(lift[at * size : (at + 2) * size], *split(sol[...]))
    for f in range(2):
        own, near = faces[f]
        image = own[:size] - permuted(select[at + f], near[:size])
        rows = slice(f * size, (f + 1) * size)
        if lifts:
            image = image + corrections[rows]
        if images:
            images[f][...] = image
        value = coef[...] * image
        if bases:
            value = bases[f][...] + value
        outs[f][...] = value
        high[rows], low[rows] = split(scale[at + f] * value)


def take(refs, *counts):
    groups = []
    for count in counts:
        groups.append(refs[:count])
        refs = refs[count:]
    return (*groups, refs)


def early_kernel(based, lifted, *refs):
    (scale, mat, own0, own1, near0, near1, select, coef), bases, lifts, outs, images, rest = take(
        refs, 8, 2 * based, 2 * lifted, 2, 2 * lifted
    )
    partial, high, low = rest
    faces = ((own0, near0), (own1, near1))
    field_into(0, faces, select, scale, coef, bases, lifts, outs, images, high, low)
    half = high.shape[0]
    for rows in (slice(0, half), slice(half, 2 * half)):
        partial[rows] = product(mat[rows, :half], high[...], low[...])


def crit_kernel(based, lifted, *refs):
    (scale, mat, own2, own3, near2, near3, select, coef, partial), bases, lifts, outs, images, rest = take(
        refs, 9, 2 * based, 2 * lifted, 2, 2 * lifted
    )
    out2, out3, high, low = rest
    faces = ((own2, near2), (own3, near3))
    field_into(2, faces, select, scale, coef, bases, lifts, outs, images, high, low)
    half = high.shape[0]
    size = half // 2
    value = partial[half:] + product(mat[half:, half:], high[...], low[...])
    out2[...] = value[:size]
    out3[...] = value[size:]


def late_kernel(others, *refs):
    (scale, mat, coupling), values, applied, other, rest = take(refs, 3, 4, 2, 4 * others)
    partial, carried, out0, out1, sums, high, low = rest
    size = out0.shape[0]
    ncl = coupling.shape[0]

    def inner(f, with_value):
        return jnp.sum(scale[f] * values[f][...] * with_value, axis=0, keepdims=True)

    coarse = None
    for f in range(4):
        parts = split(scale[f] * values[f][...])
        if f >= 2:
            rows = slice((f - 2) * size, (f - 1) * size)
            high[rows], low[rows] = parts
        term = product(coupling[:, f * size : (f + 1) * size], *parts)
        coarse = term if coarse is None else coarse + term
    sums[:ncl] = coarse
    sums[ncl + 1 : ncl + 2] = carried[ncl : ncl + 1]
    if others:
        sums[ncl + 2 : ncl + 3] = sum(inner(f, other[f][...]) for f in range(4))
    total = inner(2, applied[0][...]) + inner(3, applied[1][...])
    product_rows = partial[: 2 * size] + product(mat[: 2 * size, 2 * size :], high[...], low[...])
    for f, out in enumerate((out0, out1)):
        value = product_rows[f * size : (f + 1) * size]
        out[...] = value
        total = total + inner(f, value)
    sums[ncl : ncl + 1] = total


def gathered_sums(table, pick, ncl, stacked):
    for d in range(table.shape[0]):
        stacked[d * ncl : (d + 1) * ncl] = table[d, :ncl]
    rhs = permuted(pick[...], stacked[...])
    return rhs, [jnp.sum(table[:, row], axis=0, keepdims=True) for row in range(ncl, table.shape[1])]


def first_step_kernel(ncl, table, pick, matrix, rhs_out, sol_out, steps, stacked):
    rhs, (fine_dot, rho) = gathered_sums(table, pick, ncl, stacked)
    sol = jnp.dot(matrix[...], rhs, precision=HIGHEST)
    rho = 0.5 * rho
    curve = fine_dot + jnp.sum(rhs * sol, axis=0, keepdims=True)
    rhs_out[...] = rhs
    sol_out[...] = sol
    steps[0:1] = rho / curve
    steps[1:2] = rho
    steps[2:3] = fine_dot
    steps[3:] = jnp.zeros((steps.shape[0] - 3, steps.shape[1]), F32)


def second_step_kernel(ncl, table, pick, matrix, rhs0, sol0, steps0, sol_out, steps, stacked):
    rhs, (dot11, rho1, dot10) = gathered_sums(table, pick, ncl, stacked)
    sol = jnp.dot(matrix[...], rhs, precision=HIGHEST)
    step0, rho0, dot00 = (steps0[row : row + 1] for row in range(3))
    rho1 = 0.5 * rho1
    beta = rho1 / rho0
    coarse = jnp.sum((rhs + beta * rhs0[...]) * (sol + beta * sol0[...]), axis=0, keepdims=True)
    step1 = rho1 / (dot11 + 2.0 * beta * dot10 + beta * beta * dot00 + coarse)
    sol_out[...] = sol
    steps[0:1] = -step1
    steps[1:2] = -step1 * beta
    steps[2:3] = step0 + step1 * beta
    steps[3:4] = step1
    steps[4:] = jnp.zeros((steps.shape[0] - 4, steps.shape[1]), F32)


def tail_kernel(*refs):
    owns, nears, residuals, images, rest = take(refs, 4, 4, 4, 4)
    select, lift, sol, steps, out = rest
    size = out.shape[0] // 4
    parts = split(sol[...])
    for f in range(4):
        rows = slice(f * size, (f + 1) * size)
        image = owns[f][...] - permuted(select[f], nears[f][:size])
        image = image + product(lift[rows], *parts)
        out[rows] = residuals[f][...] + steps[0:1] * image + steps[1:2] * images[f][...]


def weighted_kernel(*refs):
    firsts, seconds, (steps, out) = take(refs, 4, 4)
    size = out.shape[0] // 4
    for f in range(4):
        out[f * size : (f + 1) * size] = steps[2:3] * firsts[f][...] + steps[3:4] * seconds[f][...]


def call(kernel, operands, shapes, scratch=(), specs=None):
    vmem = pl.BlockSpec(memory_space=pltpu.VMEM)
    specs = specs or {}
    return pl.pallas_call(
        kernel,
        in_specs=[specs.get(i, vmem) for i in range(len(operands))],
        out_specs=[vmem] * len(shapes),
        out_shape=[jax.ShapeDtypeStruct(s, F32) for s in shapes],
        scratch_shapes=list(scratch),
        compiler_params=pltpu.CompilerParams(vmem_limit_bytes=LIMIT),
        cost_estimate=pl.CostEstimate(flops=1024, bytes_accessed=1024, transcendentals=0),
    )(*operands)


def shards(loads, schur_flex, dirichlet, coupling, corner_index, face_lists, coarse_inverse):
    flex_mat = schur_flex[0, 0]
    prec_mat = dirichlet[0, 0]
    coupling_mat = coupling[0, 0]
    corners = corner_index[0, 0]
    face_index = face_lists[0, 0]
    load = loads[0, 0]
    ncoarse = coarse_inverse.shape[1]
    ncl, ni = coupling_mat.shape
    width = load.shape[1]
    face, half = ni // 4, ni // 2
    n_sx, n_sy = lax.axis_size("sx"), lax.axis_size("sy")
    at_x, at_y = lax.axis_index("sx"), lax.axis_index("sy")

    has = jnp.stack([at_x > 0, at_x < n_sx - 1, at_y > 0, at_y < n_sy - 1])
    scale = jnp.where(has, 2.0, 1.0).astype(F32)
    select = (face_index[:, :, None] == jnp.arange(face, dtype=jnp.int32)).astype(BF16)
    one = jnp.ones((1, width), F32)
    specs = {0: pl.BlockSpec(memory_space=pltpu.SMEM)}
    one_face = (face, width)

    parts = [pltpu.VMEM((half, width), BF16)] * 2

    def early(matrix, owns, nears, coef, bases, lifts):
        operands = [scale, matrix, *owns, *nears, select, coef, *bases, *lifts]
        shapes = [one_face] * (4 if lifts else 2) + [(ni, width)]
        kernel = functools.partial(early_kernel, bool(bases), bool(lifts))
        *fields, partial = call(kernel, operands, shapes, parts, specs)
        return fields[:2], fields[2:], partial

    def crit(matrix, owns, nears, coef, partial, bases, lifts):
        operands = [scale, matrix, *owns, *nears, select, coef, partial, *bases, *lifts]
        shapes = [one_face] * (6 if lifts else 4)
        kernel = functools.partial(crit_kernel, bool(bases), bool(lifts))
        *fields, a2, a3 = call(kernel, operands, shapes, parts, specs)
        return fields[:2], fields[2:], (a2, a3)

    def late(matrix, values, applied, partial, carried, other):
        operands = [scale, matrix, coupling_mat, *values, *applied, *other, partial, carried]
        shapes = [one_face, one_face, (ncl + 2 + bool(other), width)]
        return call(functools.partial(late_kernel, int(bool(other))), operands, shapes, parts, specs)

    def applied(matrix, owns, nears, coef, bases=(), lifts=(), carried=None, other=()):
        v01, q01, partial = early(matrix, owns[:2], nears[:2], coef, bases[:2], lifts)
        v23, q23, a23 = crit(matrix, owns[2:], nears[2:], coef, partial, bases[2:], lifts)
        values = (*v01, *v23)
        if carried is None:
            carried = jnp.zeros((ncl + 1, width), F32)
        a0, a1, sums = late(matrix, values, a23, partial, carried, other)
        return values, (*q01, *q23), (a0, a1, *a23), sums

    def exchanged(faces):
        far = facing(faces[2], faces[3], "sy")
        return (*facing(faces[0], faces[1], "sx"), *far)

    extra = -(-face // width) * ncl
    sent = call(pack_kernel, [load, coupling_mat], [(face + extra, width)] * 4)
    near = exchanged(sent)

    listed = jnp.zeros((1, ncoarse), F32).at[0, :ncl].set(corners.astype(F32))
    own_rows, _ = lax.optimization_barrier((jnp.concatenate([coarse_inverse, listed], axis=0), sent[0]))
    table = from_all(own_rows)
    matrix_all = table[:, :-1].reshape(ncoarse, ncoarse)
    corners_all = table[:, -1, :ncl].astype(jnp.int32)
    coarse_ids = jnp.arange(ncoarse, dtype=jnp.int32)
    pick_all = (corners_all.reshape(1, -1) == coarse_ids[:, None]).astype(BF16)
    me = at_x * n_sy + at_y
    there = jnp.clip(jnp.stack([me - n_sy, me + n_sy, me - 1, me + 1]), 0, n_sx * n_sy - 1)
    ids = jnp.concatenate([jnp.broadcast_to(corners, (4, ncl)), corners_all[there]], axis=1)
    picks = (ids[:, :, None] == coarse_ids).astype(F32)

    residual0, _, applied0, sums = applied(prec_mat, sent, near, one)
    (lift,) = call(lift_kernel, [*near, select, coupling_mat, picks], [(ni, ncoarse)])
    near = exchanged(applied0)

    stacked = [pltpu.VMEM((n_sx * n_sy * ncl, width), F32)]
    coarse_shape, steps_shape = (ncoarse, width), (8, width)
    direction0, _, fine0, sums = applied(flex_mat, applied0, near, 0.5 * one, carried=sums)
    near = exchanged(fine0)
    rhs0, sol0, steps0 = call(
        functools.partial(first_step_kernel, ncl),
        [from_all(sums), pick_all, matrix_all],
        [coarse_shape, coarse_shape, steps_shape],
        stacked,
    )
    residual1, image0, applied1, sums = applied(prec_mat, fine0, near, -steps0[0:1], residual0, (lift, sol0))
    near = exchanged(applied1)

    precond, _, fine1, sums = applied(flex_mat, applied1, near, 0.5 * one, carried=sums, other=fine0)
    near = exchanged(fine1)
    sol1, steps1 = call(
        functools.partial(second_step_kernel, ncl),
        [from_all(sums), pick_all, matrix_all, rhs0, sol0, steps0],
        [coarse_shape, steps_shape],
        stacked,
    )
    (multipliers,) = call(weighted_kernel, [*direction0, *precond, steps1], [(ni, width)])
    operands = [*fine1, *near, *residual1, *image0, select, lift, sol1, steps1]
    (residual2,) = call(tail_kernel, operands, [(ni, width)])
    return multipliers[None, None], residual2[None, None]


def solution(mesh):
    return jax.shard_map(
        shards,
        mesh=mesh,
        in_specs=(
            P("sx", "sy", None, None),
            P("sx", "sy", None, None),
            P("sx", "sy", None, None),
            P("sx", "sy", None, None),
            P("sx", "sy", None),
            P("sx", "sy", None, None),
            P(("sx", "sy"), None),
        ),
        out_specs=(P("sx", "sy", None, None), P("sx", "sy", None, None)),
        check_vma=False,
    )
```

```python
import functools

import jax
import jax.numpy as jnp
from jax import lax
from jax.experimental import pallas as pl
from jax.experimental.pallas import tpu as pltpu
from jax.sharding import PartitionSpec as P

HIGHEST = lax.Precision.HIGHEST
F32 = jnp.float32
BF16 = jnp.bfloat16
LIMIT = 8 * 1024 * 1024


def shifted(block, axis, distance):
    devices = range(lax.axis_size(axis))
    route = [(i - distance, i) for i in devices if i - distance in devices]
    return lax.ppermute(block, axis, route)


def facing(low, high, axis):
    return shifted(high, axis, 1), shifted(low, axis, -1)


def from_all(rows):
    count = lax.axis_size("sx") * lax.axis_size("sy")
    copies = jnp.broadcast_to(rows[None], (count,) + rows.shape)
    return lax.all_to_all(copies, ("sx", "sy"), 0, 0, tiled=True)


def split(x):
    high = x.astype(BF16)
    return high, (x - high.astype(F32)).astype(BF16)


def dot(a, b):
    return jnp.dot(a, b, preferred_element_type=F32)


def product(a, b_high, b_low):
    a_high, a_low = split(a)
    return dot(a_high, b_high) + (dot(a_high, b_low) + dot(a_low, b_high))


def permuted(select, rows):
    high = rows.astype(BF16)
    rest = rows - high.astype(F32)
    mid = rest.astype(BF16)
    low = (rest - mid.astype(F32)).astype(BF16)
    return dot(select, high) + (dot(select, mid) + dot(select, low))


def pack_kernel(load, coupling, *outs):
    face = load.shape[0] // len(outs)
    width = load.shape[1]
    ncl = coupling.shape[0]
    for f, out in enumerate(outs):
        out[:face] = load[f * face : (f + 1) * face]
        for block, at in enumerate(range(0, face, width)):
            rows = slice(face + block * ncl, face + (block + 1) * ncl)
            wide = min(width, face - at)
            if wide < width:
                out[rows] = jnp.zeros((ncl, width), F32)
            out[rows, :wide] = coupling[:, f * face + at : f * face + at + wide]


def lift_kernel(near0, near1, near2, near3, select, coupling, picks, out):
    face = out.shape[0] // 4
    ncl = coupling.shape[0]
    for f, near in enumerate((near0, near1, near2, near3)):
        columns = jnp.concatenate([near[at : at + ncl] for at in range(face, near.shape[0], ncl)], axis=1)
        own = jnp.dot(coupling[:, f * face : (f + 1) * face].T, picks[f, :ncl], precision=HIGHEST)
        theirs = jnp.dot(columns[:, :face].T, picks[f, ncl:], precision=HIGHEST)
        out[f * face : (f + 1) * face] = own - permuted(select[f], theirs)


def field_into(at, faces, select, scale, coef, bases, lifts, outs, images, high, low):
    size = outs[0].shape[0]
    if lifts:
        lift, sol = lifts
        corrections = product(lift[at * size : (at + 2) * size], *split(sol[...]))
    for f in range(2):
        own, near = faces[f]
        image = own[:size] - permuted(select[at + f], near[:size])
        rows = slice(f * size, (f + 1) * size)
        if lifts:
            image = image + corrections[rows]
        if images:
            images[f][...] = image
        value = coef[...] * image
        if bases:
            value = bases[f][...] + value
        outs[f][...] = value
        high[rows], low[rows] = split(scale[at + f] * value)


def take(refs, *counts):
    groups = []
    for count in counts:
        groups.append(refs[:count])
        refs = refs[count:]
    return (*groups, refs)


def early_kernel(based, lifted, *refs):
    (scale, mat, own0, own1, near0, near1, select, coef), bases, lifts, outs, images, rest = take(
        refs, 8, 2 * based, 2 * lifted, 2, 2 * lifted
    )
    partial, high, low = rest
    faces = ((own0, near0), (own1, near1))
    field_into(0, faces, select, scale, coef, bases, lifts, outs, images, high, low)
    half = high.shape[0]
    for rows in (slice(0, half), slice(half, 2 * half)):
        partial[rows] = product(mat[rows, :half], high[...], low[...])


def crit_kernel(based, lifted, *refs):
    (scale, mat, own2, own3, near2, near3, select, coef, partial), bases, lifts, outs, images, rest = take(
        refs, 9, 2 * based, 2 * lifted, 2, 2 * lifted
    )
    out2, out3, high, low = rest
    faces = ((own2, near2), (own3, near3))
    field_into(2, faces, select, scale, coef, bases, lifts, outs, images, high, low)
    half = high.shape[0]
    size = half // 2
    value = partial[half:] + product(mat[half:, half:], high[...], low[...])
    out2[...] = value[:size]
    out3[...] = value[size:]


def late_kernel(others, *refs):
    (scale, mat, coupling), values, applied, other, rest = take(refs, 3, 4, 2, 4 * others)
    partial, carried, out0, out1, sums, high, low = rest
    size = out0.shape[0]
    ncl = coupling.shape[0]

    def inner(f, with_value):
        return jnp.sum(scale[f] * values[f][...] * with_value, axis=0, keepdims=True)

    coarse = None
    for f in range(4):
        parts = split(scale[f] * values[f][...])
        if f >= 2:
            rows = slice((f - 2) * size, (f - 1) * size)
            high[rows], low[rows] = parts
        term = product(coupling[:, f * size : (f + 1) * size], *parts)
        coarse = term if coarse is None else coarse + term
    sums[:ncl] = coarse
    sums[ncl + 1 : ncl + 2] = carried[ncl : ncl + 1]
    if others:
        sums[ncl + 2 : ncl + 3] = sum(inner(f, other[f][...]) for f in range(4))
    total = inner(2, applied[0][...]) + inner(3, applied[1][...])
    product_rows = partial[: 2 * size] + product(mat[: 2 * size, 2 * size :], high[...], low[...])
    for f, out in enumerate((out0, out1)):
        value = product_rows[f * size : (f + 1) * size]
        out[...] = value
        total = total + inner(f, value)
    sums[ncl : ncl + 1] = total


def gathered_sums(table, pick, ncl, stacked):
    for d in range(table.shape[0]):
        stacked[d * ncl : (d + 1) * ncl] = table[d, :ncl]
    rhs = permuted(pick[...], stacked[...])
    return rhs, [jnp.sum(table[:, row], axis=0, keepdims=True) for row in range(ncl, table.shape[1])]


def first_step_kernel(ncl, table, pick, matrix, rhs_out, sol_out, steps, stacked):
    rhs, (fine_dot, rho) = gathered_sums(table, pick, ncl, stacked)
    sol = jnp.dot(matrix[...], rhs, precision=HIGHEST)
    rho = 0.5 * rho
    curve = fine_dot + jnp.sum(rhs * sol, axis=0, keepdims=True)
    rhs_out[...] = rhs
    sol_out[...] = sol
    steps[0:1] = rho / curve
    steps[1:2] = rho
    steps[2:3] = fine_dot
    steps[3:] = jnp.zeros((steps.shape[0] - 3, steps.shape[1]), F32)


def second_step_kernel(ncl, table, pick, matrix, rhs0, sol0, steps0, sol_out, steps, stacked):
    rhs, (dot11, rho1, dot10) = gathered_sums(table, pick, ncl, stacked)
    sol = jnp.dot(matrix[...], rhs, precision=HIGHEST)
    step0, rho0, dot00 = (steps0[row : row + 1] for row in range(3))
    rho1 = 0.5 * rho1
    beta = rho1 / rho0
    coarse = jnp.sum((rhs + beta * rhs0[...]) * (sol + beta * sol0[...]), axis=0, keepdims=True)
    step1 = rho1 / (dot11 + 2.0 * beta * dot10 + beta * beta * dot00 + coarse)
    sol_out[...] = sol
    steps[0:1] = -step1
    steps[1:2] = -step1 * beta
    steps[2:3] = step0 + step1 * beta
    steps[3:4] = step1
    steps[4:] = jnp.zeros((steps.shape[0] - 4, steps.shape[1]), F32)


def tail_kernel(*refs):
    owns, nears, residuals, images, rest = take(refs, 4, 4, 4, 4)
    select, lift, sol, steps, out = rest
    size = out.shape[0] // 4
    parts = split(sol[...])
    for f in range(4):
        rows = slice(f * size, (f + 1) * size)
        image = owns[f][...] - permuted(select[f], nears[f][:size])
        image = image + product(lift[rows], *parts)
        out[rows] = residuals[f][...] + steps[0:1] * image + steps[1:2] * images[f][...]


def weighted_kernel(*refs):
    firsts, seconds, (steps, out) = take(refs, 4, 4)
    size = out.shape[0] // 4
    for f in range(4):
        out[f * size : (f + 1) * size] = steps[2:3] * firsts[f][...] + steps[3:4] * seconds[f][...]


def call(kernel, operands, shapes, scratch=(), specs=None):
    vmem = pl.BlockSpec(memory_space=pltpu.VMEM)
    specs = specs or {}
    return pl.pallas_call(
        kernel,
        in_specs=[specs.get(i, vmem) for i in range(len(operands))],
        out_specs=[vmem] * len(shapes),
        out_shape=[jax.ShapeDtypeStruct(s, F32) for s in shapes],
        scratch_shapes=list(scratch),
        compiler_params=pltpu.CompilerParams(vmem_limit_bytes=LIMIT),
        cost_estimate=pl.CostEstimate(flops=1024, bytes_accessed=1024, transcendentals=0),
    )(*operands)


def shards(loads, schur_flex, dirichlet, coupling, corner_index, face_lists, coarse_inverse):
    flex_mat = schur_flex[0, 0]
    prec_mat = dirichlet[0, 0]
    coupling_mat = coupling[0, 0]
    corners = corner_index[0, 0]
    face_index = face_lists[0, 0]
    load = loads[0, 0]
    ncoarse = coarse_inverse.shape[1]
    ncl, ni = coupling_mat.shape
    width = load.shape[1]
    face, half = ni // 4, ni // 2
    n_sx, n_sy = lax.axis_size("sx"), lax.axis_size("sy")
    at_x, at_y = lax.axis_index("sx"), lax.axis_index("sy")

    has = jnp.stack([at_x > 0, at_x < n_sx - 1, at_y > 0, at_y < n_sy - 1])
    scale = jnp.where(has, 2.0, 1.0).astype(F32)
    select = (face_index[:, :, None] == jnp.arange(face, dtype=jnp.int32)).astype(BF16)
    one = jnp.ones((1, width), F32)
    specs = {0: pl.BlockSpec(memory_space=pltpu.SMEM)}
    one_face = (face, width)

    parts = [pltpu.VMEM((half, width), BF16)] * 2

    def early(matrix, owns, nears, coef, bases, lifts):
        operands = [scale, matrix, *owns, *nears, select, coef, *bases, *lifts]
        shapes = [one_face] * (4 if lifts else 2) + [(ni, width)]
        kernel = functools.partial(early_kernel, bool(bases), bool(lifts))
        *fields, partial = call(kernel, operands, shapes, parts, specs)
        return fields[:2], fields[2:], partial

    def crit(matrix, owns, nears, coef, partial, bases, lifts):
        operands = [scale, matrix, *owns, *nears, select, coef, partial, *bases, *lifts]
        shapes = [one_face] * (6 if lifts else 4)
        kernel = functools.partial(crit_kernel, bool(bases), bool(lifts))
        *fields, a2, a3 = call(kernel, operands, shapes, parts, specs)
        return fields[:2], fields[2:], (a2, a3)

    def late(matrix, values, applied, partial, carried, other):
        operands = [scale, matrix, coupling_mat, *values, *applied, *other, partial, carried]
        shapes = [one_face, one_face, (ncl + 2 + bool(other), width)]
        return call(functools.partial(late_kernel, int(bool(other))), operands, shapes, parts, specs)

    def applied(matrix, owns, nears, coef, bases=(), lifts=(), carried=None, other=()):
        v01, q01, partial = early(matrix, owns[:2], nears[:2], coef, bases[:2], lifts)
        v23, q23, a23 = crit(matrix, owns[2:], nears[2:], coef, partial, bases[2:], lifts)
        values = (*v01, *v23)
        if carried is None:
            carried = jnp.zeros((ncl + 1, width), F32)
        a0, a1, sums = late(matrix, values, a23, partial, carried, other)
        return values, (*q01, *q23), (a0, a1, *a23), sums

    def exchanged(faces):
        far = facing(faces[2], faces[3], "sy")
        return (*facing(faces[0], faces[1], "sx"), *far)

    extra = -(-face // width) * ncl
    sent = call(pack_kernel, [load, coupling_mat], [(face + extra, width)] * 4)
    near = exchanged(sent)

    listed = jnp.zeros((1, ncoarse), F32).at[0, :ncl].set(corners.astype(F32))
    own_rows, _ = lax.optimization_barrier((jnp.concatenate([coarse_inverse, listed], axis=0), sent[0]))
    table, first = lax.optimization_barrier((from_all(own_rows), one))
    matrix_all = table[:, :-1].reshape(ncoarse, ncoarse)
    corners_all = table[:, -1, :ncl].astype(jnp.int32)
    coarse_ids = jnp.arange(ncoarse, dtype=jnp.int32)
    pick_all = (corners_all.reshape(1, -1) == coarse_ids[:, None]).astype(BF16)
    me = at_x * n_sy + at_y
    there = jnp.clip(jnp.stack([me - n_sy, me + n_sy, me - 1, me + 1]), 0, n_sx * n_sy - 1)
    ids = jnp.concatenate([jnp.broadcast_to(corners, (4, ncl)), corners_all[there]], axis=1)
    picks = (ids[:, :, None] == coarse_ids).astype(F32)

    residual0, _, applied0, sums = applied(prec_mat, sent, near, first)
    (lift,) = call(lift_kernel, [*near, select, coupling_mat, picks], [(ni, ncoarse)])
    near = exchanged(applied0)

    stacked = [pltpu.VMEM((n_sx * n_sy * ncl, width), F32)]
    coarse_shape, steps_shape = (ncoarse, width), (8, width)
    direction0, _, fine0, sums = applied(flex_mat, applied0, near, 0.5 * one, carried=sums)
    near = exchanged(fine0)
    rhs0, sol0, steps0 = call(
        functools.partial(first_step_kernel, ncl),
        [from_all(sums), pick_all, matrix_all],
        [coarse_shape, coarse_shape, steps_shape],
        stacked,
    )
    residual1, image0, applied1, sums = applied(prec_mat, fine0, near, -steps0[0:1], residual0, (lift, sol0))
    near = exchanged(applied1)

    precond, _, fine1, sums = applied(flex_mat, applied1, near, 0.5 * one, carried=sums, other=fine0)
    near = exchanged(fine1)
    sol1, steps1 = call(
        functools.partial(second_step_kernel, ncl),
        [from_all(sums), pick_all, matrix_all, rhs0, sol0, steps0],
        [coarse_shape, steps_shape],
        stacked,
    )
    (multipliers,) = call(weighted_kernel, [*direction0, *precond, steps1], [(ni, width)])
    operands = [*fine1, *near, *residual1, *image0, select, lift, sol1, steps1]
    (residual2,) = call(tail_kernel, operands, [(ni, width)])
    return multipliers[None, None], residual2[None, None]


def solution(mesh):
    return jax.shard_map(
        shards,
        mesh=mesh,
        in_specs=(
            P("sx", "sy", None, None),
            P("sx", "sy", None, None),
            P("sx", "sy", None, None),
            P("sx", "sy", None, None),
            P("sx", "sy", None),
            P("sx", "sy", None, None),
            P(("sx", "sy"), None),
        ),
        out_specs=(P("sx", "sy", None, None), P("sx", "sy", None, None)),
        check_vma=False,
    )
```

```python
import functools

import jax
import jax.numpy as jnp
from jax import lax
from jax.experimental import pallas as pl
from jax.experimental.pallas import tpu as pltpu
from jax.sharding import PartitionSpec as P

HIGHEST = lax.Precision.HIGHEST
F32 = jnp.float32
BF16 = jnp.bfloat16
MIB = 1024 * 1024


def shifted(block, axis, distance):
    devices = range(lax.axis_size(axis))
    route = [(i - distance, i) for i in devices if i - distance in devices]
    return lax.ppermute(block, axis, route)


def facing(low, high, axis):
    return shifted(high, axis, 1), shifted(low, axis, -1)


def to_all(rows):
    return lax.all_to_all(rows, ("sx", "sy"), 0, 0, tiled=True)


def split(x):
    high = x.astype(BF16)
    return high, (x - high.astype(F32)).astype(BF16)


def dot(a, b):
    return jnp.dot(a, b, preferred_element_type=F32)


def product(a, b_high, b_low):
    a_high, a_low = split(a)
    return dot(a_high, b_high) + (dot(a_high, b_low) + dot(a_low, b_high))


def thirds(x):
    high = x.astype(BF16)
    rest = x - high.astype(F32)
    mid = rest.astype(BF16)
    return high, mid, (rest - mid.astype(F32)).astype(BF16)


def permuted(select, rows):
    high, mid, low = thirds(rows)
    return dot(select, high) + (dot(select, mid) + dot(select, low))


def pack_kernel(load, coupling, *outs):
    face = load.shape[0] // len(outs)
    width = load.shape[1]
    ncl = coupling.shape[0]
    for f, out in enumerate(outs):
        out[:face] = load[f * face : (f + 1) * face]
        for block, at in enumerate(range(0, face, width)):
            rows = slice(face + block * ncl, face + (block + 1) * ncl)
            wide = min(width, face - at)
            if wide < width:
                out[rows] = jnp.zeros((ncl, width), F32)
            out[rows, :wide] = coupling[:, f * face + at : f * face + at + wide]


def lift_kernel(scale, near0, near1, near2, near3, select, coupling, own_pick, near_pick, out):
    face = out.shape[1] // 4
    ncl = coupling.shape[0]
    for f, near in enumerate((near0, near1, near2, near3)):
        columns = jnp.concatenate([near[at : at + ncl] for at in range(face, near.shape[0], ncl)], axis=1)
        theirs = None
        for part in thirds(columns[:, :face])[::-1]:
            term = lax.dot_general(part, select[f], (((1,), (1,)), ((), ())), preferred_element_type=F32)
            theirs = term if theirs is None else theirs + term
        own = permuted(own_pick[...], coupling[:, f * face : (f + 1) * face])
        out[:, f * face : (f + 1) * face] = (0.5 * scale[f]) * (own - permuted(near_pick[f], theirs))


def fetched(refs, slots, sems):
    copies = [pltpu.make_async_copy(ref, slots.at[i], sems.at[i]) for i, ref in enumerate(refs)]
    for copy in copies:
        copy.start()
    return copies


def field_into(at, faces, select, scale, coef, bases, outs, images, high, low):
    size = outs[0].shape[0]
    for f in range(2):
        own, near = faces[f]
        image = own[:size] - permuted(select[at + f], near[:size])
        rows = slice(f * size, (f + 1) * size)
        if images:
            images[f][...] = image
        value = coef[0:1] * image
        if bases:
            copies, slots = bases
            copies[f].wait()
            value = slots[f] + value
        outs[f][...] = value
        high[rows], low[rows] = split(scale[at + f] * value)


def take(refs, *counts):
    groups = []
    for count in counts:
        groups.append(refs[:count])
        refs = refs[count:]
    return (*groups, refs)


def corrected(coupling, columns, picked):
    return product(coupling[:, columns].T, *split(picked[...]))


def early_kernel(based, *refs):
    (scale, mat, own0, own1, near0, near1, select, coef), bases, outs, images, rest = take(
        refs, 8, 2 * based, 2, 2 * based
    )
    partial, high, low, slots, sems = rest
    bases = (fetched(bases, slots, sems), slots) if based else ()
    field_into(0, ((own0, near0), (own1, near1)), select, scale, coef, bases, outs, images, high, low)
    half = high.shape[0]
    for rows in (slice(0, half), slice(half, 2 * half)):
        partial[rows] = product(mat[rows, :half], high[...], low[...])


def crit_kernel(based, coarse, *refs):
    (scale, mat, own2, own3, near2, near3, select, coef, partial), bases, coarse_refs, outs, images, rest = take(
        refs, 9, 2 * based, 2 * coarse, 2, 2 * based
    )
    out2, out3, high, low, slots, sems = rest
    bases = (fetched(bases, slots, sems), slots) if based else ()
    field_into(2, ((own2, near2), (own3, near3)), select, scale, coef, bases, outs, images, high, low)
    half = high.shape[0]
    size = half // 2
    value = partial[half:] + product(mat[half:, half:], high[...], low[...])
    if coarse:
        coupling, picked = coarse_refs
        value = value + corrected(coupling, slice(half, 2 * half), picked)
    out2[...] = value[:size]
    out3[...] = value[size:]


def late_rows(scale, mat, values, partial, high, low):
    size = values[0].shape[0]
    for f in (2, 3):
        rows = slice((f - 2) * size, (f - 1) * size)
        high[rows], low[rows] = split(scale[f] * values[f][...])
    return partial[: 2 * size] + product(mat[: 2 * size, 2 * size :], high[...], low[...])


def inner(scale, values, others):
    return sum(
        jnp.sum(scale[f] * values[f][...] * others[f][...], axis=0, keepdims=True) for f in range(4)
    )


def prec_late_kernel(*refs):
    (scale, mat), values, applied, (partial, lift, out0, out1, dots, rhs, high, low) = take(refs, 2, 4, 2)
    size = out0.shape[0]
    value = late_rows(scale, mat, values, partial, high, low)
    out0[...] = value[:size]
    out1[...] = value[size:]
    faces = (out0, out1, *applied)
    dots[...] = inner(scale, values, faces)
    total = None
    for f in range(4):
        term = product(lift[:, f * size : (f + 1) * size], *split(faces[f][...]))
        total = term if total is None else total + term
    count, rows = rhs.shape[:2]
    for d in range(count):
        rhs[d] = total[d * rows : (d + 1) * rows]


def flex_late_kernel(others, *refs):
    (scale, mat), values, applied, other, rest = take(refs, 2, 4, 2, 4 * others)
    partial, coupling, picked, carried, out0, out1, dots, high, low, slots, sems = rest
    copies = fetched(other, slots, sems)
    size = out0.shape[0]
    value = late_rows(scale, mat, values, partial, high, low)
    value = value + corrected(coupling, slice(0, 2 * size), picked)
    out0[...] = value[:size]
    out1[...] = value[size:]
    sums = [inner(scale, values, (out0, out1, *applied)), carried[...]]
    if others:
        for copy in copies:
            copy.wait()
        sums.append(inner(scale, values, [slots.at[f] for f in range(4)]))
    for row, value in enumerate(sums):
        for d in range(dots.shape[0]):
            dots[d, row : row + 1] = value


def total_kernel(table, out):
    out[...] = jnp.broadcast_to(jnp.sum(table[...], axis=0, keepdims=True), out.shape)


def solve_kernel(table, matrix, pick, out, stacked):
    count, rows = table.shape[:2]
    for d in range(count):
        stacked[d * rows : (d + 1) * rows] = table[d]
    out[...] = permuted(pick[...], jnp.dot(matrix[...], stacked[...], precision=HIGHEST))


def first_step_kernel(table, steps):
    sums = jnp.sum(table[...], axis=0)
    rho = 0.5 * sums[1:2]
    steps[0:1] = -rho / sums[0:1]
    steps[1:2] = rho
    steps[2:3] = sums[0:1]
    steps[3:] = jnp.zeros((steps.shape[0] - 3, steps.shape[1]), F32)


def second_step_kernel(table, steps0, steps):
    sums = jnp.sum(table[...], axis=0)
    rho = 0.5 * sums[1:2]
    beta = rho / steps0[1:2]
    step = rho / (sums[0:1] + 2.0 * beta * sums[2:3] + beta * beta * steps0[2:3])
    steps[0:1] = -step
    steps[1:2] = -step * beta
    steps[2:3] = step * beta - steps0[0:1]
    steps[3:4] = step
    steps[4:] = jnp.zeros((steps.shape[0] - 4, steps.shape[1]), F32)


def stored(values, out, sems):
    size = values.shape[1]
    return [
        pltpu.make_async_copy(values.at[f], out.at[pl.ds(f * size, size)], sems.at[f]) for f in range(4)
    ]


def tail_kernel(*refs):
    loaded, (select, steps, out, slots, values, load_sems, store_sems) = take(refs, 16)
    loads = fetched(loaded, slots, load_sems)
    stores = stored(values, out, store_sems)
    for f in range(4):
        for copy in loads[4 * f : 4 * f + 4]:
            copy.wait()
        own, near, residual, image = (slots[4 * f + i] for i in range(4))
        values[f] = residual + steps[0:1] * (own - permuted(select[f], near)) + steps[1:2] * image
        stores[f].start()
    for copy in stores:
        copy.wait()


def weighted_kernel(*refs):
    loaded, (steps, out, slots, values, load_sems, store_sems) = take(refs, 8)
    loads = fetched(loaded, slots, load_sems)
    stores = stored(values, out, store_sems)
    for f in range(4):
        for copy in loads[2 * f : 2 * f + 2]:
            copy.wait()
        values[f] = steps[2:3] * slots[2 * f] + steps[3:4] * slots[2 * f + 1]
        stores[f].start()
    for copy in stores:
        copy.wait()


VMEM_SPEC = pl.BlockSpec(memory_space=pltpu.VMEM)
SMEM_SPEC = pl.BlockSpec(memory_space=pltpu.SMEM)
ANY_SPEC = pl.BlockSpec(memory_space=pl.ANY)


def call(kernel, operands, shapes, scratch=(), smem=0, anywhere=(), out_spec=VMEM_SPEC, limit=8, flops=1024):
    specs = [SMEM_SPEC if i < smem else ANY_SPEC if i in anywhere else VMEM_SPEC for i in range(len(operands))]
    return pl.pallas_call(
        kernel,
        in_specs=specs,
        out_specs=[out_spec] * len(shapes),
        out_shape=[jax.ShapeDtypeStruct(s, F32) for s in shapes],
        scratch_shapes=list(scratch),
        compiler_params=pltpu.CompilerParams(vmem_limit_bytes=limit * MIB),
        cost_estimate=pl.CostEstimate(flops=flops, bytes_accessed=1024, transcendentals=0),
    )(*operands)


def shards(loads, schur_flex, dirichlet, coupling, corner_index, face_lists, coarse_inverse):
    flex_mat = schur_flex[0, 0]
    prec_mat = dirichlet[0, 0]
    coupling_mat = coupling[0, 0]
    corners = corner_index[0, 0]
    face_index = face_lists[0, 0]
    load = loads[0, 0]
    ncoarse = coarse_inverse.shape[1]
    ncl, ni = coupling_mat.shape
    width = load.shape[1]
    face, half = ni // 4, ni // 2
    n_sx, n_sy = lax.axis_size("sx"), lax.axis_size("sy")
    at_x, at_y = lax.axis_index("sx"), lax.axis_index("sy")
    count = n_sx * n_sy

    has = jnp.stack([at_x > 0, at_x < n_sx - 1, at_y > 0, at_y < n_sy - 1])
    scale = jnp.where(has, 2.0, 1.0).astype(F32)
    select = (face_index[:, :, None] == jnp.arange(face, dtype=jnp.int32)).astype(BF16)
    one = jnp.ones((1, width), F32)
    one_face = (face, width)
    parts = [pltpu.VMEM((half, width), BF16)] * 2
    CRIT_FLOPS = 8 * 10**9

    def slots(number):
        return [pltpu.VMEM((number, face, width), F32), pltpu.SemaphoreType.DMA((number,))]

    def early(matrix, owns, nears, coef, bases):
        operands = [scale, matrix, *owns, *nears, select, coef, *bases]
        shapes = [one_face] * (4 if bases else 2) + [(ni, width)]
        kernel = functools.partial(early_kernel, bool(bases))
        *fields, partial = call(kernel, operands, shapes, parts + slots(2), smem=1, anywhere=range(8, len(operands)))
        return fields[:2], fields[2:], partial

    def crit(matrix, owns, nears, coef, partial, bases, coarse):
        operands = [scale, matrix, *owns, *nears, select, coef, partial, *bases, *coarse]
        shapes = [one_face] * (6 if bases else 4)
        kernel = functools.partial(crit_kernel, bool(bases), bool(coarse))
        anywhere = range(9, 9 + len(bases))
        *fields, a2, a3 = call(
            kernel, operands, shapes, parts + slots(2), smem=1, anywhere=anywhere, flops=CRIT_FLOPS
        )
        return fields[:2], fields[2:], (a2, a3)

    def fields_of(matrix, owns, nears, coef, bases=(), coarse=()):
        v01, q01, partial = early(matrix, owns[:2], nears[:2], coef, bases[:2])
        v23, q23, a23 = crit(matrix, owns[2:], nears[2:], coef, partial, bases[2:], coarse)
        return (*v01, *v23), (*q01, *q23), a23, partial

    def prec_late(values, a23, partial, lift):
        operands = [scale, prec_mat, *values, *a23, partial, lift]
        shapes = [one_face, one_face, (1, width), (count, ncoarse // count, width)]
        a0, a1, dots, rhs = call(prec_late_kernel, operands, shapes, parts, smem=1)
        return (a0, a1, *a23), dots, rhs

    def flex_late(values, a23, partial, picked, carried, other=()):
        operands = [scale, flex_mat, *values, *a23, *other, partial, coupling_mat, picked, carried]
        shapes = [one_face, one_face, (count, 2 + bool(other), width)]
        kernel = functools.partial(flex_late_kernel, int(bool(other)))
        a0, a1, dots = call(
            kernel, operands, shapes, parts + slots(4), smem=1, anywhere=range(8, 8 + len(other))
        )
        return (a0, a1, *a23), dots

    def exchanged(faces):
        far = facing(faces[2], faces[3], "sy")
        return (*facing(faces[0], faces[1], "sx"), *far)

    extra = -(-face // width) * ncl
    sent = call(pack_kernel, [load, coupling_mat], [(face + extra, width)] * 4)
    near = exchanged(sent)

    listed = jnp.zeros((1, ncoarse), F32).at[0, :ncl].set(corners.astype(F32))
    own_rows, _ = lax.optimization_barrier((jnp.concatenate([coarse_inverse, listed], axis=0), sent[0]))
    table = to_all(jnp.broadcast_to(own_rows[None], (count,) + own_rows.shape))
    table, first = lax.optimization_barrier((table, one))
    matrix_all = table[:, :-1].reshape(ncoarse, ncoarse)
    corners_all = table[:, -1, :ncl].astype(jnp.int32)
    coarse_ids = jnp.arange(ncoarse, dtype=jnp.int32)
    me = at_x * n_sy + at_y
    there = jnp.clip(jnp.stack([me - n_sy, me + n_sy, me - 1, me + 1]), 0, count - 1)
    own_pick = (corners[None, :] == coarse_ids[:, None]).astype(BF16)
    near_pick = (corners_all[there][:, None, :] == coarse_ids[None, :, None]).astype(BF16)
    pick = (corners[:, None] == coarse_ids[None, :]).astype(BF16)

    def picked_of(rhs):
        totals = call(total_kernel, [to_all(rhs)], [rhs.shape])[0]
        scratch = [pltpu.VMEM((ncoarse, width), F32)]
        return call(solve_kernel, [to_all(totals), matrix_all, pick], [(ncl, width)], scratch)[0]

    residual0, _, a23, partial = fields_of(prec_mat, sent, near, first)
    (lift,) = call(
        lift_kernel, [scale, *near, select, coupling_mat, own_pick, near_pick], [(ncoarse, ni)], smem=1
    )
    applied0, rho0, rhs0 = prec_late(residual0, a23, partial, lift)
    near = exchanged(applied0)
    picked0 = picked_of(rhs0)

    direction0, _, a23, partial = fields_of(flex_mat, applied0, near, 0.5 * one, (), (coupling_mat, picked0))
    fine0, dots = flex_late(direction0, a23, partial, picked0, rho0)
    near = exchanged(fine0)
    (steps0,) = call(first_step_kernel, [to_all(dots)], [(8, width)])
    residual1, image0, a23, partial = fields_of(prec_mat, fine0, near, steps0, residual0)
    applied1, rho1, rhs1 = prec_late(residual1, a23, partial, lift)
    near = exchanged(applied1)
    picked1 = picked_of(rhs1)

    precond, _, a23, partial = fields_of(flex_mat, applied1, near, 0.5 * one, (), (coupling_mat, picked1))
    fine1, dots = flex_late(precond, a23, partial, picked1, rho1, fine0)
    near = exchanged(fine1)
    (steps1,) = call(second_step_kernel, [to_all(dots), steps0], [(8, width)])
    ends = [pltpu.VMEM((4, face, width), F32)]
    store_sems = [pltpu.SemaphoreType.DMA((4,))]

    def final(kernel, groups, others):
        operands = [array for faces in zip(*groups) for array in faces]
        number = len(operands)
        (loaded, load_sems) = slots(number)
        return call(
            kernel,
            operands + others,
            [(ni, width)],
            [loaded, *ends, load_sems, *store_sems],
            anywhere=range(number),
            out_spec=ANY_SPEC,
            limit=16,
        )[0]

    multipliers = final(weighted_kernel, [direction0, precond], [steps1])
    residual2 = final(tail_kernel, [fine1, near, residual1, image0], [select, steps1])
    return multipliers[None, None], residual2[None, None]


def solution(mesh):
    return jax.shard_map(
        shards,
        mesh=mesh,
        in_specs=(
            P("sx", "sy", None, None),
            P("sx", "sy", None, None),
            P("sx", "sy", None, None),
            P("sx", "sy", None, None),
            P("sx", "sy", None),
            P("sx", "sy", None, None),
            P(("sx", "sy"), None),
        ),
        out_specs=(P("sx", "sy", None, None), P("sx", "sy", None, None)),
        check_vma=False,
    )
```

```python
import functools
import math

import jax
import jax.numpy as jnp
from jax import lax
from jax.experimental import pallas as pl
from jax.experimental.pallas import tpu as pltpu
from jax.sharding import PartitionSpec as P

HIGHEST = lax.Precision.HIGHEST
F32 = jnp.float32
BF16 = jnp.bfloat16
MIB = 1024 * 1024
LIMIT = 47
CRIT_FLOPS = 8 * 10**9


def shifted(block, axis, distance):
    devices = range(lax.axis_size(axis))
    route = [(i - distance, i) for i in devices if i - distance in devices]
    return lax.ppermute(block, axis, route)


def facing(low, high, axis):
    return shifted(high, axis, 1), shifted(low, axis, -1)


def to_all(rows):
    return lax.all_to_all(rows, ("sx", "sy"), 0, 0, tiled=True)


def split(x):
    high = x.astype(BF16)
    return high, (x - high.astype(F32)).astype(BF16)


def dot(a, b):
    return jnp.dot(a, b, preferred_element_type=F32)


def product(a, b_high, b_low):
    a_high, a_low = split(a)
    return dot(a_high, b_high) + (dot(a_high, b_low) + dot(a_low, b_high))


def thirds(x):
    high = x.astype(BF16)
    rest = x - high.astype(F32)
    mid = rest.astype(BF16)
    return high, mid, (rest - mid.astype(F32)).astype(BF16)


def permuted(select, rows):
    high, mid, low = thirds(rows)
    return dot(select, high) + (dot(select, mid) + dot(select, low))


def pack_kernel(load, coupling, *outs):
    face = load.shape[0] // len(outs)
    width = load.shape[1]
    ncl = coupling.shape[0]
    for f, out in enumerate(outs):
        out[:face] = load[f * face : (f + 1) * face]
        for block, at in enumerate(range(0, face, width)):
            rows = slice(face + block * ncl, face + (block + 1) * ncl)
            wide = min(width, face - at)
            if wide < width:
                out[rows] = jnp.zeros((ncl, width), F32)
            out[rows, :wide] = coupling[:, f * face + at : f * face + at + wide]


def lift_kernel(near0, near1, near2, near3, select, coupling, picks, out):
    face = out.shape[0] // 4
    ncl = coupling.shape[0]
    for f, near in enumerate((near0, near1, near2, near3)):
        columns = jnp.concatenate([near[at : at + ncl] for at in range(face, near.shape[0], ncl)], axis=1)
        own = jnp.dot(coupling[:, f * face : (f + 1) * face].T, picks[f, :ncl], precision=HIGHEST)
        theirs = jnp.dot(columns[:, :face].T, picks[f, ncl:], precision=HIGHEST)
        out[f * face : (f + 1) * face] = own - permuted(select[f], theirs)


def fetched(refs, slots, sems):
    copies = [pltpu.make_async_copy(ref, slots.at[i], sems.at[i]) for i, ref in enumerate(refs)]
    for copy in copies:
        copy.start()
    return copies


def prepare_kernel(first, second, out):
    blocks = pl.num_programs(0) // 2
    for at, mat in enumerate((first, second)):

        @pl.when(pl.program_id(0) // blocks == at)
        def _(mat=mat):
            out[0, 0], out[0, 1] = split(mat[...])


def streamed(mats, which, row, column, blocks, sems):
    count, _, rows, columns = blocks.shape
    copies = []
    for i in range(count):
        source = mats.at[which, :, pl.ds(row + i * rows, rows), pl.ds(column, columns)]
        copies.append(pltpu.make_async_copy(source, blocks.at[i], sems.at[i]))
        copies[-1].start()
    return copies


def block_product(block, high, low):
    return dot(block[0], high[...]) + (dot(block[0], low[...]) + dot(block[1], high[...]))


def field_into(at, faces, select, scale, coef, bases, lifts, outs, images, high, low):
    size = outs[0].shape[0]
    if lifts:
        lift, sol = lifts
        corrections = product(lift[at * size : (at + 2) * size], *split(sol[...]))
    for f in range(2):
        own, near = faces[f]
        image = own[:size] - permuted(select[at + f], near[:size])
        rows = slice(f * size, (f + 1) * size)
        if lifts:
            image = image + corrections[rows]
            images[f][...] = image
        value = coef[0:1] * image
        if bases:
            copies, slots = bases
            copies[f].wait()
            value = slots[f] + value
        outs[f][...] = value
        high[rows], low[rows] = split(scale[at + f] * value)


def take(refs, *counts):
    groups = []
    for count in counts:
        groups.append(refs[:count])
        refs = refs[count:]
    return (*groups, refs)


def early_kernel(which, based, *refs):
    (scale, mats, own0, own1, near0, near1, select, coef), bases, lifts, outs, images, rest = take(
        refs, 8, 2 * based, 2 * based, 2, 2 * based
    )
    partial, high, low, slots, sems, blocks, block_sems = rest
    bases = (fetched(bases, slots, sems), slots) if based else ()
    copies = streamed(mats, which, 0, 0, blocks, block_sems)
    field_into(0, ((own0, near0), (own1, near1)), select, scale, coef, bases, lifts, outs, images, high, low)
    rows = blocks.shape[2]
    for i, copy in enumerate(copies):
        copy.wait()
        partial[i * rows : (i + 1) * rows] = block_product(blocks.at[i], high, low)


def crit_kernel(which, based, *refs):
    (scale, mats, own2, own3, near2, near3, select, coef, partial), bases, lifts, outs, images, rest = take(
        refs, 9, 2 * based, 2 * based, 2, 2 * based
    )
    out2, out3, high, low, slots, sems, blocks, block_sems = rest
    bases = (fetched(bases, slots, sems), slots) if based else ()
    rows = blocks.shape[2]
    copies = streamed(mats, which, 2 * rows, 2 * rows, blocks, block_sems)
    field_into(2, ((own2, near2), (own3, near3)), select, scale, coef, bases, lifts, outs, images, high, low)
    for i, (copy, out) in enumerate(zip(copies, (out2, out3))):
        copy.wait()
        out[...] = partial[(2 + i) * rows : (3 + i) * rows] + block_product(blocks.at[i], high, low)


def late_kernel(which, others, *refs):
    (scale, mats, coupling), values, applied, other, rest = take(refs, 3, 4, 2, 4 * others)
    partial, carried, out0, out1, sums, high, low, slots, sems, blocks, block_sems = rest
    copies = streamed(mats, which, 0, 2 * blocks.shape[2], blocks, block_sems)
    loads = fetched(other, slots, sems)
    size = out0.shape[0]
    ncl = coupling.shape[0]
    pieces = carried.shape[0]
    lanes = carried.shape[1]

    def inner(f, with_value):
        return jnp.sum(scale[f] * values[f][...] * with_value, axis=0, keepdims=True)

    def cut(rows, at):
        count = rows.shape[0]
        for piece in range(pieces):
            sums[at + piece * count : at + (piece + 1) * count] = rows[:, piece * lanes : (piece + 1) * lanes]

    coarse = None
    for f in range(4):
        parts = split(scale[f] * values[f][...])
        if f >= 2:
            rows = slice((f - 2) * size, (f - 1) * size)
            high[rows], low[rows] = parts
        term = product(coupling[:, f * size : (f + 1) * size], *parts)
        coarse = term if coarse is None else coarse + term
    dots = pieces * ncl
    sums[dots + pieces :] = jnp.zeros((sums.shape[0] - dots - pieces, lanes), F32)
    cut(coarse, 0)
    sums[dots + pieces : dots + 2 * pieces] = carried[...]
    total = inner(2, applied[0][...]) + inner(3, applied[1][...])
    for f, (copy, out) in enumerate(zip(copies, (out0, out1))):
        copy.wait()
        value = partial[f * size : (f + 1) * size] + block_product(blocks.at[f], high, low)
        out[...] = value
        total = total + inner(f, value)
    cut(total, dots)
    if others:
        for copy in loads:
            copy.wait()
        cut(sum(inner(f, slots[f]) for f in range(4)), dots + 2 * pieces)


def gathered_sums(table, pick, ncl, stacked):
    lanes = table.shape[2]
    pieces = stacked.shape[1] // lanes
    dots = pieces * ncl
    for d in range(table.shape[0]):
        for piece in range(pieces):
            columns = slice(piece * lanes, (piece + 1) * lanes)
            stacked[d * ncl : (d + 1) * ncl, columns] = table[d, piece * ncl : (piece + 1) * ncl]
    rhs = permuted(pick[...], stacked[...])
    sums = jnp.sum(table[:, dots:], axis=0)
    rows = [
        jnp.concatenate([sums[at + piece : at + piece + 1] for piece in range(pieces)], axis=1)
        for at in range(0, 3 * pieces, pieces)
    ]
    return rhs, rows


def first_step_kernel(ncl, table, pick, matrix, rhs_out, sol_out, steps, stacked):
    rhs, (fine_dot, rho, _) = gathered_sums(table, pick, ncl, stacked)
    sol = jnp.dot(matrix[...], rhs, precision=HIGHEST)
    rho = 0.5 * rho
    curve = fine_dot + jnp.sum(rhs * sol, axis=0, keepdims=True)
    rhs_out[...] = rhs
    sol_out[...] = sol
    steps[0:1] = -rho / curve
    steps[1:2] = rho
    steps[2:3] = fine_dot
    steps[3:] = jnp.zeros((steps.shape[0] - 3, steps.shape[1]), F32)


def second_step_kernel(ncl, table, pick, matrix, rhs0, sol0, steps0, sol_out, steps, stacked):
    rhs, (dot11, rho1, dot10) = gathered_sums(table, pick, ncl, stacked)
    sol = jnp.dot(matrix[...], rhs, precision=HIGHEST)
    minus_step0, rho0, dot00 = (steps0[row : row + 1] for row in range(3))
    rho1 = 0.5 * rho1
    beta = rho1 / rho0
    coarse = jnp.sum((rhs + beta * rhs0[...]) * (sol + beta * sol0[...]), axis=0, keepdims=True)
    step1 = rho1 / (dot11 + 2.0 * beta * dot10 + beta * beta * dot00 + coarse)
    sol_out[...] = sol
    steps[0:1] = -step1
    steps[1:2] = -step1 * beta
    steps[2:3] = step1 * beta - minus_step0
    steps[3:4] = step1
    steps[4:] = jnp.zeros((steps.shape[0] - 4, steps.shape[1]), F32)


def stored(values, out, sems):
    size = values.shape[1]
    return [
        pltpu.make_async_copy(values.at[f], out.at[pl.ds(f * size, size)], sems.at[f]) for f in range(4)
    ]


def tail_kernel(*refs):
    loaded, (select, lift, sol, steps, out, slots, values, load_sems, store_sems) = take(refs, 16)
    loads = fetched(loaded, slots, load_sems)
    stores = stored(values, out, store_sems)
    parts = split(sol[...])
    size = values.shape[1]
    for f in range(4):
        correction = product(lift[f * size : (f + 1) * size], *parts)
        for copy in loads[4 * f : 4 * f + 4]:
            copy.wait()
        own, near, residual, image = (slots[4 * f + i] for i in range(4))
        new_image = own - permuted(select[f], near) + correction
        values[f] = residual + steps[0:1] * new_image + steps[1:2] * image
        stores[f].start()
    for copy in stores:
        copy.wait()


def weighted_kernel(*refs):
    loaded, (steps, out, slots, values, load_sems, store_sems) = take(refs, 8)
    loads = fetched(loaded, slots, load_sems)
    stores = stored(values, out, store_sems)
    for f in range(4):
        for copy in loads[2 * f : 2 * f + 2]:
            copy.wait()
        values[f] = steps[2:3] * slots[2 * f] + steps[3:4] * slots[2 * f + 1]
        stores[f].start()
    for copy in stores:
        copy.wait()


VMEM_SPEC = pl.BlockSpec(memory_space=pltpu.VMEM)
SMEM_SPEC = pl.BlockSpec(memory_space=pltpu.SMEM)
ANY_SPEC = pl.BlockSpec(memory_space=pl.ANY)


def call(kernel, operands, shapes, scratch=(), smem=0, anywhere=(), out_spec=VMEM_SPEC, limit=LIMIT, flops=1024):
    specs = [SMEM_SPEC if i < smem else ANY_SPEC if i in anywhere else VMEM_SPEC for i in range(len(operands))]
    return pl.pallas_call(
        kernel,
        in_specs=specs,
        out_specs=[out_spec] * len(shapes),
        out_shape=[jax.ShapeDtypeStruct(s, F32) for s in shapes],
        scratch_shapes=list(scratch),
        compiler_params=pltpu.CompilerParams(vmem_limit_bytes=limit * MIB),
        cost_estimate=pl.CostEstimate(flops=flops, bytes_accessed=1024, transcendentals=0),
    )(*operands)


def prepared(first, second):
    order = first.shape[0]
    rows = order // 4
    return pl.pallas_call(
        prepare_kernel,
        grid=(8,),
        in_specs=[
            pl.BlockSpec((rows, order), lambda i: (jnp.minimum(i, 3), 0)),
            pl.BlockSpec((rows, order), lambda i: (jnp.maximum(i - 4, 0), 0)),
        ],
        out_specs=pl.BlockSpec((1, 2, rows, order), lambda i: (i // 4, 0, i % 4, 0)),
        out_shape=jax.ShapeDtypeStruct((2, 2, order, order), BF16),
        compiler_params=pltpu.CompilerParams(vmem_limit_bytes=LIMIT * MIB),
        cost_estimate=pl.CostEstimate(flops=1024, bytes_accessed=1024, transcendentals=0),
    )(first, second)


def shards(loads, schur_flex, dirichlet, coupling, corner_index, face_lists, coarse_inverse):
    flex_mat = schur_flex[0, 0]
    prec_mat = dirichlet[0, 0]
    coupling_mat = coupling[0, 0]
    corners = corner_index[0, 0]
    face_index = face_lists[0, 0]
    load = loads[0, 0]
    ncoarse = coarse_inverse.shape[1]
    ncl, ni = coupling_mat.shape
    width = load.shape[1]
    face, half = ni // 4, ni // 2
    n_sx, n_sy = lax.axis_size("sx"), lax.axis_size("sy")
    at_x, at_y = lax.axis_index("sx"), lax.axis_index("sy")
    count = n_sx * n_sy

    has = jnp.stack([at_x > 0, at_x < n_sx - 1, at_y > 0, at_y < n_sy - 1])
    scale = jnp.where(has, 2.0, 1.0).astype(F32)
    select = (face_index[:, :, None] == jnp.arange(face, dtype=jnp.int32)).astype(BF16)
    one = jnp.ones((1, width), F32)
    one_face = (face, width)
    lanes = math.gcd(width, 128)
    sum_rows = -(-(ncl + 3) * (width // lanes) // 8) * 8
    parts = [pltpu.VMEM((half, width), BF16)] * 2

    def slots(number):
        return [pltpu.VMEM((number, face, width), F32), pltpu.SemaphoreType.DMA((number,))]

    def blocks(number):
        return [pltpu.VMEM((number, 2, face, half), BF16), pltpu.SemaphoreType.DMA((number,))]

    def early(which, owns, nears, coef, bases, lifts):
        operands = [scale, mats, *owns, *nears, select, coef, *bases, *lifts]
        shapes = [one_face] * (4 if bases else 2) + [(ni, width)]
        kernel = functools.partial(early_kernel, which, bool(bases))
        anywhere = (1, *range(8, 8 + len(bases)))
        scratch = parts + slots(2) + blocks(4)
        *fields, partial = call(kernel, operands, shapes, scratch, smem=1, anywhere=anywhere)
        return fields[:2], fields[2:], partial

    def crit(which, owns, nears, coef, partial, bases, lifts):
        operands = [scale, mats, *owns, *nears, select, coef, partial, *bases, *lifts]
        shapes = [one_face] * (6 if bases else 4)
        kernel = functools.partial(crit_kernel, which, bool(bases))
        anywhere = (1, *range(9, 9 + len(bases)))
        scratch = parts + slots(2) + blocks(2)
        *fields, a2, a3 = call(kernel, operands, shapes, scratch, smem=1, anywhere=anywhere, flops=CRIT_FLOPS)
        return fields[:2], fields[2:], (a2, a3)

    def late(which, values, applied, partial, carried, other):
        operands = [scale, mats, coupling_mat, *values, *applied, *other, partial, carried]
        shapes = [one_face, one_face, (sum_rows, lanes)]
        kernel = functools.partial(late_kernel, which, int(bool(other)))
        anywhere = (1, *range(9, 9 + len(other)))
        return call(kernel, operands, shapes, parts + slots(4) + blocks(2), smem=1, anywhere=anywhere)

    def applied(which, owns, nears, coef, bases=(), lifts=(), carried=None, other=()):
        v01, q01, partial = early(which, owns[:2], nears[:2], coef, bases[:2], lifts)
        v23, q23, a23 = crit(which, owns[2:], nears[2:], coef, partial, bases[2:], lifts)
        values = (*v01, *v23)
        at = (width // lanes) * ncl
        carried = jnp.zeros((width // lanes, lanes), F32) if carried is None else carried[at : at + width // lanes]
        a0, a1, sums = late(which, values, a23, partial, carried, other)
        return values, (*q01, *q23), (a0, a1, *a23), sums

    def exchanged(faces):
        far = facing(faces[2], faces[3], "sy")
        return (*facing(faces[0], faces[1], "sx"), *far)

    extra = -(-face // width) * ncl
    sent = call(pack_kernel, [load, coupling_mat], [(face + extra, width)] * 4)
    near = exchanged(sent)

    listed = jnp.zeros((1, ncoarse), F32).at[0, :ncl].set(corners.astype(F32))
    own_rows, _ = lax.optimization_barrier((jnp.concatenate([coarse_inverse, listed], axis=0), sent[0]))
    table = to_all(jnp.broadcast_to(own_rows[None], (count,) + own_rows.shape))
    table, first = lax.optimization_barrier((table, one))
    matrix_all = table[:, :-1].reshape(ncoarse, ncoarse)
    corners_all = table[:, -1, :ncl].astype(jnp.int32)
    coarse_ids = jnp.arange(ncoarse, dtype=jnp.int32)
    pick_all = (corners_all.reshape(1, -1) == coarse_ids[:, None]).astype(BF16)
    me = at_x * n_sy + at_y
    there = jnp.clip(jnp.stack([me - n_sy, me + n_sy, me - 1, me + 1]), 0, n_sx * n_sy - 1)
    ids = jnp.concatenate([jnp.broadcast_to(corners, (4, ncl)), corners_all[there]], axis=1)
    picks = (ids[:, :, None] == coarse_ids).astype(F32)

    def gathered(sums):
        return to_all(jnp.broadcast_to(sums[None], (count, *sums.shape)))

    mats = prepared(prec_mat, flex_mat)
    PREC, FLEX = 0, 1
    residual0, _, applied0, sums = applied(PREC, sent, near, first)
    (lift,) = call(lift_kernel, [*near, select, coupling_mat, picks], [(ni, ncoarse)])
    near = exchanged(applied0)

    stacked = [pltpu.VMEM((count * ncl, width), F32)]
    coarse_shape, steps_shape = (ncoarse, width), (8, width)
    direction0, _, fine0, sums = applied(FLEX, applied0, near, 0.5 * one, carried=sums)
    near = exchanged(fine0)
    rhs0, sol0, steps0 = call(
        functools.partial(first_step_kernel, ncl),
        [gathered(sums), pick_all, matrix_all],
        [coarse_shape, coarse_shape, steps_shape],
        stacked,
    )
    residual1, image0, applied1, sums = applied(PREC, fine0, near, steps0, residual0, (lift, sol0))
    near = exchanged(applied1)

    precond, _, fine1, sums = applied(FLEX, applied1, near, 0.5 * one, carried=sums, other=fine0)
    near = exchanged(fine1)
    sol1, steps1 = call(
        functools.partial(second_step_kernel, ncl),
        [gathered(sums), pick_all, matrix_all, rhs0, sol0, steps0],
        [coarse_shape, steps_shape],
        stacked,
    )
    ends = [pltpu.VMEM((4, face, width), F32)]
    store_sems = [pltpu.SemaphoreType.DMA((4,))]

    def final(kernel, groups, others):
        operands = [array for faces in zip(*groups) for array in faces]
        number = len(operands)
        (loaded, load_sems) = slots(number)
        return call(
            kernel,
            operands + others,
            [(ni, width)],
            [loaded, *ends, load_sems, *store_sems],
            anywhere=range(number),
            out_spec=ANY_SPEC,
        )[0]

    multipliers = final(weighted_kernel, [direction0, precond], [steps1])
    residual2 = final(tail_kernel, [fine1, near, residual1, image0], [select, lift, sol1, steps1])
    return multipliers[None, None], residual2[None, None]


def solution(mesh):
    return jax.shard_map(
        shards,
        mesh=mesh,
        in_specs=(
            P("sx", "sy", None, None),
            P("sx", "sy", None, None),
            P("sx", "sy", None, None),
            P("sx", "sy", None, None),
            P("sx", "sy", None),
            P("sx", "sy", None, None),
            P(("sx", "sy"), None),
        ),
        out_specs=(P("sx", "sy", None, None), P("sx", "sy", None, None)),
        check_vma=False,
    )
```

```python
import functools

import jax
import jax.numpy as jnp
from jax import lax
from jax.experimental import pallas as pl
from jax.experimental.pallas import tpu as pltpu
from jax.sharding import PartitionSpec as P

HIGHEST = lax.Precision.HIGHEST
F32 = jnp.float32
BF16 = jnp.bfloat16
LIMIT = 8 * 1024 * 1024
CRIT_FLOPS = 8 * 10**9


def shifted(block, axis, distance):
    devices = range(lax.axis_size(axis))
    route = [(i - distance, i) for i in devices if i - distance in devices]
    return lax.ppermute(block, axis, route)


def facing(low, high, axis):
    return shifted(high, axis, 1), shifted(low, axis, -1)


def swapped(block, axis, bit):
    return lax.ppermute(block, axis, [(i, i ^ bit) for i in range(lax.axis_size(axis))])


def bits_of(axis):
    return [1 << i for i in range((lax.axis_size(axis) - 1).bit_length())]


def from_all(rows):
    for axis in ("sy", "sx"):
        for bit in bits_of(axis):
            other = swapped(rows, axis, bit)
            low = (lax.axis_index(axis) & bit) == 0
            rows = jnp.concatenate([jnp.where(low, rows, other), jnp.where(low, other, rows)], axis=0)
    return rows


def summed(kept, sent):
    total = kept + swapped(sent, "sx", 1)
    for axis, bits in (("sx", bits_of("sx")[1:]), ("sy", bits_of("sy"))):
        for bit in bits:
            total = total + swapped(total, axis, bit)
    return total


def joined(half):
    other = swapped(half, "sx", 1)
    low = (lax.axis_index("sx") & 1) == 0
    return jnp.concatenate([jnp.where(low, half, other), jnp.where(low, other, half)], axis=1)


def split(x):
    high = x.astype(BF16)
    return high, (x - high.astype(F32)).astype(BF16)


def dot(a, b):
    return jnp.dot(a, b, preferred_element_type=F32)


def product(a, b_high, b_low):
    a_high, a_low = split(a)
    return dot(a_high, b_high) + (dot(a_high, b_low) + dot(a_low, b_high))


def thirds(x):
    high = x.astype(BF16)
    rest = x - high.astype(F32)
    mid = rest.astype(BF16)
    return high, mid, (rest - mid.astype(F32)).astype(BF16)


def permuted(select, rows):
    high, mid, low = thirds(rows)
    return dot(select, high) + (dot(select, mid) + dot(select, low))


def pack_kernel(load, coupling, *outs):
    face = load.shape[0] // len(outs)
    width = load.shape[1]
    ncl = coupling.shape[0]
    for f, out in enumerate(outs):
        out[:face] = load[f * face : (f + 1) * face]
        for block, at in enumerate(range(0, face, width)):
            rows = slice(face + block * ncl, face + (block + 1) * ncl)
            wide = min(width, face - at)
            if wide < width:
                out[rows] = jnp.zeros((ncl, width), F32)
            out[rows, :wide] = coupling[:, f * face + at : f * face + at + wide]


def lift_kernel(near0, near1, near2, near3, select, coupling, picks, out):
    face = out.shape[0] // 4
    ncl = coupling.shape[0]
    for f, near in enumerate((near0, near1, near2, near3)):
        columns = jnp.concatenate([near[at : at + ncl] for at in range(face, near.shape[0], ncl)], axis=1)
        own = jnp.dot(coupling[:, f * face : (f + 1) * face].T, picks[f, :ncl], precision=HIGHEST)
        theirs = jnp.dot(columns[:, :face].T, picks[f, ncl:], precision=HIGHEST)
        out[f * face : (f + 1) * face] = own - permuted(select[f], theirs)


def field_into(at, faces, select, scale, coef, bases, lifts, outs, images, high, low):
    size = outs[0].shape[0]
    if lifts:
        lift, sol = lifts
        corrections = product(lift[at * size : (at + 2) * size], *split(sol[...]))
    for f in range(2):
        own, near = faces[f]
        image = own[:size] - permuted(select[at + f], near[:size])
        rows = slice(f * size, (f + 1) * size)
        if lifts:
            image = image + corrections[rows]
        if images:
            images[f][...] = image
        value = coef[0:1] * image
        if bases:
            value = bases[f][...] + value
        outs[f][...] = value
        high[rows], low[rows] = split(scale[at + f] * value)


def take(refs, *counts):
    groups = []
    for count in counts:
        groups.append(refs[:count])
        refs = refs[count:]
    return (*groups, refs)


def early_kernel(based, lifted, *refs):
    (scale, mat, own0, own1, near0, near1, select, coef), bases, lifts, outs, images, rest = take(
        refs, 8, 2 * based, 2 * lifted, 2, 2 * lifted
    )
    partial, high, low = rest
    faces = ((own0, near0), (own1, near1))
    field_into(0, faces, select, scale, coef, bases, lifts, outs, images, high, low)
    half = high.shape[0]
    for rows in (slice(0, half), slice(half, 2 * half)):
        partial[rows] = product(mat[rows, :half], high[...], low[...])


def crit_kernel(based, lifted, *refs):
    (scale, mat, own2, own3, near2, near3, select, coef, partial), bases, lifts, outs, images, rest = take(
        refs, 9, 2 * based, 2 * lifted, 2, 2 * lifted
    )
    out2, out3, high, low = rest
    faces = ((own2, near2), (own3, near3))
    field_into(2, faces, select, scale, coef, bases, lifts, outs, images, high, low)
    half = high.shape[0]
    size = half // 2
    value = partial[half:] + product(mat[half:, half:], high[...], low[...])
    out2[...] = value[:size]
    out3[...] = value[size:]


def late_rows(scale, mat, values, partial, high, low):
    size = values[0].shape[0]
    for f in (2, 3):
        rows = slice((f - 2) * size, (f - 1) * size)
        high[rows], low[rows] = split(scale[f] * values[f][...])
    return partial[: 2 * size] + product(mat[: 2 * size, 2 * size :], high[...], low[...])


def inner(scale, values, others):
    return sum(
        jnp.sum(scale[f] * values[f][...] * others[f][...], axis=0, keepdims=True) for f in range(4)
    )


def prec_late_kernel(*refs):
    (scale, mat), values, applied, (partial, out0, out1, dots, high, low) = take(refs, 2, 4, 2)
    size = out0.shape[0]
    value = late_rows(scale, mat, values, partial, high, low)
    out0[...] = value[:size]
    out1[...] = value[size:]
    dots[...] = inner(scale, values, (out0, out1, *applied))


def flex_late_kernel(others, *refs):
    (scale, even, mat), values, applied, other, rest = take(refs, 3, 4, 2, 4 * others)
    partial, coupling, pick, carried, out0, out1, kept, sent, high, low = rest
    size = out0.shape[0]
    coarse = None
    for f in range(4):
        term = product(coupling[:, f * size : (f + 1) * size], *split(scale[f] * values[f][...]))
        coarse = term if coarse is None else coarse + term
    value = late_rows(scale, mat, values, partial, high, low)
    out0[...] = value[:size]
    out1[...] = value[size:]
    rows = [inner(scale, values, (out0, out1, *applied)), carried[...]]
    if others:
        rows.append(inner(scale, values, other))
    ncoarse = pick.shape[0]
    end = ncoarse + len(rows)
    half = kept.shape[1]

    def halves(at, values):
        low, high = values[:, :half], values[:, half:]
        kept[at : at + values.shape[0]] = jnp.where(even[0] == 1, low, high)
        sent[at : at + values.shape[0]] = jnp.where(even[0] == 1, high, low)

    halves(0, permuted(pick[...], coarse))
    for at, row in enumerate(rows):
        halves(ncoarse + at, row)
    halves(end, jnp.zeros((kept.shape[0] - end, 2 * half), F32))


def first_step_kernel(total, matrix, out):
    ncoarse = matrix.shape[0]
    rhs = total[:ncoarse]
    sol = jnp.dot(matrix[...], rhs, precision=HIGHEST)
    fine_dot = total[ncoarse : ncoarse + 1]
    rho = 0.5 * total[ncoarse + 1 : ncoarse + 2]
    curve = fine_dot + jnp.sum(rhs * sol, axis=0, keepdims=True)
    out[:ncoarse] = sol
    out[ncoarse : ncoarse + 1] = -rho / curve
    out[ncoarse + 1 : ncoarse + 2] = rho
    out[ncoarse + 2 : ncoarse + 3] = fine_dot
    out[ncoarse + 3 :] = jnp.zeros((out.shape[0] - ncoarse - 3, out.shape[1]), F32)


def second_step_kernel(total, matrix, total0, out0, out):
    ncoarse = matrix.shape[0]
    rhs = total[:ncoarse]
    sol = jnp.dot(matrix[...], rhs, precision=HIGHEST)
    dot11, rho1, dot10 = (total[ncoarse + row : ncoarse + row + 1] for row in range(3))
    minus_step0, rho0, dot00 = (out0[ncoarse + row : ncoarse + row + 1] for row in range(3))
    rho1 = 0.5 * rho1
    beta = rho1 / rho0
    coarse = jnp.sum((rhs + beta * total0[:ncoarse]) * (sol + beta * out0[:ncoarse]), axis=0, keepdims=True)
    step1 = rho1 / (dot11 + 2.0 * beta * dot10 + beta * beta * dot00 + coarse)
    out[:ncoarse] = sol
    out[ncoarse : ncoarse + 1] = -step1
    out[ncoarse + 1 : ncoarse + 2] = -step1 * beta
    out[ncoarse + 2 : ncoarse + 3] = step1 * beta - minus_step0
    out[ncoarse + 3 : ncoarse + 4] = step1
    out[ncoarse + 4 :] = jnp.zeros((out.shape[0] - ncoarse - 4, out.shape[1]), F32)


def stored(values, out, sems):
    size = values.shape[1]
    return [
        pltpu.make_async_copy(values.at[f], out.at[pl.ds(f * size, size)], sems.at[f]) for f in range(4)
    ]


def tail_kernel(*refs):
    owns, nears, residuals, images, (select, lift, sol, steps, out, values, sems) = take(refs, 4, 4, 4, 4)
    stores = stored(values, out, sems)
    parts = split(sol[...])
    size = values.shape[1]
    for f in range(4):
        image = owns[f][...] - permuted(select[f], nears[f][...]) + product(lift[f * size : (f + 1) * size], *parts)
        values[f] = residuals[f][...] + steps[0:1] * image + steps[1:2] * images[f][...]
        stores[f].start()
    for copy in stores:
        copy.wait()


def weighted_kernel(*refs):
    firsts, seconds, (steps, out, values, sems) = take(refs, 4, 4)
    stores = stored(values, out, sems)
    for f in range(4):
        values[f] = steps[2:3] * firsts[f][...] + steps[3:4] * seconds[f][...]
        stores[f].start()
    for copy in stores:
        copy.wait()


VMEM_SPEC = pl.BlockSpec(memory_space=pltpu.VMEM)
SMEM_SPEC = pl.BlockSpec(memory_space=pltpu.SMEM)
ANY_SPEC = pl.BlockSpec(memory_space=pl.ANY)


def call(kernel, operands, shapes, scratch=(), smem=0, out_spec=VMEM_SPEC, flops=1024):
    return pl.pallas_call(
        kernel,
        in_specs=[SMEM_SPEC if i < smem else VMEM_SPEC for i in range(len(operands))],
        out_specs=[out_spec] * len(shapes),
        out_shape=[jax.ShapeDtypeStruct(s, F32) for s in shapes],
        scratch_shapes=list(scratch),
        compiler_params=pltpu.CompilerParams(vmem_limit_bytes=LIMIT),
        cost_estimate=pl.CostEstimate(flops=flops, bytes_accessed=1024, transcendentals=0),
    )(*operands)


def shards(loads, schur_flex, dirichlet, coupling, corner_index, face_lists, coarse_inverse):
    flex_mat = schur_flex[0, 0]
    prec_mat = dirichlet[0, 0]
    coupling_mat = coupling[0, 0]
    corners = corner_index[0, 0]
    face_index = face_lists[0, 0]
    load = loads[0, 0]
    ncoarse = coarse_inverse.shape[1]
    ncl, ni = coupling_mat.shape
    width = load.shape[1]
    face, half = ni // 4, ni // 2
    n_sx, n_sy = lax.axis_size("sx"), lax.axis_size("sy")
    at_x, at_y = lax.axis_index("sx"), lax.axis_index("sy")
    count = n_sx * n_sy

    has = jnp.stack([at_x > 0, at_x < n_sx - 1, at_y > 0, at_y < n_sy - 1])
    scale = jnp.where(has, 2.0, 1.0).astype(F32)
    select = (face_index[:, :, None] == jnp.arange(face, dtype=jnp.int32)).astype(BF16)
    one = jnp.ones((1, width), F32)
    one_face = (face, width)
    parts = [pltpu.VMEM((half, width), BF16)] * 2

    def early(matrix, owns, nears, coef, bases, lifts):
        operands = [scale, matrix, *owns, *nears, select, coef, *bases, *lifts]
        shapes = [one_face] * (4 if lifts else 2) + [(ni, width)]
        kernel = functools.partial(early_kernel, bool(bases), bool(lifts))
        *fields, partial = call(kernel, operands, shapes, parts, smem=1)
        return fields[:2], fields[2:], partial

    def crit(matrix, owns, nears, coef, partial, bases, lifts):
        operands = [scale, matrix, *owns, *nears, select, coef, partial, *bases, *lifts]
        shapes = [one_face] * (6 if lifts else 4)
        kernel = functools.partial(crit_kernel, bool(bases), bool(lifts))
        *fields, a2, a3 = call(kernel, operands, shapes, parts, smem=1, flops=CRIT_FLOPS)
        return fields[:2], fields[2:], (a2, a3)

    def fields_of(matrix, owns, nears, coef, bases=(), lifts=()):
        v01, q01, partial = early(matrix, owns[:2], nears[:2], coef, bases[:2], lifts)
        v23, q23, a23 = crit(matrix, owns[2:], nears[2:], coef, partial, bases[2:], lifts)
        return (*v01, *v23), (*q01, *q23), a23, partial

    def prec_late(values, a23, partial):
        operands = [scale, prec_mat, *values, *a23, partial]
        a0, a1, dots = call(prec_late_kernel, operands, [one_face, one_face, (1, width)], parts, smem=1)
        return (a0, a1, *a23), dots

    def flex_late(values, a23, partial, carried, other=()):
        operands = [scale, even, flex_mat, *values, *a23, *other, partial, coupling_mat, own_pick, carried]
        shapes = [one_face, one_face, (ncoarse + 8, width // 2), (ncoarse + 8, width // 2)]
        kernel = functools.partial(flex_late_kernel, int(bool(other)))
        a0, a1, kept, sent = call(kernel, operands, shapes, parts, smem=2)
        return (a0, a1, *a23), summed(kept, sent)

    def exchanged(faces):
        far = facing(faces[2], faces[3], "sy")
        return (*facing(faces[0], faces[1], "sx"), *far)

    def tied(total, near):
        return lax.optimization_barrier((total, *near))

    extra = -(-face // width) * ncl
    sent = call(pack_kernel, [load, coupling_mat], [(face + extra, width)] * 4)
    near = exchanged(sent)

    listed = jnp.zeros((1, ncoarse), F32).at[0, :ncl].set(corners.astype(F32))
    own_rows, _ = lax.optimization_barrier((jnp.concatenate([coarse_inverse, listed], axis=0), sent[0]))
    table = from_all(own_rows[None])
    matrix_all = table[:, :-1].reshape(ncoarse, ncoarse)
    corners_all = table[:, -1, :ncl].astype(jnp.int32)
    coarse_ids = jnp.arange(ncoarse, dtype=jnp.int32)
    own_pick = (corners[None, :] == coarse_ids[:, None]).astype(BF16)
    even = (1 - (at_x & 1)).astype(jnp.int32).reshape(1)
    me = at_x * n_sy + at_y
    there = jnp.clip(jnp.stack([me - n_sy, me + n_sy, me - 1, me + 1]), 0, n_sx * n_sy - 1)
    ids = jnp.concatenate([jnp.broadcast_to(corners, (4, ncl)), corners_all[there]], axis=1)
    picks = (ids[:, :, None] == coarse_ids).astype(F32)

    residual0, _, a23, partial = fields_of(prec_mat, sent, near, one)
    applied0, rho0 = prec_late(residual0, a23, partial)
    (lift,) = call(lift_kernel, [*near, select, coupling_mat, picks], [(ni, ncoarse)])
    near = exchanged(applied0)

    step_shape = (ncoarse + 8, width // 2)
    direction0, _, a23, partial = fields_of(flex_mat, applied0, near, 0.5 * one)
    fine0, total0 = flex_late(direction0, a23, partial, rho0)
    near = exchanged(fine0)
    total0, *near = tied(total0, near)
    (half0,) = call(first_step_kernel, [total0, matrix_all], [step_shape])
    whole0 = joined(half0)
    lifts = (lift, whole0[:ncoarse])
    residual1, image0, a23, partial = fields_of(prec_mat, fine0, near, whole0[ncoarse:], residual0, lifts)
    applied1, rho1 = prec_late(residual1, a23, partial)
    near = exchanged(applied1)

    precond, _, a23, partial = fields_of(flex_mat, applied1, near, 0.5 * one)
    fine1, total1 = flex_late(precond, a23, partial, rho1, fine0)
    near = exchanged(fine1)
    total1, *near = tied(total1, near)
    (half1,) = call(second_step_kernel, [total1, matrix_all, total0, half0], [step_shape])
    whole1 = joined(half1)
    sol1, steps1 = whole1[:ncoarse], whole1[ncoarse:]

    def final(kernel, operands):
        ends = [pltpu.VMEM((4, face, width), F32), pltpu.SemaphoreType.DMA((4,))]
        return call(kernel, operands, [(ni, width)], ends, out_spec=ANY_SPEC)[0]

    multipliers = final(weighted_kernel, [*direction0, *precond, steps1])
    residual2 = final(tail_kernel, [*fine1, *near, *residual1, *image0, select, lift, sol1, steps1])
    return multipliers[None, None], residual2[None, None]


def solution(mesh):
    return jax.shard_map(
        shards,
        mesh=mesh,
        in_specs=(
            P("sx", "sy", None, None),
            P("sx", "sy", None, None),
            P("sx", "sy", None, None),
            P("sx", "sy", None, None),
            P("sx", "sy", None),
            P("sx", "sy", None, None),
            P(("sx", "sy"), None),
        ),
        out_specs=(P("sx", "sy", None, None), P("sx", "sy", None, None)),
        check_vma=False,
    )
```

```python
import functools

import jax
import jax.numpy as jnp
from jax import lax
from jax.experimental import pallas as pl
from jax.experimental.pallas import tpu as pltpu
from jax.sharding import PartitionSpec as P

HIGHEST = lax.Precision.HIGHEST
F32 = jnp.float32
BF16 = jnp.bfloat16
LIMIT = 8 * 1024 * 1024
CRIT_FLOPS = 8 * 10**9


def swapped(block, axis, bit):
    return lax.ppermute(block, axis, [(i, i ^ bit) for i in range(lax.axis_size(axis))])


def swapped_between(block, axis):
    route = []
    for i in range(1, lax.axis_size(axis) - 1, 2):
        route += [(i, i + 1), (i + 1, i)]
    return lax.ppermute(block, axis, route)


def exchanged(slots):
    between_y = swapped_between(slots[3], "sy")
    within_y = swapped(slots[2], "sy", 1)
    between_x = swapped_between(slots[1], "sx")
    return swapped(slots[0], "sx", 1), between_x, within_y, between_y


def bits_of(axis):
    return [1 << i for i in range((lax.axis_size(axis) - 1).bit_length())]


def steps_of():
    return [("sy", 1)] + [("sx", bit) for bit in bits_of("sx")] + [("sy", bit) for bit in bits_of("sy")[1:]]


def summed(rows):
    for axis, bit in steps_of():
        rows = rows + swapped(rows, axis, bit)
    return rows


def from_all(rows):
    for axis, bit in steps_of():
        rows = jnp.concatenate([rows, swapped(rows, axis, bit)], axis=0)
    return rows


def split(x):
    high = x.astype(BF16)
    return high, (x - high.astype(F32)).astype(BF16)


def dot(a, b):
    return jnp.dot(a, b, preferred_element_type=F32)


def product(a, b_high, b_low):
    a_high, a_low = split(a)
    return dot(a_high, b_high) + (dot(a_high, b_low) + dot(a_low, b_high))


def thirds(x):
    high = x.astype(BF16)
    rest = x - high.astype(F32)
    mid = rest.astype(BF16)
    return high, mid, (rest - mid.astype(F32)).astype(BF16)


def permuted(select, rows):
    high, mid, low = thirds(rows)
    return dot(select, high) + (dot(select, mid) + dot(select, low))


def pair(flag, first, second):
    return jnp.where(flag == 1.0, second, first), jnp.where(flag == 1.0, first, second)


def faces_of(flags, slots):
    return (*pair(flags[4], slots[0], slots[1]), *pair(flags[5], slots[2], slots[3]))


def pack_kernel(flags, load, coupling, corners, *outs):
    face = load.shape[0] // 4
    width = load.shape[1]
    ncl = coupling.shape[0]
    for axis in range(2):
        faces = (2 * axis, 2 * axis + 1)
        slots = outs[2 * axis : 2 * axis + 2]

        def put(rows, columns, values, slots=slots, axis=axis):
            first, second = pair(flags[4 + axis], *values)[::-1]
            slots[0][rows, columns] = second
            slots[1][rows, columns] = first

        put(slice(0, face), slice(0, width), [load[f * face : (f + 1) * face] for f in faces])
        for block, at in enumerate(range(0, face, width)):
            rows = slice(face + block * ncl, face + (block + 1) * ncl)
            wide = min(width, face - at)
            put(rows, slice(0, wide), [coupling[:, f * face + at : f * face + at + wide] for f in faces])
            if wide < width:
                listed = jnp.broadcast_to(corners[...], (ncl, width - wide))
                put(rows, slice(wide, width), [listed, listed])


def lift_kernel(flags, near0, near1, near2, near3, select, coupling, corners, out):
    face = out.shape[0] // 4
    ncoarse = out.shape[1]
    ncl = coupling.shape[0]
    ids = lax.broadcasted_iota(jnp.int32, (ncl, ncoarse), 1).astype(F32)
    own_pick = (corners[...] == ids).astype(F32)
    nears = faces_of(flags, [near[face:] for near in (near0, near1, near2, near3)])
    for f, near in enumerate(nears):
        columns = jnp.concatenate([near[at : at + ncl] for at in range(0, near.shape[0], ncl)], axis=1)
        near_pick = (columns[:, face : face + 1] == ids).astype(F32)
        own = jnp.dot(coupling[:, f * face : (f + 1) * face].T, own_pick, precision=HIGHEST)
        theirs = jnp.dot(columns[:, :face].T, near_pick, precision=HIGHEST)
        out[f * face : (f + 1) * face] = own - permuted(select[f], theirs)


def field_into(at, owns, nears, select, flags, coef, bases, lifts, outs, images, high, low):
    size = outs[0].shape[0]
    if lifts:
        lift, sol = lifts
        corrections = product(lift[at * size : (at + 2) * size], *split(sol[...]))
    owns = pair(flags[4 + at // 2], *(own[:size] for own in owns))
    nears = pair(flags[4 + at // 2], *(near[:size] for near in nears))
    for f in range(2):
        image = owns[f] - permuted(select[at + f], nears[f])
        rows = slice(f * size, (f + 1) * size)
        if lifts:
            image = image + corrections[rows]
        if images:
            images[f][...] = image
        value = coef[0:1] * image
        if bases:
            value = bases[f][...] + value
        outs[f][...] = value
        high[rows], low[rows] = split(flags[at + f] * value)


def take(refs, *counts):
    groups = []
    for count in counts:
        groups.append(refs[:count])
        refs = refs[count:]
    return (*groups, refs)


def early_kernel(based, lifted, *refs):
    (flags, mat), owns, nears, (select, coef), bases, lifts, outs, images, rest = take(
        refs, 2, 2, 2, 2, 2 * based, 2 * lifted, 2, 2 * lifted
    )
    partial, high, low = rest
    field_into(0, owns, nears, select, flags, coef, bases, lifts, outs, images, high, low)
    half = high.shape[0]
    for rows in (slice(0, half), slice(half, 2 * half)):
        partial[rows] = product(mat[rows, :half], high[...], low[...])


def crit_kernel(based, lifted, *refs):
    (flags, mat), owns, nears, (select, coef, partial), bases, lifts, outs, images, rest = take(
        refs, 2, 2, 2, 3, 2 * based, 2 * lifted, 2, 2 * lifted
    )
    slot2, slot3, high, low = rest
    field_into(2, owns, nears, select, flags, coef, bases, lifts, outs, images, high, low)
    half = high.shape[0]
    size = half // 2
    value = partial[half:] + product(mat[half:, half:], high[...], low[...])
    slot3[...], slot2[...] = pair(flags[5], value[size:], value[:size])


def late_rows(flags, mat, values, partial, high, low, slots):
    size = values[0].shape[0]
    for f in (2, 3):
        rows = slice((f - 2) * size, (f - 1) * size)
        high[rows], low[rows] = split(flags[f] * values[f][...])
    value = partial[: 2 * size] + product(mat[: 2 * size, 2 * size :], high[...], low[...])
    slots[1][...], slots[0][...] = pair(flags[4], value[size:], value[:size])
    return faces_of(flags, [slot[...] for slot in slots])


def inner(flags, values, others):
    return sum(jnp.sum(flags[f] * values[f][...] * others[f], axis=0, keepdims=True) for f in range(4))


def prec_late_kernel(*refs):
    (flags, mat), values, applied, (partial, slot0, slot1, dots, high, low) = take(refs, 2, 4, 2)
    dots[...] = inner(flags, values, late_rows(flags, mat, values, partial, high, low, (slot0, slot1, *applied)))


def flex_late_kernel(others, *refs):
    (flags, mat), values, applied, other, rest = take(refs, 2, 4, 2, 4 * others)
    partial, coupling, pick, carried, slot0, slot1, sums, high, low = rest
    size = slot0.shape[0]
    coarse = None
    for f in range(4):
        term = product(coupling[:, f * size : (f + 1) * size], *split(flags[f] * values[f][...]))
        coarse = term if coarse is None else coarse + term
    faces = late_rows(flags, mat, values, partial, high, low, (slot0, slot1, *applied))
    rows = [inner(flags, values, faces), carried[...]]
    if others:
        rows.append(inner(flags, values, faces_of(flags, [slot[...] for slot in other])))
    ncoarse = pick.shape[0]
    sums[:ncoarse] = permuted(pick[...], coarse)
    for at, row in enumerate(rows):
        sums[ncoarse + at : ncoarse + at + 1] = row
    end = ncoarse + len(rows)
    sums[end:] = jnp.zeros((sums.shape[0] - end, sums.shape[1]), F32)


def first_step_kernel(total, matrix, order, out):
    ncoarse = matrix.shape[0]
    rhs = total[:ncoarse]
    sol = permuted(order[...], jnp.dot(matrix[...], rhs, precision=HIGHEST))
    fine_dot = total[ncoarse : ncoarse + 1]
    rho = 0.5 * total[ncoarse + 1 : ncoarse + 2]
    curve = fine_dot + jnp.sum(rhs * sol, axis=0, keepdims=True)
    out[:ncoarse] = sol
    out[ncoarse : ncoarse + 1] = -rho / curve
    out[ncoarse + 1 : ncoarse + 2] = rho
    out[ncoarse + 2 : ncoarse + 3] = fine_dot
    out[ncoarse + 3 :] = jnp.zeros((out.shape[0] - ncoarse - 3, out.shape[1]), F32)


def second_step_kernel(total, matrix, order, total0, out0, out):
    ncoarse = matrix.shape[0]
    rhs = total[:ncoarse]
    sol = permuted(order[...], jnp.dot(matrix[...], rhs, precision=HIGHEST))
    dot11, rho1, dot10 = (total[ncoarse + row : ncoarse + row + 1] for row in range(3))
    minus_step0, rho0, dot00 = (out0[ncoarse + row : ncoarse + row + 1] for row in range(3))
    rho1 = 0.5 * rho1
    beta = rho1 / rho0
    coarse = jnp.sum((rhs + beta * total0[:ncoarse]) * (sol + beta * out0[:ncoarse]), axis=0, keepdims=True)
    step1 = rho1 / (dot11 + 2.0 * beta * dot10 + beta * beta * dot00 + coarse)
    out[:ncoarse] = sol
    out[ncoarse : ncoarse + 1] = -step1
    out[ncoarse + 1 : ncoarse + 2] = -step1 * beta
    out[ncoarse + 2 : ncoarse + 3] = step1 * beta - minus_step0
    out[ncoarse + 3 : ncoarse + 4] = step1
    out[ncoarse + 4 :] = jnp.zeros((out.shape[0] - ncoarse - 4, out.shape[1]), F32)


def stored(values, out, sems):
    size = values.shape[1]
    return [
        pltpu.make_async_copy(values.at[f], out.at[pl.ds(f * size, size)], sems.at[f]) for f in range(4)
    ]


def tail_kernel(*refs):
    (flags,), owns, nears, residuals, images, (select, lift, sol, steps, out, values, sems) = take(
        refs, 1, 4, 4, 4, 4
    )
    stores = stored(values, out, sems)
    parts = split(sol[...])
    size = values.shape[1]
    owns = faces_of(flags, [own[...] for own in owns])
    nears = faces_of(flags, [near[...] for near in nears])
    for f in range(4):
        image = owns[f] - permuted(select[f], nears[f]) + product(lift[f * size : (f + 1) * size], *parts)
        values[f] = residuals[f][...] + steps[0:1] * image + steps[1:2] * images[f][...]
        stores[f].start()
    for copy in stores:
        copy.wait()


def weighted_kernel(*refs):
    firsts, seconds, (steps, out, values, sems) = take(refs, 4, 4)
    stores = stored(values, out, sems)
    for f in range(4):
        values[f] = steps[2:3] * firsts[f][...] + steps[3:4] * seconds[f][...]
        stores[f].start()
    for copy in stores:
        copy.wait()


VMEM_SPEC = pl.BlockSpec(memory_space=pltpu.VMEM)
SMEM_SPEC = pl.BlockSpec(memory_space=pltpu.SMEM)
ANY_SPEC = pl.BlockSpec(memory_space=pl.ANY)


def call(kernel, operands, shapes, scratch=(), smem=0, out_spec=VMEM_SPEC, flops=1024):
    return pl.pallas_call(
        kernel,
        in_specs=[SMEM_SPEC if i < smem else VMEM_SPEC for i in range(len(operands))],
        out_specs=[out_spec] * len(shapes),
        out_shape=[jax.ShapeDtypeStruct(s, F32) for s in shapes],
        scratch_shapes=list(scratch),
        compiler_params=pltpu.CompilerParams(vmem_limit_bytes=LIMIT),
        cost_estimate=pl.CostEstimate(flops=flops, bytes_accessed=1024, transcendentals=0),
    )(*operands)


def shards(loads, schur_flex, dirichlet, coupling, corner_index, face_lists, coarse_inverse):
    flex_mat = schur_flex[0, 0]
    prec_mat = dirichlet[0, 0]
    coupling_mat = coupling[0, 0]
    corners = corner_index[0, 0]
    face_index = face_lists[0, 0]
    load = loads[0, 0]
    ncoarse = coarse_inverse.shape[1]
    ncl, ni = coupling_mat.shape
    width = load.shape[1]
    face, half = ni // 4, ni // 2
    n_sx, n_sy = lax.axis_size("sx"), lax.axis_size("sy")
    at_x, at_y = lax.axis_index("sx"), lax.axis_index("sy")
    count = n_sx * n_sy

    has = jnp.stack([at_x > 0, at_x < n_sx - 1, at_y > 0, at_y < n_sy - 1])
    even = jnp.stack([at_x, at_y]) % 2 == 0
    flags = jnp.concatenate([jnp.where(has, 2.0, 1.0), jnp.where(even, 1.0, 0.0)]).astype(F32)
    select = (face_index[:, :, None] == jnp.arange(face, dtype=jnp.int32)).astype(BF16)
    coarse_ids = jnp.arange(ncoarse, dtype=jnp.int32)
    own_pick = (corners[None, :] == coarse_ids[:, None]).astype(BF16)
    corner_column = corners.astype(F32)[:, None]
    block = coarse_ids // (ncoarse // (n_sx * n_sy))
    origin = jnp.zeros_like(block)
    for at, (axis, bit) in enumerate(steps_of()):
        weight = bit * n_sy if axis == "sx" else bit
        origin = origin + ((block >> at) & 1) * weight
    origin = origin ^ (at_x * n_sy + at_y)
    within = coarse_ids % (ncoarse // (n_sx * n_sy))
    order = (origin * (ncoarse // (n_sx * n_sy)) + within)[None, :] == coarse_ids[:, None]
    order = order.astype(BF16)
    one_face = (face, width)
    parts = [pltpu.VMEM((half, width), BF16)] * 2
    one, select, own_pick, order, corner_column, flags = lax.optimization_barrier(
        (jnp.ones((1, width), F32), select, own_pick, order, corner_column, flags)
    )
    half_one = jnp.full((1, width), 0.5, F32)

    def early(matrix, owns, nears, coef, bases, lifts):
        operands = [flags, matrix, *owns, *nears, select, coef, *bases, *lifts]
        shapes = [one_face] * (4 if lifts else 2) + [(ni, width)]
        kernel = functools.partial(early_kernel, bool(bases), bool(lifts))
        *fields, partial = call(kernel, operands, shapes, parts, smem=1)
        return fields[:2], fields[2:], partial

    def crit(matrix, owns, nears, coef, partial, bases, lifts):
        operands = [flags, matrix, *owns, *nears, select, coef, partial, *bases, *lifts]
        shapes = [one_face] * (6 if lifts else 4)
        kernel = functools.partial(crit_kernel, bool(bases), bool(lifts))
        *fields, a2, a3 = call(kernel, operands, shapes, parts, smem=1, flops=CRIT_FLOPS)
        return fields[:2], fields[2:], (a2, a3)

    def fields_of(matrix, owns, nears, coef, bases=(), lifts=(), tied=None):
        v01, q01, partial = early(matrix, owns[:2], nears[:2], coef, bases[:2], lifts)
        coef = coef if tied is None else tied
        v23, q23, a23 = crit(matrix, owns[2:], nears[2:], coef, partial, bases[2:], lifts)
        return (*v01, *v23), (*q01, *q23), a23, partial

    def prec_late(values, a23, partial):
        operands = [flags, prec_mat, *values, *a23, partial]
        a0, a1, dots = call(prec_late_kernel, operands, [one_face, one_face, (1, width)], parts, smem=1)
        return (a0, a1, *a23), dots

    def flex_late(values, a23, partial, carried, other=()):
        operands = [flags, flex_mat, *values, *a23, *other, partial, coupling_mat, own_pick, carried]
        kernel = functools.partial(flex_late_kernel, int(bool(other)))
        a0, a1, sums = call(kernel, operands, [one_face, one_face, step_shape], parts, smem=1)
        return (a0, a1, *a23), sums

    def solved(kernel, sums, faces, others):
        total, *near = lax.optimization_barrier((summed(sums), *exchanged(faces)))
        (result,) = call(kernel, [total, matrix_all, order, *others], [step_shape])
        return near, total, result

    step_shape = (ncoarse + 8, width)
    extra = -(-face // width) * ncl
    sent = call(pack_kernel, [flags, load, coupling_mat, corner_column], [(face + extra, width)] * 4, smem=1)
    near = exchanged(sent)
    own_rows, _ = lax.optimization_barrier((coarse_inverse, sent[0]))
    matrix_all, one_later = lax.optimization_barrier((from_all(own_rows), one))

    residual0, _, a23, partial = fields_of(prec_mat, sent, near, one, tied=one_later)
    applied0, rho0 = prec_late(residual0, a23, partial)
    (lift,) = call(
        lift_kernel, [flags, *near, select, coupling_mat, corner_column], [(ni, ncoarse)], smem=1
    )
    lift, half_one = lax.optimization_barrier((lift, half_one))
    near = exchanged(applied0)

    direction0, _, a23, partial = fields_of(flex_mat, applied0, near, half_one)
    fine0, sums = flex_late(direction0, a23, partial, rho0)
    near, total0, result0 = solved(first_step_kernel, sums, fine0, [])
    lifts = (lift, result0[:ncoarse])
    residual1, image0, a23, partial = fields_of(prec_mat, fine0, near, result0[ncoarse:], residual0, lifts)
    applied1, rho1 = prec_late(residual1, a23, partial)
    near = exchanged(applied1)

    precond, _, a23, partial = fields_of(flex_mat, applied1, near, half_one)
    fine1, sums = flex_late(precond, a23, partial, rho1, fine0)
    near, _, result1 = solved(second_step_kernel, sums, fine1, [total0, result0])
    sol1, steps1 = result1[:ncoarse], result1[ncoarse:]

    def final(kernel, operands, smem=0):
        ends = [pltpu.VMEM((4, face, width), F32), pltpu.SemaphoreType.DMA((4,))]
        return call(kernel, operands, [(ni, width)], ends, smem=smem, out_spec=ANY_SPEC)[0]

    multipliers = final(weighted_kernel, [*direction0, *precond, steps1])
    operands = [flags, *fine1, *near, *residual1, *image0, select, lift, sol1, steps1]
    residual2 = final(tail_kernel, operands, smem=1)
    return multipliers[None, None], residual2[None, None]


def solution(mesh):
    return jax.shard_map(
        shards,
        mesh=mesh,
        in_specs=(
            P("sx", "sy", None, None),
            P("sx", "sy", None, None),
            P("sx", "sy", None, None),
            P("sx", "sy", None, None),
            P("sx", "sy", None),
            P("sx", "sy", None, None),
            P(("sx", "sy"), None),
        ),
        out_specs=(P("sx", "sy", None, None), P("sx", "sy", None, None)),
        check_vma=False,
    )
```

```python
import functools

import jax
import jax.numpy as jnp
from jax import lax
from jax.experimental import pallas as pl
from jax.experimental.pallas import tpu as pltpu
from jax.sharding import PartitionSpec as P

HIGHEST = lax.Precision.HIGHEST
F32 = jnp.float32
BF16 = jnp.bfloat16
LIMIT = 8 * 1024 * 1024
CRIT_FLOPS = 8 * 10**9


def swapped(block, axis, bit):
    return lax.ppermute(block, axis, [(i, i ^ bit) for i in range(lax.axis_size(axis))])


def swapped_between(block, axis):
    route = []
    for i in range(1, lax.axis_size(axis) - 1, 2):
        route += [(i, i + 1), (i + 1, i)]
    return lax.ppermute(block, axis, route)


def exchanged(slots):
    between_y = swapped_between(slots[3], "sy")
    within_y = swapped(slots[2], "sy", 1)
    between_x = swapped_between(slots[1], "sx")
    return swapped(slots[0], "sx", 1), between_x, within_y, between_y


def bits_of(axis):
    return [1 << i for i in range((lax.axis_size(axis) - 1).bit_length())]


def steps_of():
    return [("sx", bit) for bit in bits_of("sx")] + [("sy", bit) for bit in bits_of("sy")[1:]] + [("sy", 1)]


def stacked_rows(parts):
    count = parts[0].shape[0]
    total = count * len(parts)
    return sum(jnp.pad(p, ((at * count, total - (at + 1) * count), (0, 0))) for at, p in enumerate(parts))


def from_all(rows):
    for axis, bit in steps_of():
        rows = stacked_rows([rows, swapped(rows, axis, bit)])
    return rows


def block_of(other):
    return sum(1 << at for at, (axis, bit) in enumerate(steps_of()) if axis == "sy" and other & bit)


def split(x):
    high = x.astype(BF16)
    return high, (x - high.astype(F32)).astype(BF16)


def dot(a, b):
    return jnp.dot(a, b, preferred_element_type=F32)


def product(a, b_high, b_low):
    a_high, a_low = split(a)
    return dot(a_high, b_high) + (dot(a_high, b_low) + dot(a_low, b_high))


def thirds(x):
    high = x.astype(BF16)
    rest = x - high.astype(F32)
    mid = rest.astype(BF16)
    return high, mid, (rest - mid.astype(F32)).astype(BF16)


def permuted(select, rows):
    high, mid, low = thirds(rows)
    return dot(select, high) + (dot(select, mid) + dot(select, low))


def pair(flag, first, second):
    return jnp.where(flag == 1.0, second, first), jnp.where(flag == 1.0, first, second)


def faces_of(flags, slots):
    return (*pair(flags[4], slots[0], slots[1]), *pair(flags[5], slots[2], slots[3]))


def pack_kernel(corners, load, coupling, *refs):
    outs, sems = refs[:4], refs[4]
    face = load.shape[0] // 4
    width = load.shape[1]
    ncl = coupling.shape[0]
    even = [1 - lax.axis_index("sx") % 2, 1 - lax.axis_index("sy") % 2]
    faces = [even[0], 1 - even[0], 2 + even[1], 3 - even[1]]
    copies = []

    def copy(source, target):
        copies.append(pltpu.make_async_copy(source, target, sems.at[len(copies)]))
        copies[-1].start()

    for slot in (3, 2, 0, 1):
        first = pl.multiple_of(faces[slot] * face, 128)
        out = outs[slot]
        copy(load.at[pl.ds(first, face)], out.at[pl.ds(0, face)])
        for block, at in enumerate(range(0, face, width)):
            wide = min(width, face - at)
            source = coupling.at[:, pl.ds(pl.multiple_of(first + at, 128), wide)]
            copy(source, out.at[pl.ds(face + block * ncl, ncl), pl.ds(0, wide)])
    start = face + (face // width) * ncl
    for out in outs:
        for k in range(ncl):
            listed = jnp.full((1, width - face % width), corners[k].astype(F32))
            out[start + k : start + k + 1, face % width :] = listed
    for started in copies:
        started.wait()


def lift_kernel(flags, near0, near1, near2, near3, select, coupling, sent, out):
    face = out.shape[0] // 4
    ncoarse = out.shape[1]
    ncl = coupling.shape[0]
    ids = lax.broadcasted_iota(jnp.int32, (ncl, ncoarse), 1).astype(F32)
    own_pick = (sent[sent.shape[0] - ncl :, sent.shape[1] - 1 :] == ids).astype(F32)
    nears = faces_of(flags, [near[face:] for near in (near0, near1, near2, near3)])
    for f, near in enumerate(nears):
        columns = jnp.concatenate([near[at : at + ncl] for at in range(0, near.shape[0], ncl)], axis=1)
        near_pick = (columns[:, columns.shape[1] - 1 :] == ids).astype(F32)
        own = jnp.dot(coupling[:, f * face : (f + 1) * face].T, own_pick, precision=HIGHEST)
        theirs = jnp.dot(columns[:, :face].T, near_pick, precision=HIGHEST)
        out[f * face : (f + 1) * face] = own - permuted(select[f], theirs)


def field_into(at, owns, nears, select, flags, coef, bases, lifts, outs, images, high, low):
    size = outs[0].shape[0]
    if lifts:
        lift, sol = lifts
        corrections = product(lift[at * size : (at + 2) * size], *split(sol[...]))
    owns = pair(flags[4 + at // 2], *(own[:size] for own in owns))
    nears = pair(flags[4 + at // 2], *(near[:size] for near in nears))
    for f in range(2):
        image = owns[f] - permuted(select[at + f], nears[f])
        rows = slice(f * size, (f + 1) * size)
        if lifts:
            image = image + corrections[rows]
        if images:
            images[f][...] = image
        value = coef[0:1] * image
        if bases:
            value = bases[f][...] + value
        outs[f][...] = value
        high[rows], low[rows] = split(flags[at + f] * value)


def take(refs, *counts):
    groups = []
    for count in counts:
        groups.append(refs[:count])
        refs = refs[count:]
    return (*groups, refs)


def early_kernel(based, lifted, *refs):
    (flags, mat), owns, nears, (select, coef), bases, lifts, outs, images, rest = take(
        refs, 2, 2, 2, 2, 2 * based, 2 * lifted, 2, 2 * lifted
    )
    partial, high, low = rest
    field_into(0, owns, nears, select, flags, coef, bases, lifts, outs, images, high, low)
    half = high.shape[0]
    for rows in (slice(0, half), slice(half, 2 * half)):
        partial[rows] = product(mat[rows, :half], high[...], low[...])


def crit_kernel(based, lifted, *refs):
    (flags, mat), owns, nears, (select, coef, partial), bases, lifts, outs, images, rest = take(
        refs, 2, 2, 2, 3, 2 * based, 2 * lifted, 2, 2 * lifted
    )
    slot2, slot3, high, low = rest
    field_into(2, owns, nears, select, flags, coef, bases, lifts, outs, images, high, low)
    half = high.shape[0]
    size = half // 2
    value = partial[half:] + product(mat[half:, half:], high[...], low[...])
    slot3[...], slot2[...] = pair(flags[5], value[size:], value[:size])


def late_rows(flags, mat, values, partial, high, low, slots):
    size = values[0].shape[0]
    for f in (2, 3):
        rows = slice((f - 2) * size, (f - 1) * size)
        high[rows], low[rows] = split(flags[f] * values[f][...])
    value = partial[: 2 * size] + product(mat[: 2 * size, 2 * size :], high[...], low[...])
    slots[1][...], slots[0][...] = pair(flags[4], value[size:], value[:size])
    return faces_of(flags, [slot[...] for slot in slots])


def inner(flags, values, others):
    return sum(jnp.sum(flags[f] * values[f][...] * others[f], axis=0, keepdims=True) for f in range(4))


def prec_late_kernel(*refs):
    (flags, mat), values, applied, (partial, slot0, slot1, dots, high, low) = take(refs, 2, 4, 2)
    dots[...] = inner(flags, values, late_rows(flags, mat, values, partial, high, low, (slot0, slot1, *applied)))


def flex_late_kernel(others, *refs):
    (flags, mat), values, applied, other, rest = take(refs, 2, 4, 2, 4 * others)
    partial, coupling, carried, slot0, slot1, sums, high, low = rest
    size = slot0.shape[0]
    ncl = coupling.shape[0]
    coarse = None
    for f in range(4):
        term = product(coupling[:, f * size : (f + 1) * size], *split(flags[f] * values[f][...]))
        coarse = term if coarse is None else coarse + term
    faces = late_rows(flags, mat, values, partial, high, low, (slot0, slot1, *applied))
    rows = [inner(flags, values, faces), carried[...]]
    if others:
        rows.append(inner(flags, values, faces_of(flags, [slot[...] for slot in other])))
    sums[:ncl] = coarse
    for at, row in enumerate(rows):
        sums[ncl + at : ncl + at + 1] = row
    end = ncl + len(rows)
    sums[end:] = jnp.zeros((sums.shape[0] - end, sums.shape[1]), F32)


def spread_kernel(ncl, rows, origins, table, *refs):
    parts, out = refs[:-1], refs[-1]
    ncoarse = out.shape[0] - 8
    ids = lax.broadcasted_iota(jnp.int32, (ncoarse, ncl), 0).astype(F32)
    size = ncl + 8
    each = parts[0].shape[0] // size
    coarse, dots = None, None
    for at, origin in enumerate(origins):
        start = origin * rows + rows - 8
        pick = (ids == table[start : start + 1, :ncl]).astype(BF16)
        values = parts[at // each][at % each * size : (at % each + 1) * size]
        term = permuted(pick, values[:ncl])
        coarse = term if coarse is None else coarse + term
        dots = values[ncl:] if dots is None else dots + values[ncl:]
    out[:ncoarse] = coarse
    out[ncoarse:] = dots


def inverse_from(table, rows, matrix):
    own = rows - 8
    for at in range(table.shape[0] // rows):
        matrix[at * own : (at + 1) * own] = table[at * rows : at * rows + own]


def first_step_kernel(rows, total, table, order, out, matrix):
    ncoarse = matrix.shape[0]
    inverse_from(table, rows, matrix)
    rhs = total[:ncoarse]
    sol = permuted(order[...], jnp.dot(matrix[...], rhs, precision=HIGHEST))
    fine_dot = total[ncoarse : ncoarse + 1]
    rho = 0.5 * total[ncoarse + 1 : ncoarse + 2]
    curve = fine_dot + jnp.sum(rhs * sol, axis=0, keepdims=True)
    out[:ncoarse] = sol
    out[ncoarse : ncoarse + 1] = -rho / curve
    out[ncoarse + 1 : ncoarse + 2] = rho
    out[ncoarse + 2 : ncoarse + 3] = fine_dot
    out[ncoarse + 3 :] = jnp.zeros((out.shape[0] - ncoarse - 3, out.shape[1]), F32)


def second_step_kernel(rows, total, table, order, total0, out0, out, matrix):
    ncoarse = matrix.shape[0]
    inverse_from(table, rows, matrix)
    rhs = total[:ncoarse]
    sol = permuted(order[...], jnp.dot(matrix[...], rhs, precision=HIGHEST))
    dot11, rho1, dot10 = (total[ncoarse + row : ncoarse + row + 1] for row in range(3))
    minus_step0, rho0, dot00 = (out0[ncoarse + row : ncoarse + row + 1] for row in range(3))
    rho1 = 0.5 * rho1
    beta = rho1 / rho0
    coarse = jnp.sum((rhs + beta * total0[:ncoarse]) * (sol + beta * out0[:ncoarse]), axis=0, keepdims=True)
    step1 = rho1 / (dot11 + 2.0 * beta * dot10 + beta * beta * dot00 + coarse)
    out[:ncoarse] = sol
    out[ncoarse : ncoarse + 1] = -step1
    out[ncoarse + 1 : ncoarse + 2] = -step1 * beta
    out[ncoarse + 2 : ncoarse + 3] = step1 * beta - minus_step0
    out[ncoarse + 3 : ncoarse + 4] = step1
    out[ncoarse + 4 :] = jnp.zeros((out.shape[0] - ncoarse - 4, out.shape[1]), F32)


def stored(values, out, sems):
    size = values.shape[1]
    return [
        pltpu.make_async_copy(values.at[f], out.at[pl.ds(f * size, size)], sems.at[f]) for f in range(4)
    ]


def tail_kernel(*refs):
    (flags,), owns, nears, residuals, images, (select, lift, sol, steps, out, values, sems) = take(
        refs, 1, 4, 4, 4, 4
    )
    stores = stored(values, out, sems)
    parts = split(sol[...])
    size = values.shape[1]
    owns = faces_of(flags, [own[...] for own in owns])
    nears = faces_of(flags, [near[...] for near in nears])
    for f in range(4):
        image = owns[f] - permuted(select[f], nears[f]) + product(lift[f * size : (f + 1) * size], *parts)
        values[f] = residuals[f][...] + steps[0:1] * image + steps[1:2] * images[f][...]
        stores[f].start()
    for copy in stores:
        copy.wait()


def weighted_kernel(*refs):
    firsts, seconds, (steps, out, values, sems) = take(refs, 4, 4)
    stores = stored(values, out, sems)
    for f in range(4):
        values[f] = steps[2:3] * firsts[f][...] + steps[3:4] * seconds[f][...]
        stores[f].start()
    for copy in stores:
        copy.wait()


VMEM_SPEC = pl.BlockSpec(memory_space=pltpu.VMEM)
SMEM_SPEC = pl.BlockSpec(memory_space=pltpu.SMEM)
ANY_SPEC = pl.BlockSpec(memory_space=pl.ANY)


def call(kernel, operands, shapes, scratch=(), smem=0, anywhere=(), out_spec=VMEM_SPEC, flops=1024):
    return pl.pallas_call(
        kernel,
        in_specs=[SMEM_SPEC if i < smem else ANY_SPEC if i in anywhere else VMEM_SPEC for i in range(len(operands))],
        out_specs=[out_spec] * len(shapes),
        out_shape=[jax.ShapeDtypeStruct(s, F32) for s in shapes],
        scratch_shapes=list(scratch),
        compiler_params=pltpu.CompilerParams(vmem_limit_bytes=LIMIT),
        cost_estimate=pl.CostEstimate(flops=flops, bytes_accessed=1024, transcendentals=0),
    )(*operands)


def shards(loads, schur_flex, dirichlet, coupling, corner_index, face_lists, coarse_inverse):
    flex_mat = schur_flex[0, 0]
    prec_mat = dirichlet[0, 0]
    coupling_mat = coupling[0, 0]
    corners = corner_index[0, 0]
    face_index = face_lists[0, 0]
    load = loads[0, 0]
    ncoarse = coarse_inverse.shape[1]
    ncl, ni = coupling_mat.shape
    width = load.shape[1]
    face, half = ni // 4, ni // 2
    n_sx, n_sy = lax.axis_size("sx"), lax.axis_size("sy")
    at_x, at_y = lax.axis_index("sx"), lax.axis_index("sy")
    count = n_sx * n_sy

    has = jnp.stack([at_x > 0, at_x < n_sx - 1, at_y > 0, at_y < n_sy - 1])
    even = jnp.stack([at_x, at_y]) % 2 == 0
    flags = jnp.concatenate([jnp.where(has, 2.0, 1.0), jnp.where(even, 1.0, 0.0)]).astype(F32)
    select = (face_index[:, :, None] == jnp.arange(face, dtype=jnp.int32)).astype(BF16)
    coarse_ids = jnp.arange(ncoarse, dtype=jnp.int32)
    block = coarse_ids // (ncoarse // (n_sx * n_sy))
    origin = jnp.zeros_like(block)
    for at, (axis, bit) in enumerate(steps_of()):
        weight = bit * n_sy if axis == "sx" else bit
        origin = origin + ((block >> at) & 1) * weight
    origin = origin ^ (at_x * n_sy + at_y)
    within = coarse_ids % (ncoarse // (n_sx * n_sy))
    order = (origin * (ncoarse // (n_sx * n_sy)) + within)[None, :] == coarse_ids[:, None]
    order = order.astype(BF16)
    one_face = (face, width)
    parts = [pltpu.VMEM((half, width), BF16)] * 2
    one, select, order, flags = lax.optimization_barrier((jnp.ones((1, width), F32), select, order, flags))
    half_one = jnp.full((1, width), 0.5, F32)

    def early(matrix, owns, nears, coef, bases, lifts):
        operands = [flags, matrix, *owns, *nears, select, coef, *bases, *lifts]
        shapes = [one_face] * (4 if lifts else 2) + [(ni, width)]
        kernel = functools.partial(early_kernel, bool(bases), bool(lifts))
        *fields, partial = call(kernel, operands, shapes, parts, smem=1)
        return fields[:2], fields[2:], partial

    def crit(matrix, owns, nears, coef, partial, bases, lifts):
        operands = [flags, matrix, *owns, *nears, select, coef, partial, *bases, *lifts]
        shapes = [one_face] * (6 if lifts else 4)
        kernel = functools.partial(crit_kernel, bool(bases), bool(lifts))
        *fields, a2, a3 = call(kernel, operands, shapes, parts, smem=1, flops=CRIT_FLOPS)
        return fields[:2], fields[2:], (a2, a3)

    def fields_of(matrix, owns, nears, coef, bases=(), lifts=(), tied=None):
        v01, q01, partial = early(matrix, owns[:2], nears[:2], coef, bases[:2], lifts)
        coef = coef if tied is None else tied
        v23, q23, a23 = crit(matrix, owns[2:], nears[2:], coef, partial, bases[2:], lifts)
        return (*v01, *v23), (*q01, *q23), a23, partial

    def prec_late(values, a23, partial):
        operands = [flags, prec_mat, *values, *a23, partial]
        a0, a1, dots = call(prec_late_kernel, operands, [one_face, one_face, (1, width)], parts, smem=1)
        return (a0, a1, *a23), dots

    def flex_late(values, a23, partial, carried, other=()):
        operands = [flags, flex_mat, *values, *a23, *other, partial, coupling_mat, carried]
        kernel = functools.partial(flex_late_kernel, int(bool(other)))
        a0, a1, sums = call(kernel, operands, [one_face, one_face, (ncl + 8, width)], parts, smem=1)
        return (a0, a1, *a23), sums

    def solved(kernel, sums, faces, others):
        other, *faces = lax.optimization_barrier((swapped(sums, "sy", 1), *faces))
        near = exchanged(faces)
        parts = [sums, other]
        for bit in bits_of("sy")[1:]:
            rows = stacked_rows(parts)
            parts = [rows, swapped(rows, "sy", bit)]
        origins = [block_of(at) for at in range(n_sy)]
        spread = functools.partial(spread_kernel, ncl, table_rows, origins)
        (total,) = call(spread, [table, *parts], [step_shape])
        for bit in bits_of("sx"):
            total = total + swapped(total, "sx", bit)
        scratch = [pltpu.VMEM((ncoarse, ncoarse), F32)]
        kernel = functools.partial(kernel, table_rows)
        (result,) = call(kernel, [total, table, order, *others], [step_shape], scratch)
        return near, total, result

    step_shape = (ncoarse + 8, width)
    extra = -(-face // width) * ncl
    copies = 4 * (1 + -(-face // width))
    sent = call(
        pack_kernel,
        [corners, load, coupling_mat],
        [(face + extra, width)] * 4,
        [pltpu.SemaphoreType.DMA((copies,))],
        smem=1,
        anywhere=(1, 2),
    )
    near = exchanged(sent)

    own = coarse_inverse.shape[0]
    table_rows = own + 8
    listed = jnp.pad(corners.astype(F32)[None], ((own, 7), (0, ncoarse - ncl)))
    own_rows = jnp.pad(coarse_inverse, ((0, 8), (0, 0))) + listed
    own_rows, _ = lax.optimization_barrier((own_rows, sent[0]))
    table, one_later = lax.optimization_barrier((from_all(own_rows), one))

    residual0, _, a23, partial = fields_of(prec_mat, sent, near, one, tied=one_later)
    applied0, rho0 = prec_late(residual0, a23, partial)
    (lift,) = call(
        lift_kernel, [flags, *near, select, coupling_mat, sent[0]], [(ni, ncoarse)], smem=1
    )
    lift, half_one = lax.optimization_barrier((lift, half_one))
    near = exchanged(applied0)

    direction0, _, a23, partial = fields_of(flex_mat, applied0, near, half_one)
    fine0, sums = flex_late(direction0, a23, partial, rho0)
    near, total0, result0 = solved(first_step_kernel, sums, fine0, [])
    lifts = (lift, result0[:ncoarse])
    residual1, image0, a23, partial = fields_of(prec_mat, fine0, near, result0[ncoarse:], residual0, lifts)
    applied1, rho1 = prec_late(residual1, a23, partial)
    near = exchanged(applied1)

    precond, _, a23, partial = fields_of(flex_mat, applied1, near, half_one)
    fine1, sums = flex_late(precond, a23, partial, rho1, fine0)
    near, _, result1 = solved(second_step_kernel, sums, fine1, [total0, result0])
    sol1, steps1 = result1[:ncoarse], result1[ncoarse:]

    def final(kernel, operands, smem=0):
        ends = [pltpu.VMEM((4, face, width), F32), pltpu.SemaphoreType.DMA((4,))]
        return call(kernel, operands, [(ni, width)], ends, smem=smem, out_spec=ANY_SPEC)[0]

    multipliers = final(weighted_kernel, [*direction0, *precond, steps1])
    operands = [flags, *fine1, *near, *residual1, *image0, select, lift, sol1, steps1]
    residual2 = final(tail_kernel, operands, smem=1)
    return multipliers[None, None], residual2[None, None]


def solution(mesh):
    return jax.shard_map(
        shards,
        mesh=mesh,
        in_specs=(
            P("sx", "sy", None, None),
            P("sx", "sy", None, None),
            P("sx", "sy", None, None),
            P("sx", "sy", None, None),
            P("sx", "sy", None),
            P("sx", "sy", None, None),
            P(("sx", "sy"), None),
        ),
        out_specs=(P("sx", "sy", None, None), P("sx", "sy", None, None)),
        check_vma=False,
    )
```

```python
import functools

import jax
import jax.numpy as jnp
from jax import lax
from jax.experimental import pallas as pl
from jax.experimental.pallas import tpu as pltpu
from jax.sharding import PartitionSpec as P

HIGHEST = lax.Precision.HIGHEST
F32 = jnp.float32
BF16 = jnp.bfloat16
LIMIT = 8 * 1024 * 1024
CRIT_FLOPS = 8 * 10**9
FAR_ROWS = 8


def swapped(block, axis, bit):
    return lax.ppermute(block, axis, [(i, i ^ bit) for i in range(lax.axis_size(axis))])


def swapped_between(block, axis):
    route = []
    for i in range(1, lax.axis_size(axis) - 1, 2):
        route += [(i, i + 1), (i + 1, i)]
    return lax.ppermute(block, axis, route)


def exchanged(slots, axis):
    between = swapped_between(slots[1], axis)
    return swapped(slots[0], axis, 1), between


def bits_of(axis):
    return [1 << i for i in range((lax.axis_size(axis) - 1).bit_length())]


def steps_of():
    return [("sx", bit) for bit in bits_of("sx")] + [("sy", bit) for bit in bits_of("sy")[:0:-1]] + [("sy", 1)]


def stacked_rows(parts):
    count = parts[0].shape[0]
    total = count * len(parts)
    return sum(jnp.pad(p, ((at * count, total - (at + 1) * count), (0, 0))) for at, p in enumerate(parts))


def doubled(rows, steps):
    for axis, bit in steps:
        rows = stacked_rows([rows, swapped(rows, axis, bit)])
    return rows


def block_of(other):
    return sum(1 << at for at, (axis, bit) in enumerate(steps_of()) if axis == "sy" and other & bit)


def split(x):
    high = x.astype(BF16)
    return high, (x - high.astype(F32)).astype(BF16)


def dot(a, b):
    return jnp.dot(a, b, preferred_element_type=F32)


def product(a, b_high, b_low):
    a_high, a_low = split(a)
    return dot(a_high, b_high) + (dot(a_high, b_low) + dot(a_low, b_high))


def thirds(x):
    high = x.astype(BF16)
    rest = x - high.astype(F32)
    mid = rest.astype(BF16)
    return high, mid, (rest - mid.astype(F32)).astype(BF16)


def permuted(select, rows):
    high, mid, low = thirds(rows)
    return dot(select, high) + (dot(select, mid) + dot(select, low))


def pair(flag, first, second):
    return jnp.where(flag == 1.0, second, first), jnp.where(flag == 1.0, first, second)


def faces_of(flags, slots):
    return (*pair(flags[4], slots[0], slots[1]), *pair(flags[5], slots[2], slots[3]))


def pack_kernel(corners, load, coupling, *refs):
    outs, sems = refs[:4], refs[4]
    face = load.shape[0] // 4
    width = load.shape[1]
    ncl = coupling.shape[0]
    even = [1 - lax.axis_index("sx") % 2, 1 - lax.axis_index("sy") % 2]
    faces = [even[0], 1 - even[0], 2 + even[1], 3 - even[1]]
    copies = []

    def copy(source, target):
        copies.append(pltpu.make_async_copy(source, target, sems.at[len(copies)]))
        copies[-1].start()

    for slot in (3, 2, 0, 1):
        first = pl.multiple_of(faces[slot] * face, 128)
        out = outs[slot]
        copy(load.at[pl.ds(first, face)], out.at[pl.ds(0, face)])
        for block, at in enumerate(range(0, face, width)):
            wide = min(width, face - at)
            source = coupling.at[:, pl.ds(pl.multiple_of(first + at, 128), wide)]
            copy(source, out.at[pl.ds(face + block * ncl, ncl), pl.ds(0, wide)])
    start = face + (face // width) * ncl
    for out in outs:
        for k in range(ncl):
            listed = jnp.full((1, width - face % width), corners[k].astype(F32))
            out[start + k : start + k + 1, face % width :] = listed
    for started in copies:
        started.wait()


def lift_kernel(flags, near0, near1, near2, near3, select, coupling, sent, out):
    face = out.shape[0] // 4
    ncoarse = out.shape[1]
    ncl = coupling.shape[0]
    ids = lax.broadcasted_iota(jnp.int32, (ncl, ncoarse), 1).astype(F32)
    own_pick = (sent[sent.shape[0] - ncl :, sent.shape[1] - 1 :] == ids).astype(F32)
    nears = faces_of(flags, [near[face:] for near in (near0, near1, near2, near3)])
    for f, near in enumerate(nears):
        columns = jnp.concatenate([near[at : at + ncl] for at in range(0, near.shape[0], ncl)], axis=1)
        near_pick = (columns[:, columns.shape[1] - 1 :] == ids).astype(F32)
        own = jnp.dot(coupling[:, f * face : (f + 1) * face].T, own_pick, precision=HIGHEST)
        theirs = jnp.dot(columns[:, :face].T, near_pick, precision=HIGHEST)
        out[f * face : (f + 1) * face] = own - permuted(select[f], theirs)


def field_into(at, owns, nears, select, flags, coef, bases, lifts, outs, images, high, low):
    size = outs[0].shape[0]
    if lifts:
        lift, sol = lifts
        corrections = product(lift[at * size : (at + 2) * size], *split(sol[...]))
    owns = pair(flags[4 + at // 2], *(own[:size] for own in owns))
    nears = pair(flags[4 + at // 2], *(near[:size] for near in nears))
    for f in range(2):
        image = owns[f] - permuted(select[at + f], nears[f])
        rows = slice(f * size, (f + 1) * size)
        if lifts:
            image = image + corrections[rows]
        if images:
            images[f][...] = image
        value = coef[0:1] * image
        if bases:
            value = bases[f][...] + value
        outs[f][...] = value
        high[rows], low[rows] = split(flags[at + f] * value)


def take(refs, *counts):
    groups = []
    for count in counts:
        groups.append(refs[:count])
        refs = refs[count:]
    return (*groups, refs)


def early_kernel(based, lifted, *refs):
    (flags, mat), owns, nears, (select, coef), bases, lifts, outs, images, rest = take(
        refs, 2, 2, 2, 2, 2 * based, 2 * lifted, 2, 2 * lifted
    )
    partial, high, low = rest
    field_into(0, owns, nears, select, flags, coef, bases, lifts, outs, images, high, low)
    half = high.shape[0]
    for rows in (slice(0, half), slice(half, 2 * half)):
        partial[rows] = product(mat[rows, :half], high[...], low[...])


def crit_kernel(based, lifted, *refs):
    (flags, mat), owns, nears, (select, coef, partial), bases, lifts, outs, images, rest = take(
        refs, 2, 2, 2, 3, 2 * based, 2 * lifted, 2, 2 * lifted
    )
    slot2, slot3, high, low = rest
    field_into(2, owns, nears, select, flags, coef, bases, lifts, outs, images, high, low)
    half = high.shape[0]
    size = half // 2
    value = partial[half:] + product(mat[half:, half:], high[...], low[...])
    slot3[:size], slot2[:size] = pair(flags[5], value[size:], value[:size])
    for slot in (slot2, slot3):
        slot[size:] = jnp.zeros((slot.shape[0] - size, slot.shape[1]), F32)


def late_rows(flags, mat, values, partial, high, low, slots):
    size = values[0].shape[0]
    for f in (2, 3):
        rows = slice((f - 2) * size, (f - 1) * size)
        high[rows], low[rows] = split(flags[f] * values[f][...])
    value = partial[: 2 * size] + product(mat[: 2 * size, 2 * size :], high[...], low[...])
    slots[1][...], slots[0][...] = pair(flags[4], value[size:], value[:size])
    return faces_of(flags, [slot[:size] for slot in slots])


def inner(flags, values, others):
    return sum(jnp.sum(flags[f] * values[f][...] * others[f], axis=0, keepdims=True) for f in range(4))


def prec_late_kernel(*refs):
    (flags, mat), values, applied, (partial, slot0, slot1, dots, high, low) = take(refs, 2, 4, 2)
    dots[...] = inner(flags, values, late_rows(flags, mat, values, partial, high, low, (slot0, slot1, *applied)))


def flex_late_kernel(others, *refs):
    (flags, mat), values, applied, other, rest = take(refs, 2, 4, 2, 4 * others)
    partial, coupling, carried, slot0, slot1, sums, high, low = rest
    size = slot0.shape[0]
    ncl = coupling.shape[0]
    coarse = None
    for f in range(4):
        term = product(coupling[:, f * size : (f + 1) * size], *split(flags[f] * values[f][...]))
        coarse = term if coarse is None else coarse + term
    faces = late_rows(flags, mat, values, partial, high, low, (slot0, slot1, *applied))
    rows = [inner(flags, values, faces), carried[...]]
    if others:
        rows.append(inner(flags, values, faces_of(flags, [slot[:size] for slot in other])))
    sums[:ncl] = coarse
    for at, row in enumerate(rows):
        sums[ncl + at : ncl + at + 1] = row
    end = ncl + len(rows)
    sums[end:] = jnp.zeros((sums.shape[0] - end, sums.shape[1]), F32)


def spread_kernel(ncl, rows, origins, table, *refs):
    parts, out = refs[:-1], refs[-1]
    ncoarse = out.shape[0] - 8
    ids = lax.broadcasted_iota(jnp.int32, (ncoarse, ncl), 0).astype(F32)
    size = ncl + 8
    each = parts[0].shape[0] // size
    coarse, dots = None, None
    for at, origin in enumerate(origins):
        start = origin * rows + rows - 8
        pick = (ids == table[start : start + 1, :ncl]).astype(BF16)
        values = parts[at // each][at % each * size : (at % each + 1) * size]
        term = permuted(pick, values[:ncl])
        coarse = term if coarse is None else coarse + term
        dots = values[ncl:] if dots is None else dots + values[ncl:]
    out[:ncoarse] = coarse
    out[ncoarse:] = dots


def inverse_from(table, rows, matrix):
    own = rows - 8
    for at in range(table.shape[0] // rows):
        matrix[at * own : (at + 1) * own] = table[at * rows : at * rows + own]


def first_step_kernel(rows, total, table, order, out, matrix):
    ncoarse = matrix.shape[0]
    inverse_from(table, rows, matrix)
    rhs = total[:ncoarse]
    sol = permuted(order[...], jnp.dot(matrix[...], rhs, precision=HIGHEST))
    fine_dot = total[ncoarse : ncoarse + 1]
    rho = 0.5 * total[ncoarse + 1 : ncoarse + 2]
    curve = fine_dot + jnp.sum(rhs * sol, axis=0, keepdims=True)
    out[:ncoarse] = sol
    out[ncoarse : ncoarse + 1] = -rho / curve
    out[ncoarse + 1 : ncoarse + 2] = rho
    out[ncoarse + 2 : ncoarse + 3] = fine_dot
    out[ncoarse + 3 :] = jnp.zeros((out.shape[0] - ncoarse - 3, out.shape[1]), F32)


def second_step_kernel(rows, total, table, order, total0, out0, out, matrix):
    ncoarse = matrix.shape[0]
    inverse_from(table, rows, matrix)
    rhs = total[:ncoarse]
    sol = permuted(order[...], jnp.dot(matrix[...], rhs, precision=HIGHEST))
    dot11, rho1, dot10 = (total[ncoarse + row : ncoarse + row + 1] for row in range(3))
    minus_step0, rho0, dot00 = (out0[ncoarse + row : ncoarse + row + 1] for row in range(3))
    rho1 = 0.5 * rho1
    beta = rho1 / rho0
    coarse = jnp.sum((rhs + beta * total0[:ncoarse]) * (sol + beta * out0[:ncoarse]), axis=0, keepdims=True)
    step1 = rho1 / (dot11 + 2.0 * beta * dot10 + beta * beta * dot00 + coarse)
    out[:ncoarse] = sol
    out[ncoarse : ncoarse + 1] = -step1
    out[ncoarse + 1 : ncoarse + 2] = -step1 * beta
    out[ncoarse + 2 : ncoarse + 3] = step1 * beta - minus_step0
    out[ncoarse + 3 : ncoarse + 4] = step1
    out[ncoarse + 4 :] = jnp.zeros((out.shape[0] - ncoarse - 4, out.shape[1]), F32)


def stored(values, out, sems):
    size = values.shape[1]
    return [
        pltpu.make_async_copy(values.at[f], out.at[pl.ds(f * size, size)], sems.at[f]) for f in range(4)
    ]


def tail_kernel(*refs):
    (flags,), owns, nears, residuals, images, (select, lift, sol, steps, out, values, sems) = take(
        refs, 1, 4, 4, 4, 4
    )
    stores = stored(values, out, sems)
    parts = split(sol[...])
    size = values.shape[1]
    owns = faces_of(flags, [own[:size] for own in owns])
    nears = faces_of(flags, [near[:size] for near in nears])
    for f in range(4):
        image = owns[f] - permuted(select[f], nears[f]) + product(lift[f * size : (f + 1) * size], *parts)
        values[f] = residuals[f][...] + steps[0:1] * image + steps[1:2] * images[f][...]
        stores[f].start()
    for copy in stores:
        copy.wait()


def weighted_kernel(*refs):
    firsts, seconds, (steps, out, values, sems) = take(refs, 4, 4)
    stores = stored(values, out, sems)
    for f in range(4):
        values[f] = steps[2:3] * firsts[f][...] + steps[3:4] * seconds[f][...]
        stores[f].start()
    for copy in stores:
        copy.wait()


VMEM_SPEC = pl.BlockSpec(memory_space=pltpu.VMEM)
SMEM_SPEC = pl.BlockSpec(memory_space=pltpu.SMEM)
ANY_SPEC = pl.BlockSpec(memory_space=pl.ANY)


def call(kernel, operands, shapes, scratch=(), smem=0, anywhere=(), out_spec=VMEM_SPEC, flops=1024, limit=LIMIT):
    return pl.pallas_call(
        kernel,
        in_specs=[SMEM_SPEC if i < smem else ANY_SPEC if i in anywhere else VMEM_SPEC for i in range(len(operands))],
        out_specs=[out_spec] * len(shapes),
        out_shape=[jax.ShapeDtypeStruct(s, F32) for s in shapes],
        scratch_shapes=list(scratch),
        compiler_params=pltpu.CompilerParams(vmem_limit_bytes=limit),
        cost_estimate=pl.CostEstimate(flops=flops, bytes_accessed=1024, transcendentals=0),
    )(*operands)


def shards(loads, schur_flex, dirichlet, coupling, corner_index, face_lists, coarse_inverse):
    flex_mat = schur_flex[0, 0]
    prec_mat = dirichlet[0, 0]
    coupling_mat = coupling[0, 0]
    corners = corner_index[0, 0]
    face_index = face_lists[0, 0]
    load = loads[0, 0]
    ncoarse = coarse_inverse.shape[1]
    ncl, ni = coupling_mat.shape
    width = load.shape[1]
    face, half = ni // 4, ni // 2
    n_sx, n_sy = lax.axis_size("sx"), lax.axis_size("sy")
    at_x, at_y = lax.axis_index("sx"), lax.axis_index("sy")
    count = n_sx * n_sy

    has = jnp.stack([at_x > 0, at_x < n_sx - 1, at_y > 0, at_y < n_sy - 1])
    even = jnp.stack([at_x, at_y]) % 2 == 0
    flags = jnp.concatenate([jnp.where(has, 2.0, 1.0), jnp.where(even, 1.0, 0.0)]).astype(F32)
    select = (face_index[:, :, None] == jnp.arange(face, dtype=jnp.int32)).astype(BF16)
    coarse_ids = jnp.arange(ncoarse, dtype=jnp.int32)
    block = coarse_ids // (ncoarse // (n_sx * n_sy))
    origin = jnp.zeros_like(block)
    for at, (axis, bit) in enumerate(steps_of()):
        weight = bit * n_sy if axis == "sx" else bit
        origin = origin + ((block >> at) & 1) * weight
    origin = origin ^ (at_x * n_sy + at_y)
    within = coarse_ids % (ncoarse // (n_sx * n_sy))
    order = (origin * (ncoarse // (n_sx * n_sy)) + within)[None, :] == coarse_ids[:, None]
    order = order.astype(BF16)
    one_face, far_face = (face, width), (face + FAR_ROWS, width)
    parts = [pltpu.VMEM((half, width), BF16)] * 2
    one, select, order, flags = lax.optimization_barrier((jnp.ones((1, width), F32), select, order, flags))
    half_one = jnp.full((1, width), 0.5, F32)

    def early(matrix, owns, nears, coef, bases, lifts):
        operands = [flags, matrix, *owns, *nears, select, coef, *bases, *lifts]
        shapes = [one_face] * (4 if lifts else 2) + [(ni, width)]
        kernel = functools.partial(early_kernel, bool(bases), bool(lifts))
        *fields, partial = call(kernel, operands, shapes, parts, smem=1)
        return fields[:2], fields[2:], partial

    def crit(matrix, owns, nears, coef, partial, bases, lifts):
        operands = [flags, matrix, *owns, *nears, select, coef, partial, *bases, *lifts]
        shapes = [one_face] * (4 if lifts else 2) + [far_face] * 2
        kernel = functools.partial(crit_kernel, bool(bases), bool(lifts))
        *fields, a2, a3 = call(kernel, operands, shapes, parts, smem=1, flops=CRIT_FLOPS)
        return fields[:2], fields[2:], (a2, a3)

    def fields_of(matrix, owns, nears, coef, bases=(), lifts=(), beside=None):
        v01, q01, partial = early(matrix, owns[:2], nears[:2], coef, bases[:2], lifts)
        if beside is not None:
            partial, coef, made = beside(partial, coef)
        v23, q23, a23 = crit(matrix, owns[2:], nears[2:], coef, partial, bases[2:], lifts)
        fields = (*v01, *v23), (*q01, *q23), a23, partial
        return fields if beside is None else (*fields, made)

    def prec_late(values, a23, partial):
        operands = [flags, prec_mat, *values, *a23, partial]
        a0, a1, dots = call(prec_late_kernel, operands, [one_face, one_face, (1, width)], parts, smem=1)
        return (a0, a1, *a23), dots

    def flex_late(values, a23, partial, carried, other=()):
        operands = [flags, flex_mat, *values, *a23, *other, partial, coupling_mat, carried]
        kernel = functools.partial(flex_late_kernel, int(bool(other)))
        a0, a1, sums = call(kernel, operands, [one_face, one_face, (ncl + 8, width)], parts, smem=1)
        return (a0, a1, *a23), sums

    def solved(kernel, sums, faces, others):
        other, *far = lax.optimization_barrier((swapped(sums, "sy", 1), *faces[2:]))
        far = exchanged(far, "sy")
        close = faces[:2]
        parts, origins = [sums, other], [0, 1]
        for bit in bits_of("sy")[:0:-1]:
            rows = stacked_rows(parts)
            other, *close = lax.optimization_barrier((swapped(rows, "sy", bit), *close))
            parts = [rows, other]
            origins = origins + [at ^ bit for at in origins]
        origins = [block_of(at) for at in origins]
        spread = functools.partial(spread_kernel, ncl, table_rows, origins)
        (total,) = call(spread, [table, *parts], [step_shape])
        for bit in bits_of("sx"):
            total = total + swapped(total, "sx", bit)
        scratch = [pltpu.VMEM((ncoarse, ncoarse), F32)]
        kernel = functools.partial(kernel, table_rows)
        (result,) = call(kernel, [total, table, order, *others], [step_shape], scratch)
        return (*exchanged(close, "sx"), *far), total, result

    step_shape = (ncoarse + 8, width)
    extra = -(-face // width) * ncl
    copies = 4 * (1 + -(-face // width))
    sent = call(
        pack_kernel,
        [corners, load, coupling_mat],
        [(face + extra, width)] * 4,
        [pltpu.SemaphoreType.DMA((copies,))],
        smem=1,
        anywhere=(1, 2),
        limit=7 * LIMIT,
    )
    near = (*exchanged(sent[:2], "sx"), *exchanged(sent[2:], "sy"))

    own = coarse_inverse.shape[0]
    table_rows = own + 8
    listed = jnp.pad(corners.astype(F32)[None], ((own, 7), (0, ncoarse - ncl)))
    own_rows = jnp.pad(coarse_inverse, ((0, 8), (0, 0))) + listed
    own_rows, _ = lax.optimization_barrier((own_rows, sent[0]))
    most_rows = doubled(own_rows, steps_of()[:-1])

    def last_step(partial, coef):
        partial, rows = lax.optimization_barrier((partial, most_rows))
        table, coef = lax.optimization_barrier((doubled(rows, steps_of()[-1:]), coef))
        return partial, coef, table

    residual0, _, a23, partial, table = fields_of(prec_mat, sent, near, one, beside=last_step)
    applied0, rho0 = prec_late(residual0, a23, partial)
    (lift,) = call(
        lift_kernel, [flags, *near, select, coupling_mat, sent[0]], [(ni, ncoarse)], smem=1
    )
    lift, half_one = lax.optimization_barrier((lift, half_one))
    near = (*exchanged(applied0[:2], "sx"), *exchanged(applied0[2:], "sy"))

    direction0, _, a23, partial = fields_of(flex_mat, applied0, near, half_one)
    fine0, sums = flex_late(direction0, a23, partial, rho0)
    near, total0, result0 = solved(first_step_kernel, sums, fine0, [])
    lifts = (lift, result0[:ncoarse])
    residual1, image0, a23, partial = fields_of(prec_mat, fine0, near, result0[ncoarse:], residual0, lifts)
    applied1, rho1 = prec_late(residual1, a23, partial)
    near = (*exchanged(applied1[:2], "sx"), *exchanged(applied1[2:], "sy"))

    precond, _, a23, partial = fields_of(flex_mat, applied1, near, half_one)
    fine1, sums = flex_late(precond, a23, partial, rho1, fine0)
    near, _, result1 = solved(second_step_kernel, sums, fine1, [total0, result0])
    sol1, steps1 = result1[:ncoarse], result1[ncoarse:]

    def final(kernel, operands, smem=0):
        ends = [pltpu.VMEM((4, face, width), F32), pltpu.SemaphoreType.DMA((4,))]
        return call(kernel, operands, [(ni, width)], ends, smem=smem, out_spec=ANY_SPEC)[0]

    multipliers = final(weighted_kernel, [*direction0, *precond, steps1])
    operands = [flags, *fine1, *near, *residual1, *image0, select, lift, sol1, steps1]
    residual2 = final(tail_kernel, operands, smem=1)
    return multipliers[None, None], residual2[None, None]


def solution(mesh):
    return jax.shard_map(
        shards,
        mesh=mesh,
        in_specs=(
            P("sx", "sy", None, None),
            P("sx", "sy", None, None),
            P("sx", "sy", None, None),
            P("sx", "sy", None, None),
            P("sx", "sy", None),
            P("sx", "sy", None, None),
            P(("sx", "sy"), None),
        ),
        out_specs=(P("sx", "sy", None, None), P("sx", "sy", None, None)),
        check_vma=False,
    )
```

```python
import functools

import jax
import jax.numpy as jnp
from jax import lax
from jax.experimental import pallas as pl
from jax.experimental.pallas import tpu as pltpu
from jax.sharding import PartitionSpec as P

HIGHEST = lax.Precision.HIGHEST
F32 = jnp.float32
BF16 = jnp.bfloat16
LIMIT = 8 * 1024 * 1024
CRIT_FLOPS = 8 * 10**9
FAR_ROWS = 8


def swapped(block, axis, bit):
    return lax.ppermute(block, axis, [(i, i ^ bit) for i in range(lax.axis_size(axis))])


def swapped_between(block, axis):
    route = []
    for i in range(1, lax.axis_size(axis) - 1, 2):
        route += [(i, i + 1), (i + 1, i)]
    return lax.ppermute(block, axis, route)


def exchanged(slots, axis):
    between = swapped_between(slots[1], axis)
    return swapped(slots[0], axis, 1), between


def bits_of(axis):
    return [1 << i for i in range((lax.axis_size(axis) - 1).bit_length())]


def steps_of():
    return [("sy", 1)] + [("sx", bit) for bit in bits_of("sx")] + [("sy", bit) for bit in bits_of("sy")[:0:-1]]


def stacked_rows(parts):
    count = parts[0].shape[0]
    total = count * len(parts)
    return sum(jnp.pad(p, ((at * count, total - (at + 1) * count), (0, 0))) for at, p in enumerate(parts))


def doubled(rows, steps):
    for axis, bit in steps:
        rows = stacked_rows([rows, swapped(rows, axis, bit)])
    return rows


def block_of(other):
    return sum(1 << at for at, (axis, bit) in enumerate(steps_of()) if axis == "sy" and other & bit)


def split(x):
    high = x.astype(BF16)
    return high, (x - high.astype(F32)).astype(BF16)


def dot(a, b):
    return jnp.dot(a, b, preferred_element_type=F32)


def product(a, b_high, b_low):
    a_high, a_low = split(a)
    return dot(a_high, b_high) + (dot(a_high, b_low) + dot(a_low, b_high))


def thirds(x):
    high = x.astype(BF16)
    rest = x - high.astype(F32)
    mid = rest.astype(BF16)
    return high, mid, (rest - mid.astype(F32)).astype(BF16)


def permuted(select, rows):
    high, mid, low = thirds(rows)
    return dot(select, high) + (dot(select, mid) + dot(select, low))


def pair(flag, first, second):
    return jnp.where(flag == 1.0, second, first), jnp.where(flag == 1.0, first, second)


def faces_of(flags, slots):
    return (*pair(flags[4], slots[0], slots[1]), *pair(flags[5], slots[2], slots[3]))


def pack_kernel(corners, load, coupling, *refs):
    outs, (lists, sems) = refs[:4], refs[4:]
    face = load.shape[0] // 4
    width = load.shape[1]
    ncl = coupling.shape[0]
    even = [1 - lax.axis_index("sx") % 2, 1 - lax.axis_index("sy") % 2]
    faces = [even[0], 1 - even[0], 2 + even[1], 3 - even[1]]
    copies = []

    def copy(source, target):
        copies.append(pltpu.make_async_copy(source, target, sems.at[len(copies)]))
        copies[-1].start()

    for slot in (3, 2, 0, 1):
        first = pl.multiple_of(faces[slot] * face, 128)
        out = outs[slot]
        copy(load.at[pl.ds(first, face)], out.at[pl.ds(0, face)])
        for block, at in enumerate(range(0, face, width)):
            wide = min(width, face - at)
            source = coupling.at[:, pl.ds(pl.multiple_of(first + at, 128), wide)]
            copy(source, out.at[pl.ds(face + block * ncl, ncl), pl.ds(0, wide)])
    start = face + (face // width) * ncl
    for k in range(ncl):
        lists[k : k + 1] = jnp.full((1, lists.shape[1]), corners[k].astype(F32))
    for out in outs:
        copy(lists, out.at[pl.ds(start, ncl), pl.ds(face % width, lists.shape[1])])
    for started in copies:
        started.wait()


def lift_kernel(flags, near0, near1, near2, near3, select, coupling, sent, out):
    face = out.shape[0] // 4
    ncoarse = out.shape[1]
    ncl = coupling.shape[0]
    ids = lax.broadcasted_iota(jnp.int32, (ncl, ncoarse), 1).astype(F32)
    own_pick = (sent[sent.shape[0] - ncl :, sent.shape[1] - 1 :] == ids).astype(F32)
    nears = faces_of(flags, [near[face:] for near in (near0, near1, near2, near3)])
    for f, near in enumerate(nears):
        columns = jnp.concatenate([near[at : at + ncl] for at in range(0, near.shape[0], ncl)], axis=1)
        near_pick = (columns[:, columns.shape[1] - 1 :] == ids).astype(F32)
        own = jnp.dot(coupling[:, f * face : (f + 1) * face].T, own_pick, precision=HIGHEST)
        theirs = jnp.dot(columns[:, :face].T, near_pick, precision=HIGHEST)
        out[f * face : (f + 1) * face] = own - permuted(select[f], theirs)


def field_into(at, owns, nears, select, flags, coef, bases, lifts, outs, images, high, low):
    size = outs[0].shape[0]
    if lifts:
        lift, sol = lifts
        corrections = product(lift[at * size : (at + 2) * size], *split(sol[...]))
    owns = pair(flags[4 + at // 2], *(own[:size] for own in owns))
    nears = pair(flags[4 + at // 2], *(near[:size] for near in nears))
    for f in range(2):
        image = owns[f] - permuted(select[at + f], nears[f])
        rows = slice(f * size, (f + 1) * size)
        if lifts:
            image = image + corrections[rows]
        if images:
            images[f][...] = image
        value = coef[0:1] * image
        if bases:
            value = bases[f][...] + value
        outs[f][...] = value
        high[rows], low[rows] = split(flags[at + f] * value)


def take(refs, *counts):
    groups = []
    for count in counts:
        groups.append(refs[:count])
        refs = refs[count:]
    return (*groups, refs)


def early_kernel(based, lifted, *refs):
    (flags, mat), owns, nears, (select, coef), bases, lifts, outs, images, rest = take(
        refs, 2, 2, 2, 2, 2 * based, 2 * lifted, 2, 2 * lifted
    )
    partial, high, low = rest
    field_into(0, owns, nears, select, flags, coef, bases, lifts, outs, images, high, low)
    half = high.shape[0]
    for rows in (slice(0, half), slice(half, 2 * half)):
        partial[rows] = product(mat[rows, :half], high[...], low[...])


def crit_kernel(based, lifted, *refs):
    (flags, mat), owns, nears, (select, coef, partial), bases, lifts, outs, images, rest = take(
        refs, 2, 2, 2, 3, 2 * based, 2 * lifted, 2, 2 * lifted
    )
    slot2, slot3, high, low = rest
    field_into(2, owns, nears, select, flags, coef, bases, lifts, outs, images, high, low)
    half = high.shape[0]
    size = half // 2
    value = partial[half:] + product(mat[half:, half:], high[...], low[...])
    slot3[:size], slot2[:size] = pair(flags[5], value[size:], value[:size])
    for slot in (slot2, slot3):
        slot[size:] = jnp.zeros((slot.shape[0] - size, slot.shape[1]), F32)


def late_rows(flags, mat, values, partial, high, low, slots):
    size = values[0].shape[0]
    for f in (2, 3):
        rows = slice((f - 2) * size, (f - 1) * size)
        high[rows], low[rows] = split(flags[f] * values[f][...])
    value = partial[: 2 * size] + product(mat[: 2 * size, 2 * size :], high[...], low[...])
    slots[1][...], slots[0][...] = pair(flags[4], value[size:], value[:size])
    return faces_of(flags, [slot[:size] for slot in slots])


def inner(flags, values, others):
    return sum(jnp.sum(flags[f] * values[f][...] * others[f], axis=0, keepdims=True) for f in range(4))


def prec_late_kernel(*refs):
    (flags, mat), values, applied, (partial, slot0, slot1, dots, high, low) = take(refs, 2, 4, 2)
    dots[...] = inner(flags, values, late_rows(flags, mat, values, partial, high, low, (slot0, slot1, *applied)))


def flex_late_kernel(others, *refs):
    (flags, mat), values, applied, other, rest = take(refs, 2, 4, 2, 4 * others)
    partial, coupling, carried, slot0, slot1, sums, high, low = rest
    size = slot0.shape[0]
    ncl = coupling.shape[0]
    coarse = None
    for f in range(4):
        term = product(coupling[:, f * size : (f + 1) * size], *split(flags[f] * values[f][...]))
        coarse = term if coarse is None else coarse + term
    faces = late_rows(flags, mat, values, partial, high, low, (slot0, slot1, *applied))
    rows = [inner(flags, values, faces), carried[...]]
    if others:
        rows.append(inner(flags, values, faces_of(flags, [slot[:size] for slot in other])))
    sums[:ncl] = coarse
    for at, row in enumerate(rows):
        sums[ncl + at : ncl + at + 1] = row
    end = ncl + len(rows)
    sums[end:] = jnp.zeros((sums.shape[0] - end, sums.shape[1]), F32)


def spread_kernel(ncl, rows, origins, table, *refs):
    parts, out = refs[:-1], refs[-1]
    ncoarse = out.shape[0] - 8
    ids = lax.broadcasted_iota(jnp.int32, (ncoarse, ncl), 0).astype(F32)
    size = ncl + 8
    each = parts[0].shape[0] // size
    coarse, dots = None, None
    for at, origin in enumerate(origins):
        start = origin * rows + rows - 8
        pick = (ids == table[start : start + 1, :ncl]).astype(BF16)
        values = parts[at // each][at % each * size : (at % each + 1) * size]
        term = permuted(pick, values[:ncl])
        coarse = term if coarse is None else coarse + term
        dots = values[ncl:] if dots is None else dots + values[ncl:]
    out[:ncoarse] = coarse
    out[ncoarse:] = dots


def inverse_from(table, rows, matrix):
    own = rows - 8
    for at in range(table.shape[0] // rows):
        matrix[at * own : (at + 1) * own] = table[at * rows : at * rows + own]


def first_step_kernel(rows, total, table, order, out, matrix):
    ncoarse = matrix.shape[0]
    inverse_from(table, rows, matrix)
    rhs = total[:ncoarse]
    sol = permuted(order[...], jnp.dot(matrix[...], rhs, precision=HIGHEST))
    fine_dot = total[ncoarse : ncoarse + 1]
    rho = 0.5 * total[ncoarse + 1 : ncoarse + 2]
    curve = fine_dot + jnp.sum(rhs * sol, axis=0, keepdims=True)
    out[:ncoarse] = sol
    out[ncoarse : ncoarse + 1] = -rho / curve
    out[ncoarse + 1 : ncoarse + 2] = rho
    out[ncoarse + 2 : ncoarse + 3] = fine_dot
    out[ncoarse + 3 :] = jnp.zeros((out.shape[0] - ncoarse - 3, out.shape[1]), F32)


def second_step_kernel(rows, total, table, order, total0, out0, out, matrix):
    ncoarse = matrix.shape[0]
    inverse_from(table, rows, matrix)
    rhs = total[:ncoarse]
    sol = permuted(order[...], jnp.dot(matrix[...], rhs, precision=HIGHEST))
    dot11, rho1, dot10 = (total[ncoarse + row : ncoarse + row + 1] for row in range(3))
    minus_step0, rho0, dot00 = (out0[ncoarse + row : ncoarse + row + 1] for row in range(3))
    rho1 = 0.5 * rho1
    beta = rho1 / rho0
    coarse = jnp.sum((rhs + beta * total0[:ncoarse]) * (sol + beta * out0[:ncoarse]), axis=0, keepdims=True)
    step1 = rho1 / (dot11 + 2.0 * beta * dot10 + beta * beta * dot00 + coarse)
    out[:ncoarse] = sol
    out[ncoarse : ncoarse + 1] = -step1
    out[ncoarse + 1 : ncoarse + 2] = -step1 * beta
    out[ncoarse + 2 : ncoarse + 3] = step1 * beta - minus_step0
    out[ncoarse + 3 : ncoarse + 4] = step1
    out[ncoarse + 4 :] = jnp.zeros((out.shape[0] - ncoarse - 4, out.shape[1]), F32)


def stored(values, out, sems):
    size = values.shape[1]
    return [
        pltpu.make_async_copy(values.at[f], out.at[pl.ds(f * size, size)], sems.at[f]) for f in range(4)
    ]


def moved_kernel(*refs):
    (flags,), owns, nears, (select,), outs = take(refs, 1, 4, 4, 1)
    size = outs[0].shape[0]
    owns = faces_of(flags, [own[:size] for own in owns])
    nears = faces_of(flags, [near[:size] for near in nears])
    for f, out in enumerate(outs):
        out[...] = owns[f] - permuted(select[f], nears[f])


def tail_kernel(*refs):
    moved, residuals, images, (lift, sol, steps, out, values, sems) = take(refs, 4, 4, 4)
    stores = stored(values, out, sems)
    parts = split(sol[...])
    size = values.shape[1]
    for f in range(4):
        image = moved[f][...] + product(lift[f * size : (f + 1) * size], *parts)
        values[f] = residuals[f][...] + steps[0:1] * image + steps[1:2] * images[f][...]
        stores[f].start()
    for copy in stores:
        copy.wait()


def weighted_kernel(*refs):
    firsts, seconds, (steps, out, values, sems) = take(refs, 4, 4)
    stores = stored(values, out, sems)
    for f in range(4):
        values[f] = steps[2:3] * firsts[f][...] + steps[3:4] * seconds[f][...]
        stores[f].start()
    for copy in stores:
        copy.wait()


VMEM_SPEC = pl.BlockSpec(memory_space=pltpu.VMEM)
SMEM_SPEC = pl.BlockSpec(memory_space=pltpu.SMEM)
ANY_SPEC = pl.BlockSpec(memory_space=pl.ANY)


def call(kernel, operands, shapes, scratch=(), smem=0, anywhere=(), out_spec=VMEM_SPEC, flops=1024, limit=LIMIT):
    return pl.pallas_call(
        kernel,
        in_specs=[SMEM_SPEC if i < smem else ANY_SPEC if i in anywhere else VMEM_SPEC for i in range(len(operands))],
        out_specs=[out_spec] * len(shapes),
        out_shape=[jax.ShapeDtypeStruct(s, F32) for s in shapes],
        scratch_shapes=list(scratch),
        compiler_params=pltpu.CompilerParams(vmem_limit_bytes=limit),
        cost_estimate=pl.CostEstimate(flops=flops, bytes_accessed=1024, transcendentals=0),
    )(*operands)


def shards(loads, schur_flex, dirichlet, coupling, corner_index, face_lists, coarse_inverse):
    flex_mat = schur_flex[0, 0]
    prec_mat = dirichlet[0, 0]
    coupling_mat = coupling[0, 0]
    corners = corner_index[0, 0]
    face_index = face_lists[0, 0]
    load = loads[0, 0]
    ncoarse = coarse_inverse.shape[1]
    ncl, ni = coupling_mat.shape
    width = load.shape[1]
    face, half = ni // 4, ni // 2
    n_sx, n_sy = lax.axis_size("sx"), lax.axis_size("sy")
    at_x, at_y = lax.axis_index("sx"), lax.axis_index("sy")
    count = n_sx * n_sy

    has = jnp.stack([at_x > 0, at_x < n_sx - 1, at_y > 0, at_y < n_sy - 1])
    even = jnp.stack([at_x, at_y]) % 2 == 0
    flags = jnp.concatenate([jnp.where(has, 2.0, 1.0), jnp.where(even, 1.0, 0.0)]).astype(F32)
    select = (face_index[:, :, None] == jnp.arange(face, dtype=jnp.int32)).astype(BF16)
    coarse_ids = jnp.arange(ncoarse, dtype=jnp.int32)
    block = coarse_ids // (ncoarse // (n_sx * n_sy))
    origin = jnp.zeros_like(block)
    for at, (axis, bit) in enumerate(steps_of()):
        weight = bit * n_sy if axis == "sx" else bit
        origin = origin + ((block >> at) & 1) * weight
    origin = origin ^ (at_x * n_sy + at_y)
    within = coarse_ids % (ncoarse // (n_sx * n_sy))
    order = (origin * (ncoarse // (n_sx * n_sy)) + within)[None, :] == coarse_ids[:, None]
    order = order.astype(BF16)
    one_face, far_face = (face, width), (face + FAR_ROWS, width)
    parts = [pltpu.VMEM((half, width), BF16)] * 2
    one, select, order, flags = lax.optimization_barrier((jnp.ones((1, width), F32), select, order, flags))
    half_one = jnp.full((1, width), 0.5, F32)

    def early(matrix, owns, nears, coef, bases, lifts):
        operands = [flags, matrix, *owns, *nears, select, coef, *bases, *lifts]
        shapes = [one_face] * (4 if lifts else 2) + [(ni, width)]
        kernel = functools.partial(early_kernel, bool(bases), bool(lifts))
        *fields, partial = call(kernel, operands, shapes, parts, smem=1)
        return fields[:2], fields[2:], partial

    def crit(matrix, owns, nears, coef, partial, bases, lifts):
        operands = [flags, matrix, *owns, *nears, select, coef, partial, *bases, *lifts]
        shapes = [one_face] * (4 if lifts else 2) + [far_face] * 2
        kernel = functools.partial(crit_kernel, bool(bases), bool(lifts))
        *fields, a2, a3 = call(kernel, operands, shapes, parts, smem=1, flops=CRIT_FLOPS)
        return fields[:2], fields[2:], (a2, a3)

    def fields_of(matrix, owns, nears, coef, bases=(), lifts=(), beside=None):
        v01, q01, partial = early(matrix, owns[:2], nears[:2], coef, bases[:2], lifts)
        if beside is not None:
            partial, coef, made = beside(partial, coef)
        v23, q23, a23 = crit(matrix, owns[2:], nears[2:], coef, partial, bases[2:], lifts)
        fields = (*v01, *v23), (*q01, *q23), a23, partial
        return fields if beside is None else (*fields, made)

    def prec_late(values, a23, partial):
        operands = [flags, prec_mat, *values, *a23, partial]
        a0, a1, dots = call(prec_late_kernel, operands, [one_face, one_face, (1, width)], parts, smem=1)
        return (a0, a1, *a23), dots

    def flex_late(values, a23, partial, carried, other=()):
        operands = [flags, flex_mat, *values, *a23, *other, partial, coupling_mat, carried]
        kernel = functools.partial(flex_late_kernel, int(bool(other)))
        a0, a1, sums = call(kernel, operands, [one_face, one_face, (ncl + 8, width)], parts, smem=1)
        return (a0, a1, *a23), sums

    def solved(kernel, sums, faces, more, before=None):
        both = stacked_rows([sums, swapped(sums, "sy", 1)])
        others = [swapped(both, "sy", at) for at in range(2, n_sy, 2)]
        others, faces = lax.optimization_barrier((others, faces))
        near = (*exchanged(faces[:2], "sx"), *exchanged(faces[2:], "sy"))
        parts = [both, *others]
        origins = [block_of(at) for at in range(n_sy)]
        spread = functools.partial(spread_kernel, ncl, table_rows, origins)
        (total,) = call(spread, [table, *parts], [step_shape])
        for bit in bits_of("sx"):
            total = total + swapped(total, "sx", bit)
        scratch = [pltpu.VMEM((ncoarse, ncoarse), F32)]
        kernel = functools.partial(kernel, table_rows)
        if before is not None:
            total, near = before(total, near)
        (result,) = call(kernel, [total, table, order, *more], [step_shape], scratch)
        return near, total, result

    step_shape = (ncoarse + 8, width)
    extra = -(-face // width) * ncl
    copies = 4 * (2 + -(-face // width))
    sent = call(
        pack_kernel,
        [corners, load, coupling_mat],
        [(face + extra, width)] * 4,
        [pltpu.VMEM((ncl, width - face % width), F32), pltpu.SemaphoreType.DMA((copies,))],
        smem=1,
        anywhere=(1, 2),
        out_spec=ANY_SPEC,
        limit=7 * LIMIT,
    )
    near = (*exchanged(sent[:2], "sx"), *exchanged(sent[2:], "sy"))

    own = coarse_inverse.shape[0]
    table_rows = own + 8
    listed = jnp.pad(corners.astype(F32)[None], ((own, 7), (0, ncoarse - ncl)))
    own_rows = jnp.pad(coarse_inverse, ((0, 8), (0, 0))) + listed
    own_rows, _ = lax.optimization_barrier((own_rows, sent[0]))

    def most_steps(partial, coef):
        rows, coef = lax.optimization_barrier((doubled(own_rows, steps_of()[:-1]), coef))
        return partial, coef, rows

    residual0, _, a23, partial, most_rows = fields_of(prec_mat, sent, near, one, beside=most_steps)
    applied0, rho0 = prec_late(residual0, a23, partial)
    (lift,) = call(
        lift_kernel, [flags, *near, select, coupling_mat, sent[0]], [(ni, ncoarse)], smem=1
    )
    table, half_one = lax.optimization_barrier((doubled(most_rows, steps_of()[-1:]), half_one))
    near = (*exchanged(applied0[:2], "sx"), *exchanged(applied0[2:], "sy"))

    direction0, _, a23, partial = fields_of(flex_mat, applied0, near, half_one)
    fine0, sums = flex_late(direction0, a23, partial, rho0)
    near, total0, result0 = solved(first_step_kernel, sums, fine0, [])
    lifts = (lift, result0[:ncoarse])
    residual1, image0, a23, partial = fields_of(prec_mat, fine0, near, result0[ncoarse:], residual0, lifts)
    applied1, rho1 = prec_late(residual1, a23, partial)
    near = (*exchanged(applied1[:2], "sx"), *exchanged(applied1[2:], "sy"))

    precond, _, a23, partial = fields_of(flex_mat, applied1, near, half_one)
    fine1, sums = flex_late(precond, a23, partial, rho1, fine0)

    def jump_first(total, near):
        moved = call(moved_kernel, [flags, *fine1, *near, select], [one_face] * 4, smem=1)
        return lax.optimization_barrier((total, moved))

    moved, _, result1 = solved(second_step_kernel, sums, fine1, [total0, result0], jump_first)
    sol1, steps1 = result1[:ncoarse], result1[ncoarse:]

    def final(kernel, operands):
        ends = [pltpu.VMEM((4, face, width), F32), pltpu.SemaphoreType.DMA((4,))]
        return call(kernel, operands, [(ni, width)], ends, out_spec=ANY_SPEC)[0]

    multipliers = final(weighted_kernel, [*direction0, *precond, steps1])
    residual2 = final(tail_kernel, [*moved, *residual1, *image0, lift, sol1, steps1])
    return multipliers[None, None], residual2[None, None]


def solution(mesh):
    return jax.shard_map(
        shards,
        mesh=mesh,
        in_specs=(
            P("sx", "sy", None, None),
            P("sx", "sy", None, None),
            P("sx", "sy", None, None),
            P("sx", "sy", None, None),
            P("sx", "sy", None),
            P("sx", "sy", None, None),
            P(("sx", "sy"), None),
        ),
        out_specs=(P("sx", "sy", None, None), P("sx", "sy", None, None)),
        check_vma=False,
    )
```

```python
import functools

import jax
import jax.numpy as jnp
from jax import lax
from jax.experimental import pallas as pl
from jax.experimental.pallas import tpu as pltpu
from jax.sharding import PartitionSpec as P

HIGHEST = lax.Precision.HIGHEST
F32 = jnp.float32
BF16 = jnp.bfloat16
LIMIT = 8 * 1024 * 1024
CRIT_FLOPS = 8 * 10**9
FAR_ROWS = 8


def swapped(block, axis, bit):
    return lax.ppermute(block, axis, [(i, i ^ bit) for i in range(lax.axis_size(axis))])


def swapped_between(block, axis):
    route = []
    for i in range(1, lax.axis_size(axis) - 1, 2):
        route += [(i, i + 1), (i + 1, i)]
    return lax.ppermute(block, axis, route)


def exchanged(slots, axis):
    between = swapped_between(slots[1], axis)
    return swapped(slots[0], axis, 1), between


def bits_of(axis):
    return [1 << i for i in range((lax.axis_size(axis) - 1).bit_length())]


def steps_of():
    return [("sy", 1)] + [("sx", bit) for bit in bits_of("sx")] + [("sy", bit) for bit in bits_of("sy")[:0:-1]]


def stacked_rows(parts):
    count = parts[0].shape[0]
    total = count * len(parts)
    return sum(jnp.pad(p, ((at * count, total - (at + 1) * count), (0, 0))) for at, p in enumerate(parts))


def doubled(rows, steps):
    for axis, bit in steps:
        rows = stacked_rows([rows, swapped(rows, axis, bit)])
    return rows


def block_of(other):
    return sum(1 << at for at, (axis, bit) in enumerate(steps_of()) if axis == "sy" and other & bit)


def split(x):
    high = x.astype(BF16)
    return high, (x - high.astype(F32)).astype(BF16)


def dot(a, b):
    return jnp.dot(a, b, preferred_element_type=F32)


def product(a, b_high, b_low):
    a_high, a_low = split(a)
    return dot(a_high, b_high) + (dot(a_high, b_low) + dot(a_low, b_high))


def thirds(x):
    high = x.astype(BF16)
    rest = x - high.astype(F32)
    mid = rest.astype(BF16)
    return high, mid, (rest - mid.astype(F32)).astype(BF16)


def permuted(select, rows):
    high, mid, low = thirds(rows)
    return dot(select, high) + (dot(select, mid) + dot(select, low))


def pair(flag, first, second):
    return jnp.where(flag == 1.0, second, first), jnp.where(flag == 1.0, first, second)


def faces_of(flags, slots):
    return (*pair(flags[4], slots[0], slots[1]), *pair(flags[5], slots[2], slots[3]))


def pack_kernel(corners, load, coupling, *refs):
    outs, sems = refs[:4], refs[4]
    face = load.shape[0] // 4
    width = load.shape[1]
    ncl = coupling.shape[0]
    even = [1 - lax.axis_index("sx") % 2, 1 - lax.axis_index("sy") % 2]
    faces = [even[0], 1 - even[0], 2 + even[1], 3 - even[1]]
    copies = []

    def copy(source, target):
        copies.append(pltpu.make_async_copy(source, target, sems.at[len(copies)]))
        copies[-1].start()

    for slot in (3, 2, 0, 1):
        first = pl.multiple_of(faces[slot] * face, 128)
        out = outs[slot]
        copy(load.at[pl.ds(first, face)], out.at[pl.ds(0, face)])
        for block, at in enumerate(range(0, face, width)):
            wide = min(width, face - at)
            source = coupling.at[:, pl.ds(pl.multiple_of(first + at, 128), wide)]
            copy(source, out.at[pl.ds(face + block * ncl, ncl), pl.ds(0, wide)])
    start = face + (face // width) * ncl
    for out in outs:
        for k in range(ncl):
            listed = jnp.full((1, width - face % width), corners[k].astype(F32))
            out[start + k : start + k + 1, face % width :] = listed
    for started in copies:
        started.wait()


def rows_kernel(corners, inverse, out):
    own = inverse.shape[0]
    out[:own] = inverse[...]
    out[own:] = jnp.zeros((out.shape[0] - own, out.shape[1]), F32)
    columns = lax.broadcasted_iota(jnp.int32, (1, out.shape[1]), 1)
    listed = jnp.zeros((1, out.shape[1]), F32)
    for k in range(corners.shape[0]):
        listed = jnp.where(columns == k, corners[k].astype(F32), listed)
    out[own : own + 1] = listed


def lift_kernel(flags, near0, near1, near2, near3, select, coupling, sent, out):
    face = out.shape[0] // 4
    ncoarse = out.shape[1]
    ncl = coupling.shape[0]
    ids = lax.broadcasted_iota(jnp.int32, (ncl, ncoarse), 1).astype(F32)
    own_pick = (sent[sent.shape[0] - ncl :, sent.shape[1] - 1 :] == ids).astype(F32)
    nears = faces_of(flags, [near[face:] for near in (near0, near1, near2, near3)])
    for f, near in enumerate(nears):
        columns = jnp.concatenate([near[at : at + ncl] for at in range(0, near.shape[0], ncl)], axis=1)
        near_pick = (columns[:, columns.shape[1] - 1 :] == ids).astype(F32)
        own = jnp.dot(coupling[:, f * face : (f + 1) * face].T, own_pick, precision=HIGHEST)
        theirs = jnp.dot(columns[:, :face].T, near_pick, precision=HIGHEST)
        out[f * face : (f + 1) * face] = own - permuted(select[f], theirs)


def field_into(at, owns, nears, select, flags, coef, bases, lifts, outs, images, high, low):
    size = outs[0].shape[0]
    if lifts:
        lift, sol = lifts
        corrections = product(lift[at * size : (at + 2) * size], *split(sol[...]))
    owns = pair(flags[4 + at // 2], *(own[:size] for own in owns))
    nears = pair(flags[4 + at // 2], *(near[:size] for near in nears))
    for f in range(2):
        image = owns[f] - permuted(select[at + f], nears[f])
        rows = slice(f * size, (f + 1) * size)
        if lifts:
            image = image + corrections[rows]
        if images:
            images[f][...] = image
        value = coef[0:1] * image
        if bases:
            value = bases[f][...] + value
        outs[f][...] = value
        high[rows], low[rows] = split(flags[at + f] * value)


def take(refs, *counts):
    groups = []
    for count in counts:
        groups.append(refs[:count])
        refs = refs[count:]
    return (*groups, refs)


def early_kernel(based, lifted, *refs):
    (flags, mat), owns, nears, (select, coef), bases, lifts, outs, images, rest = take(
        refs, 2, 2, 2, 2, 2 * based, 2 * lifted, 2, 2 * lifted
    )
    partial, high, low = rest
    field_into(0, owns, nears, select, flags, coef, bases, lifts, outs, images, high, low)
    half = high.shape[0]
    for rows in (slice(0, half), slice(half, 2 * half)):
        partial[rows] = product(mat[rows, :half], high[...], low[...])


def crit_kernel(based, lifted, *refs):
    (flags, mat), owns, nears, (select, coef, partial), bases, lifts, outs, images, rest = take(
        refs, 2, 2, 2, 3, 2 * based, 2 * lifted, 2, 2 * lifted
    )
    slot2, slot3, high, low = rest
    field_into(2, owns, nears, select, flags, coef, bases, lifts, outs, images, high, low)
    half = high.shape[0]
    size = half // 2
    value = partial[half:] + product(mat[half:, half:], high[...], low[...])
    slot3[:size], slot2[:size] = pair(flags[5], value[size:], value[:size])
    for slot in (slot2, slot3):
        slot[size:] = jnp.zeros((slot.shape[0] - size, slot.shape[1]), F32)


def late_rows(flags, mat, values, partial, high, low, slots):
    size = values[0].shape[0]
    for f in (2, 3):
        rows = slice((f - 2) * size, (f - 1) * size)
        high[rows], low[rows] = split(flags[f] * values[f][...])
    value = partial[: 2 * size] + product(mat[: 2 * size, 2 * size :], high[...], low[...])
    slots[1][...], slots[0][...] = pair(flags[4], value[size:], value[:size])
    return faces_of(flags, [slot[:size] for slot in slots])


def inner(flags, values, others):
    return sum(jnp.sum(flags[f] * values[f][...] * others[f], axis=0, keepdims=True) for f in range(4))


def prec_late_kernel(*refs):
    (flags, mat), values, applied, (partial, slot0, slot1, dots, high, low) = take(refs, 2, 4, 2)
    dots[...] = inner(flags, values, late_rows(flags, mat, values, partial, high, low, (slot0, slot1, *applied)))


def flex_late_kernel(others, *refs):
    (flags, mat), values, applied, other, rest = take(refs, 2, 4, 2, 4 * others)
    partial, coupling, carried, slot0, slot1, sums, high, low = rest
    size = slot0.shape[0]
    ncl = coupling.shape[0]
    coarse = None
    for f in range(4):
        term = product(coupling[:, f * size : (f + 1) * size], *split(flags[f] * values[f][...]))
        coarse = term if coarse is None else coarse + term
    faces = late_rows(flags, mat, values, partial, high, low, (slot0, slot1, *applied))
    rows = [inner(flags, values, faces), carried[...]]
    if others:
        rows.append(inner(flags, values, faces_of(flags, [slot[:size] for slot in other])))
    sums[:ncl] = coarse
    for at, row in enumerate(rows):
        sums[ncl + at : ncl + at + 1] = row
    end = ncl + len(rows)
    sums[end:] = jnp.zeros((sums.shape[0] - end, sums.shape[1]), F32)


def spread_kernel(ncl, rows, origins, table, *refs):
    parts, out = refs[:-1], refs[-1]
    ncoarse = out.shape[0] - 8
    ids = lax.broadcasted_iota(jnp.int32, (ncoarse, ncl), 0).astype(F32)
    size = ncl + 8
    each = parts[0].shape[0] // size
    coarse, dots = None, None
    for at, origin in enumerate(origins):
        start = origin * rows + rows - 8
        pick = (ids == table[start : start + 1, :ncl]).astype(BF16)
        values = parts[at // each][at % each * size : (at % each + 1) * size]
        term = permuted(pick, values[:ncl])
        coarse = term if coarse is None else coarse + term
        dots = values[ncl:] if dots is None else dots + values[ncl:]
    out[:ncoarse] = coarse
    out[ncoarse:] = dots


def inverse_from(table, rows, matrix):
    own = rows - 8
    for at in range(table.shape[0] // rows):
        matrix[at * own : (at + 1) * own] = table[at * rows : at * rows + own]


def first_step_kernel(rows, total, table, order, out, matrix):
    ncoarse = matrix.shape[0]
    inverse_from(table, rows, matrix)
    rhs = total[:ncoarse]
    sol = permuted(order[...], jnp.dot(matrix[...], rhs, precision=HIGHEST))
    fine_dot = total[ncoarse : ncoarse + 1]
    rho = 0.5 * total[ncoarse + 1 : ncoarse + 2]
    curve = fine_dot + jnp.sum(rhs * sol, axis=0, keepdims=True)
    out[:ncoarse] = sol
    out[ncoarse : ncoarse + 1] = -rho / curve
    out[ncoarse + 1 : ncoarse + 2] = rho
    out[ncoarse + 2 : ncoarse + 3] = fine_dot
    out[ncoarse + 3 :] = jnp.zeros((out.shape[0] - ncoarse - 3, out.shape[1]), F32)


def second_step_kernel(rows, total, table, order, total0, out0, out, matrix):
    ncoarse = matrix.shape[0]
    inverse_from(table, rows, matrix)
    rhs = total[:ncoarse]
    sol = permuted(order[...], jnp.dot(matrix[...], rhs, precision=HIGHEST))
    dot11, rho1, dot10 = (total[ncoarse + row : ncoarse + row + 1] for row in range(3))
    minus_step0, rho0, dot00 = (out0[ncoarse + row : ncoarse + row + 1] for row in range(3))
    rho1 = 0.5 * rho1
    beta = rho1 / rho0
    coarse = jnp.sum((rhs + beta * total0[:ncoarse]) * (sol + beta * out0[:ncoarse]), axis=0, keepdims=True)
    step1 = rho1 / (dot11 + 2.0 * beta * dot10 + beta * beta * dot00 + coarse)
    out[:ncoarse] = sol
    out[ncoarse : ncoarse + 1] = -step1
    out[ncoarse + 1 : ncoarse + 2] = -step1 * beta
    out[ncoarse + 2 : ncoarse + 3] = step1 * beta - minus_step0
    out[ncoarse + 3 : ncoarse + 4] = step1
    out[ncoarse + 4 :] = jnp.zeros((out.shape[0] - ncoarse - 4, out.shape[1]), F32)


def stored(values, out, sems):
    size = values.shape[1]
    return [
        pltpu.make_async_copy(values.at[f], out.at[pl.ds(f * size, size)], sems.at[f]) for f in range(4)
    ]


def moved_kernel(*refs):
    (flags,), owns, nears, (select,), outs = take(refs, 1, 4, 4, 1)
    size = outs[0].shape[0]
    owns = faces_of(flags, [own[:size] for own in owns])
    nears = faces_of(flags, [near[:size] for near in nears])
    for f, out in enumerate(outs):
        out[...] = owns[f] - permuted(select[f], nears[f])


def tail_kernel(*refs):
    moved, residuals, images, (lift, sol, steps, out, values, sems) = take(refs, 4, 4, 4)
    stores = stored(values, out, sems)
    parts = split(sol[...])
    size = values.shape[1]
    for f in range(4):
        image = moved[f][...] + product(lift[f * size : (f + 1) * size], *parts)
        values[f] = residuals[f][...] + steps[0:1] * image + steps[1:2] * images[f][...]
        stores[f].start()
    for copy in stores:
        copy.wait()


def weighted_kernel(*refs):
    firsts, seconds, (steps, out, values, sems) = take(refs, 4, 4)
    stores = stored(values, out, sems)
    for f in range(4):
        values[f] = steps[2:3] * firsts[f][...] + steps[3:4] * seconds[f][...]
        stores[f].start()
    for copy in stores:
        copy.wait()


VMEM_SPEC = pl.BlockSpec(memory_space=pltpu.VMEM)
SMEM_SPEC = pl.BlockSpec(memory_space=pltpu.SMEM)
ANY_SPEC = pl.BlockSpec(memory_space=pl.ANY)


def call(kernel, operands, shapes, scratch=(), smem=0, anywhere=(), out_spec=VMEM_SPEC, flops=1024, limit=LIMIT):
    return pl.pallas_call(
        kernel,
        in_specs=[SMEM_SPEC if i < smem else ANY_SPEC if i in anywhere else VMEM_SPEC for i in range(len(operands))],
        out_specs=[out_spec] * len(shapes),
        out_shape=[jax.ShapeDtypeStruct(s, F32) for s in shapes],
        scratch_shapes=list(scratch),
        compiler_params=pltpu.CompilerParams(vmem_limit_bytes=limit),
        cost_estimate=pl.CostEstimate(flops=flops, bytes_accessed=1024, transcendentals=0),
    )(*operands)


def shards(loads, schur_flex, dirichlet, coupling, corner_index, face_lists, coarse_inverse):
    flex_mat = schur_flex[0, 0]
    prec_mat = dirichlet[0, 0]
    coupling_mat = coupling[0, 0]
    corners = corner_index[0, 0]
    face_index = face_lists[0, 0]
    load = loads[0, 0]
    ncoarse = coarse_inverse.shape[1]
    ncl, ni = coupling_mat.shape
    width = load.shape[1]
    face, half = ni // 4, ni // 2
    n_sx, n_sy = lax.axis_size("sx"), lax.axis_size("sy")
    at_x, at_y = lax.axis_index("sx"), lax.axis_index("sy")
    count = n_sx * n_sy

    has = jnp.stack([at_x > 0, at_x < n_sx - 1, at_y > 0, at_y < n_sy - 1])
    even = jnp.stack([at_x, at_y]) % 2 == 0
    flags = jnp.concatenate([jnp.where(has, 2.0, 1.0), jnp.where(even, 1.0, 0.0)]).astype(F32)
    select = (face_index[:, :, None] == jnp.arange(face, dtype=jnp.int32)).astype(BF16)
    coarse_ids = jnp.arange(ncoarse, dtype=jnp.int32)
    block = coarse_ids // (ncoarse // (n_sx * n_sy))
    origin = jnp.zeros_like(block)
    for at, (axis, bit) in enumerate(steps_of()):
        weight = bit * n_sy if axis == "sx" else bit
        origin = origin + ((block >> at) & 1) * weight
    origin = origin ^ (at_x * n_sy + at_y)
    within = coarse_ids % (ncoarse // (n_sx * n_sy))
    order = (origin * (ncoarse // (n_sx * n_sy)) + within)[None, :] == coarse_ids[:, None]
    order = order.astype(BF16)
    one_face, far_face = (face, width), (face + FAR_ROWS, width)
    parts = [pltpu.VMEM((half, width), BF16)] * 2
    one, select, order, flags = lax.optimization_barrier((jnp.ones((1, width), F32), select, order, flags))
    half_one = jnp.full((1, width), 0.5, F32)

    def early(matrix, owns, nears, coef, bases, lifts):
        operands = [flags, matrix, *owns, *nears, select, coef, *bases, *lifts]
        shapes = [one_face] * (4 if lifts else 2) + [(ni, width)]
        kernel = functools.partial(early_kernel, bool(bases), bool(lifts))
        *fields, partial = call(kernel, operands, shapes, parts, smem=1)
        return fields[:2], fields[2:], partial

    def crit(matrix, owns, nears, coef, partial, bases, lifts):
        operands = [flags, matrix, *owns, *nears, select, coef, partial, *bases, *lifts]
        shapes = [one_face] * (4 if lifts else 2) + [far_face] * 2
        kernel = functools.partial(crit_kernel, bool(bases), bool(lifts))
        *fields, a2, a3 = call(kernel, operands, shapes, parts, smem=1, flops=CRIT_FLOPS)
        return fields[:2], fields[2:], (a2, a3)

    def fields_of(matrix, owns, nears, coef, bases=(), lifts=(), beside=None):
        v01, q01, partial = early(matrix, owns[:2], nears[:2], coef, bases[:2], lifts)
        if beside is not None:
            partial, coef, made = beside(partial, coef)
        v23, q23, a23 = crit(matrix, owns[2:], nears[2:], coef, partial, bases[2:], lifts)
        fields = (*v01, *v23), (*q01, *q23), a23, partial
        return fields if beside is None else (*fields, made)

    def prec_late(values, a23, partial):
        operands = [flags, prec_mat, *values, *a23, partial]
        a0, a1, dots = call(prec_late_kernel, operands, [one_face, one_face, (1, width)], parts, smem=1)
        return (a0, a1, *a23), dots

    def flex_late(values, a23, partial, carried, other=()):
        operands = [flags, flex_mat, *values, *a23, *other, partial, coupling_mat, carried]
        kernel = functools.partial(flex_late_kernel, int(bool(other)))
        a0, a1, sums = call(kernel, operands, [one_face, one_face, (ncl + 8, width)], parts, smem=1)
        return (a0, a1, *a23), sums

    def solved(kernel, sums, faces, more, before=None):
        both = stacked_rows([sums, swapped(sums, "sy", 1)])
        others = [swapped(both, "sy", at) for at in range(2, n_sy, 2)]
        others, faces = lax.optimization_barrier((others, faces))
        near = (*exchanged(faces[:2], "sx"), *exchanged(faces[2:], "sy"))
        parts = [both, *others]
        origins = [block_of(at) for at in range(n_sy)]
        spread = functools.partial(spread_kernel, ncl, table_rows, origins)
        (total,) = call(spread, [table, *parts], [step_shape])
        for bit in bits_of("sx"):
            total = total + swapped(total, "sx", bit)
        scratch = [pltpu.VMEM((ncoarse, ncoarse), F32)]
        kernel = functools.partial(kernel, table_rows)
        if before is not None:
            total, near = before(total, near)
        (result,) = call(kernel, [total, table, order, *more], [step_shape], scratch)
        return near, total, result

    step_shape = (ncoarse + 8, width)
    extra = -(-face // width) * ncl
    copies = 4 * (1 + -(-face // width))
    sent = call(
        pack_kernel,
        [corners, load, coupling_mat],
        [(face + extra, width)] * 4,
        [pltpu.SemaphoreType.DMA((copies,))],
        smem=1,
        anywhere=(1, 2),
        limit=7 * LIMIT,
    )
    near = (*exchanged(sent[:2], "sx"), *exchanged(sent[2:], "sy"))

    own = coarse_inverse.shape[0]
    table_rows = own + 8
    inverse, _ = lax.optimization_barrier((coarse_inverse, sent[0]))
    (own_rows,) = call(rows_kernel, [corners, inverse], [(table_rows, ncoarse)], smem=1, flops=CRIT_FLOPS)

    def gather(partial, coef):
        table, coef = lax.optimization_barrier((doubled(own_rows, steps_of()), coef))
        return partial, coef, table

    residual0, _, a23, partial, table = fields_of(prec_mat, sent, near, one, beside=gather)
    applied0, rho0 = prec_late(residual0, a23, partial)
    (lift,) = call(
        lift_kernel, [flags, *near, select, coupling_mat, sent[0]], [(ni, ncoarse)], smem=1
    )
    near = (*exchanged(applied0[:2], "sx"), *exchanged(applied0[2:], "sy"))

    direction0, _, a23, partial = fields_of(flex_mat, applied0, near, half_one)
    fine0, sums = flex_late(direction0, a23, partial, rho0)
    near, total0, result0 = solved(first_step_kernel, sums, fine0, [])
    lifts = (lift, result0[:ncoarse])
    residual1, image0, a23, partial = fields_of(prec_mat, fine0, near, result0[ncoarse:], residual0, lifts)
    applied1, rho1 = prec_late(residual1, a23, partial)
    near = (*exchanged(applied1[:2], "sx"), *exchanged(applied1[2:], "sy"))

    precond, _, a23, partial = fields_of(flex_mat, applied1, near, half_one)
    fine1, sums = flex_late(precond, a23, partial, rho1, fine0)

    def jump_first(total, near):
        moved = call(moved_kernel, [flags, *fine1, *near, select], [one_face] * 4, smem=1)
        return lax.optimization_barrier((total, moved))

    moved, _, result1 = solved(second_step_kernel, sums, fine1, [total0, result0], jump_first)
    sol1, steps1 = result1[:ncoarse], result1[ncoarse:]

    def final(kernel, operands):
        ends = [pltpu.VMEM((4, face, width), F32), pltpu.SemaphoreType.DMA((4,))]
        return call(kernel, operands, [(ni, width)], ends, out_spec=ANY_SPEC)[0]

    multipliers = final(weighted_kernel, [*direction0, *precond, steps1])
    residual2 = final(tail_kernel, [*moved, *residual1, *image0, lift, sol1, steps1])
    return multipliers[None, None], residual2[None, None]


def solution(mesh):
    return jax.shard_map(
        shards,
        mesh=mesh,
        in_specs=(
            P("sx", "sy", None, None),
            P("sx", "sy", None, None),
            P("sx", "sy", None, None),
            P("sx", "sy", None, None),
            P("sx", "sy", None),
            P("sx", "sy", None, None),
            P(("sx", "sy"), None),
        ),
        out_specs=(P("sx", "sy", None, None), P("sx", "sy", None, None)),
        check_vma=False,
    )
```

```python
import functools

import jax
import jax.numpy as jnp
from jax import lax
from jax.experimental import pallas as pl
from jax.experimental.pallas import tpu as pltpu
from jax.sharding import PartitionSpec as P

HIGHEST = lax.Precision.HIGHEST
F32 = jnp.float32
BF16 = jnp.bfloat16
LIMIT = 8 * 1024 * 1024
CRIT_FLOPS = 8 * 10**9
FAR_ROWS = 8


def swapped(block, axis, bit):
    return lax.ppermute(block, axis, [(i, i ^ bit) for i in range(lax.axis_size(axis))])


def swapped_between(block, axis):
    route = []
    for i in range(1, lax.axis_size(axis) - 1, 2):
        route += [(i, i + 1), (i + 1, i)]
    return lax.ppermute(block, axis, route)


def exchanged(slots, axis):
    between = swapped_between(slots[1], axis)
    return swapped(slots[0], axis, 1), between


def bits_of(axis):
    return [1 << i for i in range((lax.axis_size(axis) - 1).bit_length())]


def steps_of():
    sx, sy = ([(axis, bit) for bit in bits_of(axis)[::-1]] for axis in ("sx", "sy"))
    return sy[-1:] + sy[:-1] + sx


def stacked_rows(parts):
    count = parts[0].shape[0]
    total = count * len(parts)
    return sum(jnp.pad(p, ((at * count, total - (at + 1) * count), (0, 0))) for at, p in enumerate(parts))


def doubled(rows, steps):
    for axis, bit in steps:
        rows = stacked_rows([rows, swapped(rows, axis, bit)])
    return rows


def block_of(other):
    return sum(1 << at for at, (axis, bit) in enumerate(steps_of()) if axis == "sy" and other & bit)


def split(x):
    high = x.astype(BF16)
    return high, (x - high.astype(F32)).astype(BF16)


def dot(a, b):
    return jnp.dot(a, b, preferred_element_type=F32)


def product(a, b_high, b_low):
    a_high, a_low = split(a)
    return dot(a_high, b_high) + (dot(a_high, b_low) + dot(a_low, b_high))


def thirds(x):
    high = x.astype(BF16)
    rest = x - high.astype(F32)
    mid = rest.astype(BF16)
    return high, mid, (rest - mid.astype(F32)).astype(BF16)


def permuted(select, rows):
    high, mid, low = thirds(rows)
    return dot(select, high) + (dot(select, mid) + dot(select, low))


def pair(flag, first, second):
    return jnp.where(flag == 1.0, second, first), jnp.where(flag == 1.0, first, second)


def faces_of(flags, slots):
    return (*pair(flags[4], slots[0], slots[1]), *pair(flags[5], slots[2], slots[3]))


def pack_kernel(corners, load, coupling, *refs):
    outs, sems = refs[:4], refs[4]
    face = load.shape[0] // 4
    width = load.shape[1]
    ncl = coupling.shape[0]
    even = [1 - lax.axis_index("sx") % 2, 1 - lax.axis_index("sy") % 2]
    faces = [even[0], 1 - even[0], 2 + even[1], 3 - even[1]]
    copies = []

    def copy(source, target):
        copies.append(pltpu.make_async_copy(source, target, sems.at[len(copies)]))
        copies[-1].start()

    for slot in (3, 2, 0, 1):
        first = pl.multiple_of(faces[slot] * face, 128)
        out = outs[slot]
        copy(load.at[pl.ds(first, face)], out.at[pl.ds(0, face)])
        for block, at in enumerate(range(0, face, width)):
            wide = min(width, face - at)
            source = coupling.at[:, pl.ds(pl.multiple_of(first + at, 128), wide)]
            copy(source, out.at[pl.ds(face + block * ncl, ncl), pl.ds(0, wide)])
    start = face + (face // width) * ncl
    for out in outs:
        for k in range(ncl):
            listed = jnp.full((1, width - face % width), corners[k].astype(F32))
            out[start + k : start + k + 1, face % width :] = listed
    for started in copies:
        started.wait()


def rows_kernel(corners, inverse, out):
    own = inverse.shape[0]
    out[:own] = inverse[...]
    out[own:] = jnp.zeros((out.shape[0] - own, out.shape[1]), F32)
    columns = lax.broadcasted_iota(jnp.int32, (1, out.shape[1]), 1)
    listed = jnp.zeros((1, out.shape[1]), F32)
    for k in range(corners.shape[0]):
        listed = jnp.where(columns == k, corners[k].astype(F32), listed)
    out[own : own + 1] = listed


def lift_kernel(flags, near0, near1, near2, near3, select, coupling, sent, out):
    face = out.shape[0] // 4
    ncoarse = out.shape[1]
    ncl = coupling.shape[0]
    ids = lax.broadcasted_iota(jnp.int32, (ncl, ncoarse), 1).astype(F32)
    own_pick = (sent[sent.shape[0] - ncl :, sent.shape[1] - 1 :] == ids).astype(F32)
    nears = faces_of(flags, [near[face:] for near in (near0, near1, near2, near3)])
    for f, near in enumerate(nears):
        columns = jnp.concatenate([near[at : at + ncl] for at in range(0, near.shape[0], ncl)], axis=1)
        near_pick = (columns[:, columns.shape[1] - 1 :] == ids).astype(F32)
        own = jnp.dot(coupling[:, f * face : (f + 1) * face].T, own_pick, precision=HIGHEST)
        theirs = jnp.dot(columns[:, :face].T, near_pick, precision=HIGHEST)
        out[f * face : (f + 1) * face] = own - permuted(select[f], theirs)


def field_into(at, owns, nears, select, flags, coef, bases, lifts, outs, images, high, low):
    size = outs[0].shape[0]
    if lifts:
        lift, sol = lifts
        corrections = product(lift[at * size : (at + 2) * size], *split(sol[...]))
    owns = pair(flags[4 + at // 2], *(own[:size] for own in owns))
    nears = pair(flags[4 + at // 2], *(near[:size] for near in nears))
    for f in range(2):
        image = owns[f] - permuted(select[at + f], nears[f])
        rows = slice(f * size, (f + 1) * size)
        if lifts:
            image = image + corrections[rows]
        if images:
            images[f][...] = image
        value = coef[0:1] * image
        if bases:
            value = bases[f][...] + value
        outs[f][...] = value
        high[rows], low[rows] = split(flags[at + f] * value)


def take(refs, *counts):
    groups = []
    for count in counts:
        groups.append(refs[:count])
        refs = refs[count:]
    return (*groups, refs)


def early_kernel(based, lifted, *refs):
    (flags, mat), owns, nears, (select, coef), bases, lifts, outs, images, rest = take(
        refs, 2, 2, 2, 2, 2 * based, 2 * lifted, 2, 2 * lifted
    )
    partial, high, low = rest
    field_into(0, owns, nears, select, flags, coef, bases, lifts, outs, images, high, low)
    half = high.shape[0]
    for rows in (slice(0, half), slice(half, 2 * half)):
        partial[rows] = product(mat[rows, :half], high[...], low[...])


def crit_kernel(based, lifted, *refs):
    (flags, mat), owns, nears, (select, coef, partial), bases, lifts, outs, images, rest = take(
        refs, 2, 2, 2, 3, 2 * based, 2 * lifted, 2, 2 * lifted
    )
    slot2, slot3, high, low = rest
    field_into(2, owns, nears, select, flags, coef, bases, lifts, outs, images, high, low)
    half = high.shape[0]
    size = half // 2
    value = partial[half:] + product(mat[half:, half:], high[...], low[...])
    slot3[:size], slot2[:size] = pair(flags[5], value[size:], value[:size])
    for slot in (slot2, slot3):
        slot[size:] = jnp.zeros((slot.shape[0] - size, slot.shape[1]), F32)


def late_rows(flags, mat, values, partial, high, low, slots):
    size = values[0].shape[0]
    for f in (2, 3):
        rows = slice((f - 2) * size, (f - 1) * size)
        high[rows], low[rows] = split(flags[f] * values[f][...])
    value = partial[: 2 * size] + product(mat[: 2 * size, 2 * size :], high[...], low[...])
    slots[1][...], slots[0][...] = pair(flags[4], value[size:], value[:size])
    return faces_of(flags, [slot[:size] for slot in slots])


def inner(flags, values, others):
    return sum(jnp.sum(flags[f] * values[f][...] * others[f], axis=0, keepdims=True) for f in range(4))


def prec_late_kernel(*refs):
    (flags, mat), values, applied, (partial, slot0, slot1, dots, high, low) = take(refs, 2, 4, 2)
    dots[...] = inner(flags, values, late_rows(flags, mat, values, partial, high, low, (slot0, slot1, *applied)))


def flex_late_kernel(others, *refs):
    (flags, mat), values, applied, other, rest = take(refs, 2, 4, 2, 4 * others)
    partial, coupling, carried, slot0, slot1, sums, high, low = rest
    size = slot0.shape[0]
    ncl = coupling.shape[0]
    coarse = None
    for f in range(4):
        term = product(coupling[:, f * size : (f + 1) * size], *split(flags[f] * values[f][...]))
        coarse = term if coarse is None else coarse + term
    faces = late_rows(flags, mat, values, partial, high, low, (slot0, slot1, *applied))
    rows = [inner(flags, values, faces), carried[...]]
    if others:
        rows.append(inner(flags, values, faces_of(flags, [slot[:size] for slot in other])))
    sums[:ncl] = coarse
    for at, row in enumerate(rows):
        sums[ncl + at : ncl + at + 1] = row
    end = ncl + len(rows)
    sums[end:] = jnp.zeros((sums.shape[0] - end, sums.shape[1]), F32)


def spread_kernel(ncl, rows, origins, table, *refs):
    parts, out = refs[:-1], refs[-1]
    ncoarse = out.shape[0] - 8
    ids = lax.broadcasted_iota(jnp.int32, (ncoarse, ncl), 0).astype(F32)
    size = ncl + 8
    each = parts[0].shape[0] // size
    coarse, dots = None, None
    for at, origin in enumerate(origins):
        start = origin * rows + rows - 8
        pick = (ids == table[start : start + 1, :ncl]).astype(BF16)
        values = parts[at // each][at % each * size : (at % each + 1) * size]
        term = permuted(pick, values[:ncl])
        coarse = term if coarse is None else coarse + term
        dots = values[ncl:] if dots is None else dots + values[ncl:]
    out[:ncoarse] = coarse
    out[ncoarse:] = dots


def inverse_from(table, rows, matrix):
    own = rows - 8
    for at in range(table.shape[0] // rows):
        matrix[at * own : (at + 1) * own] = table[at * rows : at * rows + own]


def first_step_kernel(rows, total, table, order, out, matrix):
    ncoarse = matrix.shape[0]
    inverse_from(table, rows, matrix)
    rhs = total[:ncoarse]
    sol = permuted(order[...], jnp.dot(matrix[...], rhs, precision=HIGHEST))
    fine_dot = total[ncoarse : ncoarse + 1]
    rho = 0.5 * total[ncoarse + 1 : ncoarse + 2]
    curve = fine_dot + jnp.sum(rhs * sol, axis=0, keepdims=True)
    out[:ncoarse] = sol
    out[ncoarse : ncoarse + 1] = -rho / curve
    out[ncoarse + 1 : ncoarse + 2] = rho
    out[ncoarse + 2 : ncoarse + 3] = fine_dot
    out[ncoarse + 3 :] = jnp.zeros((out.shape[0] - ncoarse - 3, out.shape[1]), F32)


def second_step_kernel(rows, total, table, order, total0, out0, out, matrix):
    ncoarse = matrix.shape[0]
    inverse_from(table, rows, matrix)
    rhs = total[:ncoarse]
    sol = permuted(order[...], jnp.dot(matrix[...], rhs, precision=HIGHEST))
    dot11, rho1, dot10 = (total[ncoarse + row : ncoarse + row + 1] for row in range(3))
    minus_step0, rho0, dot00 = (out0[ncoarse + row : ncoarse + row + 1] for row in range(3))
    rho1 = 0.5 * rho1
    beta = rho1 / rho0
    coarse = jnp.sum((rhs + beta * total0[:ncoarse]) * (sol + beta * out0[:ncoarse]), axis=0, keepdims=True)
    step1 = rho1 / (dot11 + 2.0 * beta * dot10 + beta * beta * dot00 + coarse)
    out[:ncoarse] = sol
    out[ncoarse : ncoarse + 1] = -step1
    out[ncoarse + 1 : ncoarse + 2] = -step1 * beta
    out[ncoarse + 2 : ncoarse + 3] = step1 * beta - minus_step0
    out[ncoarse + 3 : ncoarse + 4] = step1
    out[ncoarse + 4 :] = jnp.zeros((out.shape[0] - ncoarse - 4, out.shape[1]), F32)


def stored(values, out, sems):
    size = values.shape[1]
    return [
        pltpu.make_async_copy(values.at[f], out.at[pl.ds(f * size, size)], sems.at[f]) for f in range(4)
    ]


def tail_kernel(*refs):
    (flags,), owns, nears, residuals, images, (select, lift, sol, steps, out, values, sems) = take(
        refs, 1, 4, 4, 4, 4
    )
    stores = stored(values, out, sems)
    parts = split(sol[...])
    size = values.shape[1]
    owns = faces_of(flags, [own[:size] for own in owns])
    nears = faces_of(flags, [near[:size] for near in nears])
    for f in range(4):
        image = owns[f] - permuted(select[f], nears[f]) + product(lift[f * size : (f + 1) * size], *parts)
        values[f] = residuals[f][...] + steps[0:1] * image + steps[1:2] * images[f][...]
        stores[f].start()
    for copy in stores:
        copy.wait()


def weighted_kernel(*refs):
    firsts, seconds, (steps, out, values, sems) = take(refs, 4, 4)
    stores = stored(values, out, sems)
    for f in range(4):
        values[f] = steps[2:3] * firsts[f][...] + steps[3:4] * seconds[f][...]
        stores[f].start()
    for copy in stores:
        copy.wait()


VMEM_SPEC = pl.BlockSpec(memory_space=pltpu.VMEM)
SMEM_SPEC = pl.BlockSpec(memory_space=pltpu.SMEM)
ANY_SPEC = pl.BlockSpec(memory_space=pl.ANY)


def call(kernel, operands, shapes, scratch=(), smem=0, anywhere=(), out_spec=VMEM_SPEC, flops=1024, limit=LIMIT):
    return pl.pallas_call(
        kernel,
        in_specs=[SMEM_SPEC if i < smem else ANY_SPEC if i in anywhere else VMEM_SPEC for i in range(len(operands))],
        out_specs=[out_spec] * len(shapes),
        out_shape=[jax.ShapeDtypeStruct(s, F32) for s in shapes],
        scratch_shapes=list(scratch),
        compiler_params=pltpu.CompilerParams(vmem_limit_bytes=limit),
        cost_estimate=pl.CostEstimate(flops=flops, bytes_accessed=1024, transcendentals=0),
    )(*operands)


def shards(loads, schur_flex, dirichlet, coupling, corner_index, face_lists, coarse_inverse):
    flex_mat = schur_flex[0, 0]
    prec_mat = dirichlet[0, 0]
    coupling_mat = coupling[0, 0]
    corners = corner_index[0, 0]
    face_index = face_lists[0, 0]
    load = loads[0, 0]
    ncoarse = coarse_inverse.shape[1]
    ncl, ni = coupling_mat.shape
    width = load.shape[1]
    face, half = ni // 4, ni // 2
    n_sx, n_sy = lax.axis_size("sx"), lax.axis_size("sy")
    at_x, at_y = lax.axis_index("sx"), lax.axis_index("sy")
    count = n_sx * n_sy

    has = jnp.stack([at_x > 0, at_x < n_sx - 1, at_y > 0, at_y < n_sy - 1])
    even = jnp.stack([at_x, at_y]) % 2 == 0
    flags = jnp.concatenate([jnp.where(has, 2.0, 1.0), jnp.where(even, 1.0, 0.0)]).astype(F32)
    select = (face_index[:, :, None] == jnp.arange(face, dtype=jnp.int32)).astype(BF16)
    coarse_ids = jnp.arange(ncoarse, dtype=jnp.int32)
    block = coarse_ids // (ncoarse // (n_sx * n_sy))
    origin = jnp.zeros_like(block)
    for at, (axis, bit) in enumerate(steps_of()):
        weight = bit * n_sy if axis == "sx" else bit
        origin = origin + ((block >> at) & 1) * weight
    origin = origin ^ (at_x * n_sy + at_y)
    within = coarse_ids % (ncoarse // (n_sx * n_sy))
    order = (origin * (ncoarse // (n_sx * n_sy)) + within)[None, :] == coarse_ids[:, None]
    order = order.astype(BF16)
    one_face, far_face = (face, width), (face + FAR_ROWS, width)
    parts = [pltpu.VMEM((half, width), BF16)] * 2
    one, select, order, flags = lax.optimization_barrier((jnp.ones((1, width), F32), select, order, flags))
    half_one = jnp.full((1, width), 0.5, F32)

    def early(matrix, owns, nears, coef, bases, lifts):
        operands = [flags, matrix, *owns, *nears, select, coef, *bases, *lifts]
        shapes = [one_face] * (4 if lifts else 2) + [(ni, width)]
        kernel = functools.partial(early_kernel, bool(bases), bool(lifts))
        *fields, partial = call(kernel, operands, shapes, parts, smem=1)
        return fields[:2], fields[2:], partial

    def crit(matrix, owns, nears, coef, partial, bases, lifts):
        operands = [flags, matrix, *owns, *nears, select, coef, partial, *bases, *lifts]
        shapes = [one_face] * (4 if lifts else 2) + [far_face] * 2
        kernel = functools.partial(crit_kernel, bool(bases), bool(lifts))
        *fields, a2, a3 = call(kernel, operands, shapes, parts, smem=1, flops=CRIT_FLOPS)
        return fields[:2], fields[2:], (a2, a3)

    def fields_of(matrix, owns, nears, coef, bases=(), lifts=(), beside=None):
        v01, q01, partial = early(matrix, owns[:2], nears[:2], coef, bases[:2], lifts)
        if beside is not None:
            partial, coef, made = beside(partial, coef)
        v23, q23, a23 = crit(matrix, owns[2:], nears[2:], coef, partial, bases[2:], lifts)
        fields = (*v01, *v23), (*q01, *q23), a23, partial
        return fields if beside is None else (*fields, made)

    def prec_late(values, a23, partial):
        operands = [flags, prec_mat, *values, *a23, partial]
        a0, a1, dots = call(prec_late_kernel, operands, [one_face, one_face, (1, width)], parts, smem=1)
        return (a0, a1, *a23), dots

    def flex_late(values, a23, partial, carried, other=()):
        operands = [flags, flex_mat, *values, *a23, *other, partial, coupling_mat, carried]
        kernel = functools.partial(flex_late_kernel, int(bool(other)))
        a0, a1, sums = call(kernel, operands, [one_face, one_face, (ncl + 8, width)], parts, smem=1)
        return (a0, a1, *a23), sums

    def solved(kernel, sums, faces, more):
        other, *far = lax.optimization_barrier((swapped(sums, "sy", 1), *faces[2:]))
        far = exchanged(far, "sy")
        close = faces[:2]
        parts, origins = [sums, other], [0, 1]
        for bit in bits_of("sy")[:0:-1]:
            rows = stacked_rows(parts)
            other, *close = lax.optimization_barrier((swapped(rows, "sy", bit), *close))
            parts = [rows, other]
            origins = origins + [at ^ bit for at in origins]
        origins = [block_of(at) for at in origins]
        spread = functools.partial(spread_kernel, ncl, table_rows, origins)
        (total,) = call(spread, [table, *parts], [step_shape])
        for bit in bits_of("sx"):
            total = total + swapped(total, "sx", bit)
        scratch = [pltpu.VMEM((ncoarse, ncoarse), F32)]
        kernel = functools.partial(kernel, table_rows)
        (result,) = call(kernel, [total, table, order, *more], [step_shape], scratch)
        return (*exchanged(close, "sx"), *far), total, result

    step_shape = (ncoarse + 8, width)
    extra = -(-face // width) * ncl
    copies = 4 * (1 + -(-face // width))
    sent = call(
        pack_kernel,
        [corners, load, coupling_mat],
        [(face + extra, width)] * 4,
        [pltpu.SemaphoreType.DMA((copies,))],
        smem=1,
        anywhere=(1, 2),
        limit=7 * LIMIT,
    )
    near = (*exchanged(sent[:2], "sx"), *exchanged(sent[2:], "sy"))

    own = coarse_inverse.shape[0]
    table_rows = own + 8
    inverse, _ = lax.optimization_barrier((coarse_inverse, sent[0]))
    (own_rows,) = call(rows_kernel, [corners, inverse], [(table_rows, ncoarse)], smem=1, flops=CRIT_FLOPS)

    def gather(partial, coef):
        rows, coef = lax.optimization_barrier((doubled(own_rows, steps_of()[:-1]), coef))
        return partial, coef, rows

    residual0, _, a23, partial, rows = fields_of(prec_mat, sent, near, one, beside=gather)
    applied0, rho0 = prec_late(residual0, a23, partial)
    (lift,) = call(
        lift_kernel, [flags, *near, select, coupling_mat, sent[0]], [(ni, ncoarse)], smem=1
    )
    table, half_one = lax.optimization_barrier((doubled(rows, steps_of()[-1:]), half_one))
    near = (*exchanged(applied0[:2], "sx"), *exchanged(applied0[2:], "sy"))

    direction0, _, a23, partial = fields_of(flex_mat, applied0, near, half_one)
    fine0, sums = flex_late(direction0, a23, partial, rho0)
    near, total0, result0 = solved(first_step_kernel, sums, fine0, [])
    lifts = (lift, result0[:ncoarse])
    residual1, image0, a23, partial = fields_of(prec_mat, fine0, near, result0[ncoarse:], residual0, lifts)
    applied1, rho1 = prec_late(residual1, a23, partial)
    near = (*exchanged(applied1[:2], "sx"), *exchanged(applied1[2:], "sy"))

    precond, _, a23, partial = fields_of(flex_mat, applied1, near, half_one)
    fine1, sums = flex_late(precond, a23, partial, rho1, fine0)
    near, _, result1 = solved(second_step_kernel, sums, fine1, [total0, result0])
    sol1, steps1 = result1[:ncoarse], result1[ncoarse:]

    def final(kernel, operands, smem=0):
        ends = [pltpu.VMEM((4, face, width), F32), pltpu.SemaphoreType.DMA((4,))]
        return call(kernel, operands, [(ni, width)], ends, smem=smem, out_spec=ANY_SPEC)[0]

    multipliers = final(weighted_kernel, [*direction0, *precond, steps1])
    operands = [flags, *fine1, *near, *residual1, *image0, select, lift, sol1, steps1]
    residual2 = final(tail_kernel, operands, smem=1)
    return multipliers[None, None], residual2[None, None]


def solution(mesh):
    return jax.shard_map(
        shards,
        mesh=mesh,
        in_specs=(
            P("sx", "sy", None, None),
            P("sx", "sy", None, None),
            P("sx", "sy", None, None),
            P("sx", "sy", None, None),
            P("sx", "sy", None),
            P("sx", "sy", None, None),
            P(("sx", "sy"), None),
        ),
        out_specs=(P("sx", "sy", None, None), P("sx", "sy", None, None)),
        check_vma=False,
    )
```

```python
import functools

import jax
import jax.numpy as jnp
from jax import lax
from jax.experimental import pallas as pl
from jax.experimental.pallas import tpu as pltpu
from jax.sharding import PartitionSpec as P

HIGHEST = lax.Precision.HIGHEST
F32 = jnp.float32
BF16 = jnp.bfloat16
LIMIT = 8 * 1024 * 1024
CRIT_FLOPS = 8 * 10**9
FAR_ROWS = 8


def swapped(block, axis, bit):
    return lax.ppermute(block, axis, [(i, i ^ bit) for i in range(lax.axis_size(axis))])


def swapped_between(block, axis):
    route = []
    for i in range(1, lax.axis_size(axis) - 1, 2):
        route += [(i, i + 1), (i + 1, i)]
    return lax.ppermute(block, axis, route)


def exchanged(slots, axis):
    between = swapped_between(slots[1], axis)
    return swapped(slots[0], axis, 1), between


def bits_of(axis):
    return [1 << i for i in range((lax.axis_size(axis) - 1).bit_length())]


def steps_of():
    return [("sy", 1)] + [("sx", bit) for bit in bits_of("sx")] + [("sy", bit) for bit in bits_of("sy")[:0:-1]]


def stacked_rows(parts):
    count = parts[0].shape[0]
    total = count * len(parts)
    return sum(jnp.pad(p, ((at * count, total - (at + 1) * count), (0, 0))) for at, p in enumerate(parts))


def doubled(rows, steps):
    for axis, bit in steps:
        rows = stacked_rows([rows, swapped(rows, axis, bit)])
    return rows


def block_of(other):
    return sum(1 << at for at, (axis, bit) in enumerate(steps_of()) if axis == "sy" and other & bit)


def split(x):
    high = x.astype(BF16)
    return high, (x - high.astype(F32)).astype(BF16)


def dot(a, b):
    return jnp.dot(a, b, preferred_element_type=F32)


def product(a, b_high, b_low):
    a_high, a_low = split(a)
    return dot(a_high, b_high) + (dot(a_high, b_low) + dot(a_low, b_high))


def thirds(x):
    high = x.astype(BF16)
    rest = x - high.astype(F32)
    mid = rest.astype(BF16)
    return high, mid, (rest - mid.astype(F32)).astype(BF16)


def permuted(select, rows):
    high, mid, low = thirds(rows)
    return dot(select, high) + (dot(select, mid) + dot(select, low))


def pair(flag, first, second):
    return jnp.where(flag == 1.0, second, first), jnp.where(flag == 1.0, first, second)


def faces_of(flags, slots):
    return (*pair(flags[4], slots[0], slots[1]), *pair(flags[5], slots[2], slots[3]))


def pack_kernel(corners, load, coupling, *refs):
    outs, sems = refs[:4], refs[4]
    face = load.shape[0] // 4
    width = load.shape[1]
    ncl = coupling.shape[0]
    even = [1 - lax.axis_index("sx") % 2, 1 - lax.axis_index("sy") % 2]
    faces = [even[0], 1 - even[0], 2 + even[1], 3 - even[1]]
    copies = []

    def copy(source, target):
        copies.append(pltpu.make_async_copy(source, target, sems.at[len(copies)]))
        copies[-1].start()

    for slot in (3, 2, 0, 1):
        first = pl.multiple_of(faces[slot] * face, 128)
        out = outs[slot]
        copy(load.at[pl.ds(first, face)], out.at[pl.ds(0, face)])
        for block, at in enumerate(range(0, face, width)):
            wide = min(width, face - at)
            source = coupling.at[:, pl.ds(pl.multiple_of(first + at, 128), wide)]
            copy(source, out.at[pl.ds(face + block * ncl, ncl), pl.ds(0, wide)])
    start = face + (face // width) * ncl
    for out in outs:
        for k in range(ncl):
            listed = jnp.full((1, width - face % width), corners[k].astype(F32))
            out[start + k : start + k + 1, face % width :] = listed
        if out.shape[0] > start + ncl:
            out[start + ncl :] = jnp.zeros((out.shape[0] - start - ncl, width), F32)
    for started in copies:
        started.wait()


def rows_kernel(corners, inverse, out):
    own = inverse.shape[0]
    out[:own] = inverse[...]
    out[own:] = jnp.zeros((out.shape[0] - own, out.shape[1]), F32)
    columns = lax.broadcasted_iota(jnp.int32, (1, out.shape[1]), 1)
    listed = jnp.zeros((1, out.shape[1]), F32)
    for k in range(corners.shape[0]):
        listed = jnp.where(columns == k, corners[k].astype(F32), listed)
    out[own : own + 1] = listed


def lift_kernel(flags, near0, near1, near2, near3, select, coupling, sent, out):
    face = out.shape[0] // 4
    ncoarse = out.shape[1]
    ncl = coupling.shape[0]
    ids = lax.broadcasted_iota(jnp.int32, (ncl, ncoarse), 1).astype(F32)
    own_pick = (sent[sent.shape[0] - ncl :, sent.shape[1] - 1 :] == ids).astype(F32)
    end = near0.shape[0]
    nears = faces_of(flags, [near[face:end] for near in (near0, near1, near2, near3)])
    for f, near in enumerate(nears):
        columns = jnp.concatenate([near[at : at + ncl] for at in range(0, near.shape[0], ncl)], axis=1)
        near_pick = (columns[:, columns.shape[1] - 1 :] == ids).astype(F32)
        own = jnp.dot(coupling[:, f * face : (f + 1) * face].T, own_pick, precision=HIGHEST)
        theirs = jnp.dot(columns[:, :face].T, near_pick, precision=HIGHEST)
        out[f * face : (f + 1) * face] = own - permuted(select[f], theirs)


def field_into(at, owns, nears, select, flags, coef, bases, lifts, outs, images, high, low):
    size = outs[0].shape[0]
    if lifts:
        lift, sol = lifts
        corrections = product(lift[at * size : (at + 2) * size], *split(sol[...]))
    owns = pair(flags[4 + at // 2], *(own[:size] for own in owns))
    nears = pair(flags[4 + at // 2], *(near[:size] for near in nears))
    for f in range(2):
        image = owns[f] - permuted(select[at + f], nears[f])
        rows = slice(f * size, (f + 1) * size)
        if lifts:
            image = image + corrections[rows]
        if images:
            images[f][...] = image
        value = coef[0:1] * image
        if bases:
            value = bases[f][...] + value
        outs[f][...] = value
        high[rows], low[rows] = split(flags[at + f] * value)


def take(refs, *counts):
    groups = []
    for count in counts:
        groups.append(refs[:count])
        refs = refs[count:]
    return (*groups, refs)


def early_kernel(based, lifted, *refs):
    (flags, mat), owns, nears, (select, coef), bases, lifts, outs, images, rest = take(
        refs, 2, 2, 2, 2, 2 * based, 2 * lifted, 2, 2 * lifted
    )
    partial, high, low = rest
    field_into(0, owns, nears, select, flags, coef, bases, lifts, outs, images, high, low)
    half = high.shape[0]
    for rows in (slice(0, half), slice(half, 2 * half)):
        partial[rows] = product(mat[rows, :half], high[...], low[...])


def crit_kernel(based, lifted, *refs):
    (flags, mat), owns, nears, (select, coef, partial), bases, lifts, outs, images, rest = take(
        refs, 2, 2, 2, 3, 2 * based, 2 * lifted, 2, 2 * lifted
    )
    slot2, slot3, high, low = rest
    field_into(2, owns, nears, select, flags, coef, bases, lifts, outs, images, high, low)
    half = high.shape[0]
    size = half // 2
    value = partial[half:] + product(mat[half:, half:], high[...], low[...])
    slot3[:size], slot2[:size] = pair(flags[5], value[size:], value[:size])
    for slot in (slot2, slot3):
        slot[size:] = jnp.zeros((slot.shape[0] - size, slot.shape[1]), F32)


def late_rows(flags, mat, values, partial, high, low, slots):
    size = values[0].shape[0]
    for f in (2, 3):
        rows = slice((f - 2) * size, (f - 1) * size)
        high[rows], low[rows] = split(flags[f] * values[f][...])
    value = partial[: 2 * size] + product(mat[: 2 * size, 2 * size :], high[...], low[...])
    slots[1][...], slots[0][...] = pair(flags[4], value[size:], value[:size])
    return faces_of(flags, [slot[:size] for slot in slots])


def inner(flags, values, others):
    return sum(jnp.sum(flags[f] * values[f][...] * others[f], axis=0, keepdims=True) for f in range(4))


def prec_late_kernel(*refs):
    (flags, mat), values, applied, (partial, slot0, slot1, dots, high, low) = take(refs, 2, 4, 2)
    dots[...] = inner(flags, values, late_rows(flags, mat, values, partial, high, low, (slot0, slot1, *applied)))


def flex_late_kernel(others, *refs):
    (flags, mat), values, applied, other, rest = take(refs, 2, 4, 2, 4 * others)
    partial, coupling, carried, slot0, slot1, sums, high, low = rest
    size = slot0.shape[0]
    ncl = coupling.shape[0]
    coarse = None
    for f in range(4):
        term = product(coupling[:, f * size : (f + 1) * size], *split(flags[f] * values[f][...]))
        coarse = term if coarse is None else coarse + term
    faces = late_rows(flags, mat, values, partial, high, low, (slot0, slot1, *applied))
    rows = [inner(flags, values, faces), carried[...]]
    if others:
        rows.append(inner(flags, values, faces_of(flags, [slot[:size] for slot in other])))
    sums[:ncl] = coarse
    for at, row in enumerate(rows):
        sums[ncl + at : ncl + at + 1] = row
    end = ncl + len(rows)
    sums[end:] = jnp.zeros((sums.shape[0] - end, sums.shape[1]), F32)


def spread_kernel(ncl, rows, origins, table, *refs):
    parts, out = refs[:-1], refs[-1]
    ncoarse = out.shape[0] - 8
    ids = lax.broadcasted_iota(jnp.int32, (ncoarse, ncl), 0).astype(F32)
    size = ncl + 8
    each = parts[0].shape[0] // size
    coarse, dots = None, None
    for at, origin in enumerate(origins):
        start = origin * rows + rows - 8
        pick = (ids == table[start : start + 1, :ncl]).astype(BF16)
        values = parts[at // each][at % each * size : (at % each + 1) * size]
        term = permuted(pick, values[:ncl])
        coarse = term if coarse is None else coarse + term
        dots = values[ncl:] if dots is None else dots + values[ncl:]
    out[:ncoarse] = coarse
    out[ncoarse:] = dots


def inverse_from(table, rows, matrix):
    own = rows - 8
    for at in range(table.shape[0] // rows):
        matrix[at * own : (at + 1) * own] = table[at * rows : at * rows + own]


def first_step_kernel(rows, total, table, order, out, matrix):
    ncoarse = matrix.shape[0]
    inverse_from(table, rows, matrix)
    rhs = total[:ncoarse]
    sol = permuted(order[...], jnp.dot(matrix[...], rhs, precision=HIGHEST))
    fine_dot = total[ncoarse : ncoarse + 1]
    rho = 0.5 * total[ncoarse + 1 : ncoarse + 2]
    curve = fine_dot + jnp.sum(rhs * sol, axis=0, keepdims=True)
    out[:ncoarse] = sol
    out[ncoarse : ncoarse + 1] = -rho / curve
    out[ncoarse + 1 : ncoarse + 2] = rho
    out[ncoarse + 2 : ncoarse + 3] = fine_dot
    out[ncoarse + 3 :] = jnp.zeros((out.shape[0] - ncoarse - 3, out.shape[1]), F32)


def second_step_kernel(rows, total, table, order, total0, out0, out, matrix):
    ncoarse = matrix.shape[0]
    inverse_from(table, rows, matrix)
    rhs = total[:ncoarse]
    sol = permuted(order[...], jnp.dot(matrix[...], rhs, precision=HIGHEST))
    dot11, rho1, dot10 = (total[ncoarse + row : ncoarse + row + 1] for row in range(3))
    minus_step0, rho0, dot00 = (out0[ncoarse + row : ncoarse + row + 1] for row in range(3))
    rho1 = 0.5 * rho1
    beta = rho1 / rho0
    coarse = jnp.sum((rhs + beta * total0[:ncoarse]) * (sol + beta * out0[:ncoarse]), axis=0, keepdims=True)
    step1 = rho1 / (dot11 + 2.0 * beta * dot10 + beta * beta * dot00 + coarse)
    out[:ncoarse] = sol
    out[ncoarse : ncoarse + 1] = -step1
    out[ncoarse + 1 : ncoarse + 2] = -step1 * beta
    out[ncoarse + 2 : ncoarse + 3] = step1 * beta - minus_step0
    out[ncoarse + 3 : ncoarse + 4] = step1
    out[ncoarse + 4 :] = jnp.zeros((out.shape[0] - ncoarse - 4, out.shape[1]), F32)


def stored(values, out, sems):
    size = values.shape[1]
    return [
        pltpu.make_async_copy(values.at[f], out.at[pl.ds(f * size, size)], sems.at[f]) for f in range(4)
    ]


def tail_kernel(*refs):
    (flags,), owns, nears, residuals, images, (select, lift, sol, steps, out, values, sems) = take(
        refs, 1, 4, 4, 4, 4
    )
    stores = stored(values, out, sems)
    parts = split(sol[...])
    size = values.shape[1]
    owns = faces_of(flags, [own[:size] for own in owns])
    nears = faces_of(flags, [near[:size] for near in nears])
    for f in range(4):
        image = owns[f] - permuted(select[f], nears[f]) + product(lift[f * size : (f + 1) * size], *parts)
        values[f] = residuals[f][...] + steps[0:1] * image + steps[1:2] * images[f][...]
        stores[f].start()
    for copy in stores:
        copy.wait()


def weighted_kernel(*refs):
    firsts, seconds, (steps, out, values, sems) = take(refs, 4, 4)
    stores = stored(values, out, sems)
    for f in range(4):
        values[f] = steps[2:3] * firsts[f][...] + steps[3:4] * seconds[f][...]
        stores[f].start()
    for copy in stores:
        copy.wait()


VMEM_SPEC = pl.BlockSpec(memory_space=pltpu.VMEM)
SMEM_SPEC = pl.BlockSpec(memory_space=pltpu.SMEM)
ANY_SPEC = pl.BlockSpec(memory_space=pl.ANY)


def call(kernel, operands, shapes, scratch=(), smem=0, anywhere=(), out_spec=VMEM_SPEC, flops=1024, limit=LIMIT):
    return pl.pallas_call(
        kernel,
        in_specs=[SMEM_SPEC if i < smem else ANY_SPEC if i in anywhere else VMEM_SPEC for i in range(len(operands))],
        out_specs=[out_spec] * len(shapes),
        out_shape=[jax.ShapeDtypeStruct(s, F32) for s in shapes],
        scratch_shapes=list(scratch),
        compiler_params=pltpu.CompilerParams(vmem_limit_bytes=limit),
        cost_estimate=pl.CostEstimate(flops=flops, bytes_accessed=1024, transcendentals=0),
    )(*operands)


def shards(loads, schur_flex, dirichlet, coupling, corner_index, face_lists, coarse_inverse):
    flex_mat = schur_flex[0, 0]
    prec_mat = dirichlet[0, 0]
    coupling_mat = coupling[0, 0]
    corners = corner_index[0, 0]
    face_index = face_lists[0, 0]
    load = loads[0, 0]
    ncoarse = coarse_inverse.shape[1]
    ncl, ni = coupling_mat.shape
    width = load.shape[1]
    face, half = ni // 4, ni // 2
    n_sx, n_sy = lax.axis_size("sx"), lax.axis_size("sy")
    at_x, at_y = lax.axis_index("sx"), lax.axis_index("sy")
    count = n_sx * n_sy

    has = jnp.stack([at_x > 0, at_x < n_sx - 1, at_y > 0, at_y < n_sy - 1])
    even = jnp.stack([at_x, at_y]) % 2 == 0
    flags = jnp.concatenate([jnp.where(has, 2.0, 1.0), jnp.where(even, 1.0, 0.0)]).astype(F32)
    select = (face_index[:, :, None] == jnp.arange(face, dtype=jnp.int32)).astype(BF16)
    coarse_ids = jnp.arange(ncoarse, dtype=jnp.int32)
    block = coarse_ids // (ncoarse // (n_sx * n_sy))
    origin = jnp.zeros_like(block)
    for at, (axis, bit) in enumerate(steps_of()):
        weight = bit * n_sy if axis == "sx" else bit
        origin = origin + ((block >> at) & 1) * weight
    origin = origin ^ (at_x * n_sy + at_y)
    within = coarse_ids % (ncoarse // (n_sx * n_sy))
    order = (origin * (ncoarse // (n_sx * n_sy)) + within)[None, :] == coarse_ids[:, None]
    order = order.astype(BF16)
    one_face, far_face = (face, width), (face + FAR_ROWS, width)
    parts = [pltpu.VMEM((half, width), BF16)] * 2
    one, select, order, flags = lax.optimization_barrier((jnp.ones((1, width), F32), select, order, flags))
    half_one = jnp.full((1, width), 0.5, F32)

    def early(matrix, owns, nears, coef, bases, lifts):
        operands = [flags, matrix, *owns, *nears, select, coef, *bases, *lifts]
        shapes = [one_face] * (4 if lifts else 2) + [(ni, width)]
        kernel = functools.partial(early_kernel, bool(bases), bool(lifts))
        *fields, partial = call(kernel, operands, shapes, parts, smem=1)
        return fields[:2], fields[2:], partial

    def crit(matrix, owns, nears, coef, partial, bases, lifts):
        operands = [flags, matrix, *owns, *nears, select, coef, partial, *bases, *lifts]
        shapes = [one_face] * (4 if lifts else 2) + [far_face] * 2
        kernel = functools.partial(crit_kernel, bool(bases), bool(lifts))
        *fields, a2, a3 = call(kernel, operands, shapes, parts, smem=1, flops=CRIT_FLOPS)
        return fields[:2], fields[2:], (a2, a3)

    def fields_of(matrix, owns, nears, coef, bases=(), lifts=(), beside=None):
        v01, q01, partial = early(matrix, owns[:2], nears[:2], coef, bases[:2], lifts)
        if beside is not None:
            partial, coef, made = beside(partial, coef)
        v23, q23, a23 = crit(matrix, owns[2:], nears[2:], coef, partial, bases[2:], lifts)
        fields = (*v01, *v23), (*q01, *q23), a23, partial
        return fields if beside is None else (*fields, made)

    def prec_late(values, a23, partial):
        operands = [flags, prec_mat, *values, *a23, partial]
        a0, a1, dots = call(prec_late_kernel, operands, [one_face, one_face, (1, width)], parts, smem=1)
        return (a0, a1, *a23), dots

    def flex_late(values, a23, partial, carried, other=()):
        operands = [flags, flex_mat, *values, *a23, *other, partial, coupling_mat, carried]
        kernel = functools.partial(flex_late_kernel, int(bool(other)))
        a0, a1, sums = call(kernel, operands, [one_face, one_face, (ncl + 8, width)], parts, smem=1)
        return (a0, a1, *a23), sums

    def solved(kernel, sums, faces, more):
        other, *far = lax.optimization_barrier((swapped(sums, "sy", 1), *faces[2:]))
        far = exchanged(far, "sy")
        close = faces[:2]
        parts, origins = [sums, other], [0, 1]
        for bit in bits_of("sy")[:0:-1]:
            rows = stacked_rows(parts)
            other, *close = lax.optimization_barrier((swapped(rows, "sy", bit), *close))
            parts = [rows, other]
            origins = origins + [at ^ bit for at in origins]
        origins = [block_of(at) for at in origins]
        spread = functools.partial(spread_kernel, ncl, table_rows, origins)
        (total,) = call(spread, [table, *parts], [step_shape])
        for bit in bits_of("sx"):
            total = total + swapped(total, "sx", bit)
        scratch = [pltpu.VMEM((ncoarse, ncoarse), F32)]
        kernel = functools.partial(kernel, table_rows)
        (result,) = call(kernel, [total, table, order, *more], [step_shape], scratch)
        return (*exchanged(close, "sx"), *far), total, result

    step_shape = (ncoarse + 8, width)
    extra = -(-face // width) * ncl
    copies = 4 * (1 + -(-face // width))
    sent = call(
        pack_kernel,
        [corners, load, coupling_mat],
        [(face + extra, width)] * 2 + [(face + extra + FAR_ROWS, width)] * 2,
        [pltpu.SemaphoreType.DMA((copies,))],
        smem=1,
        anywhere=(1, 2),
        limit=7 * LIMIT,
    )
    near = (*exchanged(sent[:2], "sx"), *exchanged(sent[2:], "sy"))

    own = coarse_inverse.shape[0]
    table_rows = own + 8
    inverse, flags, order, _ = lax.optimization_barrier((coarse_inverse, flags, order, sent[0]))
    (own_rows,) = call(rows_kernel, [corners, inverse], [(table_rows, ncoarse)], smem=1, flops=CRIT_FLOPS)

    def gather(partial, coef):
        rows, coef = lax.optimization_barrier((doubled(own_rows, steps_of()[:-1]), coef))
        return partial, coef, rows

    residual0, _, a23, partial, rows = fields_of(prec_mat, sent, near, one, beside=gather)
    applied0, rho0 = prec_late(residual0, a23, partial)
    (lift,) = call(
        lift_kernel, [flags, *near, select, coupling_mat, sent[0]], [(ni, ncoarse)], smem=1
    )
    table, half_one = lax.optimization_barrier((doubled(rows, steps_of()[-1:]), half_one))
    near = (*exchanged(applied0[:2], "sx"), *exchanged(applied0[2:], "sy"))

    direction0, _, a23, partial = fields_of(flex_mat, applied0, near, half_one)
    fine0, sums = flex_late(direction0, a23, partial, rho0)
    near, total0, result0 = solved(first_step_kernel, sums, fine0, [])
    lifts = (lift, result0[:ncoarse])
    residual1, image0, a23, partial = fields_of(prec_mat, fine0, near, result0[ncoarse:], residual0, lifts)
    applied1, rho1 = prec_late(residual1, a23, partial)
    near = (*exchanged(applied1[:2], "sx"), *exchanged(applied1[2:], "sy"))

    precond, _, a23, partial = fields_of(flex_mat, applied1, near, half_one)
    fine1, sums = flex_late(precond, a23, partial, rho1, fine0)
    near, _, result1 = solved(second_step_kernel, sums, fine1, [total0, result0])
    sol1, steps1 = result1[:ncoarse], result1[ncoarse:]

    def final(kernel, operands, smem=0):
        ends = [pltpu.VMEM((4, face, width), F32), pltpu.SemaphoreType.DMA((4,))]
        return call(kernel, operands, [(ni, width)], ends, smem=smem, out_spec=ANY_SPEC)[0]

    multipliers = final(weighted_kernel, [*direction0, *precond, steps1])
    operands = [flags, *fine1, *near, *residual1, *image0, select, lift, sol1, steps1]
    residual2 = final(tail_kernel, operands, smem=1)
    return multipliers[None, None], residual2[None, None]


def solution(mesh):
    return jax.shard_map(
        shards,
        mesh=mesh,
        in_specs=(
            P("sx", "sy", None, None),
            P("sx", "sy", None, None),
            P("sx", "sy", None, None),
            P("sx", "sy", None, None),
            P("sx", "sy", None),
            P("sx", "sy", None, None),
            P(("sx", "sy"), None),
        ),
        out_specs=(P("sx", "sy", None, None), P("sx", "sy", None, None)),
        check_vma=False,
    )
```

```python
import functools

import jax
import jax.numpy as jnp
from jax import lax
from jax.experimental import pallas as pl
from jax.experimental.pallas import tpu as pltpu
from jax.sharding import PartitionSpec as P

HIGHEST = lax.Precision.HIGHEST
F32 = jnp.float32
BF16 = jnp.bfloat16
LIMIT = 8 * 1024 * 1024
CRIT_FLOPS = 8 * 10**9
FAR_ROWS = 8


def swapped(block, axis, bit):
    return lax.ppermute(block, axis, [(i, i ^ bit) for i in range(lax.axis_size(axis))])


def swapped_between(block, axis):
    route = []
    for i in range(1, lax.axis_size(axis) - 1, 2):
        route += [(i, i + 1), (i + 1, i)]
    return lax.ppermute(block, axis, route)


def exchanged(slots, axis):
    between = swapped_between(slots[1], axis)
    return swapped(slots[0], axis, 1), between


def bits_of(axis):
    return [1 << i for i in range((lax.axis_size(axis) - 1).bit_length())]


def steps_of():
    return [("sy", 1)] + [("sx", bit) for bit in bits_of("sx")[::-1]] + [("sy", bit) for bit in bits_of("sy")[:0:-1]]


def stacked_rows(parts):
    count = parts[0].shape[0]
    total = count * len(parts)
    return sum(jnp.pad(p, ((at * count, total - (at + 1) * count), (0, 0))) for at, p in enumerate(parts))


def doubled(rows, steps):
    for axis, bit in steps:
        rows = stacked_rows([rows, swapped(rows, axis, bit)])
    return rows


def block_of(other):
    return sum(1 << at for at, (axis, bit) in enumerate(steps_of()) if axis == "sy" and other & bit)


def split(x):
    high = x.astype(BF16)
    return high, (x - high.astype(F32)).astype(BF16)


def dot(a, b):
    return jnp.dot(a, b, preferred_element_type=F32)


def product(a, b_high, b_low):
    a_high, a_low = split(a)
    return dot(a_high, b_high) + (dot(a_high, b_low) + dot(a_low, b_high))


def thirds(x):
    high = x.astype(BF16)
    rest = x - high.astype(F32)
    mid = rest.astype(BF16)
    return high, mid, (rest - mid.astype(F32)).astype(BF16)


def permuted(select, rows):
    high, mid, low = thirds(rows)
    return dot(select, high) + (dot(select, mid) + dot(select, low))


def pair(flag, first, second):
    return jnp.where(flag == 1.0, second, first), jnp.where(flag == 1.0, first, second)


def faces_of(flags, slots):
    return (*pair(flags[4], slots[0], slots[1]), *pair(flags[5], slots[2], slots[3]))


def pack_kernel(corners, load, coupling, *refs):
    outs, sems = refs[:4], refs[4]
    face = load.shape[0] // 4
    width = load.shape[1]
    ncl = coupling.shape[0]
    even = [1 - lax.axis_index("sx") % 2, 1 - lax.axis_index("sy") % 2]
    faces = [even[0], 1 - even[0], 2 + even[1], 3 - even[1]]
    copies = []

    def copy(source, target):
        copies.append(pltpu.make_async_copy(source, target, sems.at[len(copies)]))
        copies[-1].start()

    for slot in (3, 2, 0, 1):
        first = pl.multiple_of(faces[slot] * face, 128)
        out = outs[slot]
        copy(load.at[pl.ds(first, face)], out.at[pl.ds(0, face)])
        for block, at in enumerate(range(0, face, width)):
            wide = min(width, face - at)
            source = coupling.at[:, pl.ds(pl.multiple_of(first + at, 128), wide)]
            copy(source, out.at[pl.ds(face + block * ncl, ncl), pl.ds(0, wide)])
    start = face + (face // width) * ncl
    for out in outs:
        for k in range(ncl):
            listed = jnp.full((1, width - face % width), corners[k].astype(F32))
            out[start + k : start + k + 1, face % width :] = listed
        if out.shape[0] > start + ncl:
            out[start + ncl :] = jnp.zeros((out.shape[0] - start - ncl, width), F32)
    for started in copies:
        started.wait()


def rows_kernel(corners, inverse, out):
    own = inverse.shape[0]
    out[:own] = inverse[...]
    out[own:] = jnp.zeros((out.shape[0] - own, out.shape[1]), F32)
    columns = lax.broadcasted_iota(jnp.int32, (1, out.shape[1]), 1)
    listed = jnp.zeros((1, out.shape[1]), F32)
    for k in range(corners.shape[0]):
        listed = jnp.where(columns == k, corners[k].astype(F32), listed)
    out[own : own + 1] = listed


def lift_kernel(flags, near0, near1, near2, near3, select, coupling, sent, out):
    face = out.shape[0] // 4
    ncoarse = out.shape[1]
    ncl = coupling.shape[0]
    ids = lax.broadcasted_iota(jnp.int32, (ncl, ncoarse), 1).astype(F32)
    own_pick = (sent[sent.shape[0] - ncl :, sent.shape[1] - 1 :] == ids).astype(F32)
    end = near0.shape[0]
    nears = faces_of(flags, [near[face:end] for near in (near0, near1, near2, near3)])
    for f, near in enumerate(nears):
        columns = jnp.concatenate([near[at : at + ncl] for at in range(0, near.shape[0], ncl)], axis=1)
        near_pick = (columns[:, columns.shape[1] - 1 :] == ids).astype(F32)
        own = jnp.dot(coupling[:, f * face : (f + 1) * face].T, own_pick, precision=HIGHEST)
        theirs = jnp.dot(columns[:, :face].T, near_pick, precision=HIGHEST)
        out[f * face : (f + 1) * face] = own - permuted(select[f], theirs)


def field_into(at, owns, nears, select, flags, coef, bases, lifts, outs, images, high, low):
    size = outs[0].shape[0]
    if lifts:
        lift, sol = lifts
        corrections = product(lift[at * size : (at + 2) * size], *split(sol[...]))
    owns = pair(flags[4 + at // 2], *(own[:size] for own in owns))
    nears = pair(flags[4 + at // 2], *(near[:size] for near in nears))
    for f in range(2):
        image = owns[f] - permuted(select[at + f], nears[f])
        rows = slice(f * size, (f + 1) * size)
        if lifts:
            image = image + corrections[rows]
        if images:
            images[f][...] = image
        value = coef[0:1] * image
        if bases:
            value = bases[f][...] + value
        outs[f][...] = value
        high[rows], low[rows] = split(flags[at + f] * value)


def take(refs, *counts):
    groups = []
    for count in counts:
        groups.append(refs[:count])
        refs = refs[count:]
    return (*groups, refs)


def early_kernel(based, lifted, *refs):
    (flags, mat), owns, nears, (select, coef), bases, lifts, outs, images, rest = take(
        refs, 2, 2, 2, 2, 2 * based, 2 * lifted, 2, 2 * lifted
    )
    partial, high, low = rest
    field_into(0, owns, nears, select, flags, coef, bases, lifts, outs, images, high, low)
    half = high.shape[0]
    for rows in (slice(0, half), slice(half, 2 * half)):
        partial[rows] = product(mat[rows, :half], high[...], low[...])


def crit_kernel(based, lifted, *refs):
    (flags, mat), owns, nears, (select, coef, partial), bases, lifts, outs, images, rest = take(
        refs, 2, 2, 2, 3, 2 * based, 2 * lifted, 2, 2 * lifted
    )
    slot2, slot3, high, low = rest
    field_into(2, owns, nears, select, flags, coef, bases, lifts, outs, images, high, low)
    half = high.shape[0]
    size = half // 2
    value = partial[half:] + product(mat[half:, half:], high[...], low[...])
    slot3[:size], slot2[:size] = pair(flags[5], value[size:], value[:size])
    for slot in (slot2, slot3):
        slot[size:] = jnp.zeros((slot.shape[0] - size, slot.shape[1]), F32)


def late_rows(flags, mat, values, partial, high, low, slots):
    size = values[0].shape[0]
    for f in (2, 3):
        rows = slice((f - 2) * size, (f - 1) * size)
        high[rows], low[rows] = split(flags[f] * values[f][...])
    value = partial[: 2 * size] + product(mat[: 2 * size, 2 * size :], high[...], low[...])
    slots[1][...], slots[0][...] = pair(flags[4], value[size:], value[:size])
    return faces_of(flags, [slot[:size] for slot in slots])


def inner(flags, values, others):
    return sum(jnp.sum(flags[f] * values[f][...] * others[f], axis=0, keepdims=True) for f in range(4))


def prec_late_kernel(*refs):
    (flags, mat), values, applied, (partial, slot0, slot1, dots, high, low) = take(refs, 2, 4, 2)
    dots[...] = inner(flags, values, late_rows(flags, mat, values, partial, high, low, (slot0, slot1, *applied)))


def flex_late_kernel(others, *refs):
    (flags, mat), values, applied, other, rest = take(refs, 2, 4, 2, 4 * others)
    partial, coupling, carried, slot0, slot1, sums, high, low = rest
    size = slot0.shape[0]
    ncl = coupling.shape[0]
    coarse = None
    for f in range(4):
        term = product(coupling[:, f * size : (f + 1) * size], *split(flags[f] * values[f][...]))
        coarse = term if coarse is None else coarse + term
    faces = late_rows(flags, mat, values, partial, high, low, (slot0, slot1, *applied))
    rows = [inner(flags, values, faces), carried[...]]
    if others:
        rows.append(inner(flags, values, faces_of(flags, [slot[:size] for slot in other])))
    sums[:ncl] = coarse
    for at, row in enumerate(rows):
        sums[ncl + at : ncl + at + 1] = row
    end = ncl + len(rows)
    sums[end:] = jnp.zeros((sums.shape[0] - end, sums.shape[1]), F32)


def spread_kernel(ncl, rows, origins, table, *refs):
    parts, out = refs[:-1], refs[-1]
    ncoarse = out.shape[0] - 8
    ids = lax.broadcasted_iota(jnp.int32, (ncoarse, ncl), 0).astype(F32)
    size = ncl + 8
    each = parts[0].shape[0] // size
    coarse, dots = None, None
    for at, origin in enumerate(origins):
        start = origin * rows + rows - 8
        pick = (ids == table[start : start + 1, :ncl]).astype(BF16)
        values = parts[at // each][at % each * size : (at % each + 1) * size]
        term = permuted(pick, values[:ncl])
        coarse = term if coarse is None else coarse + term
        dots = values[ncl:] if dots is None else dots + values[ncl:]
    out[:ncoarse] = coarse
    out[ncoarse:] = dots


def inverse_from(table, rows, matrix):
    own = rows - 8
    for at in range(table.shape[0] // rows):
        matrix[at * own : (at + 1) * own] = table[at * rows : at * rows + own]


def first_step_kernel(rows, total, table, order, out, matrix):
    ncoarse = matrix.shape[0]
    inverse_from(table, rows, matrix)
    rhs = total[:ncoarse]
    sol = permuted(order[...], jnp.dot(matrix[...], rhs, precision=HIGHEST))
    fine_dot = total[ncoarse : ncoarse + 1]
    rho = 0.5 * total[ncoarse + 1 : ncoarse + 2]
    curve = fine_dot + jnp.sum(rhs * sol, axis=0, keepdims=True)
    out[:ncoarse] = sol
    out[ncoarse : ncoarse + 1] = -rho / curve
    out[ncoarse + 1 : ncoarse + 2] = rho
    out[ncoarse + 2 : ncoarse + 3] = fine_dot
    out[ncoarse + 3 :] = jnp.zeros((out.shape[0] - ncoarse - 3, out.shape[1]), F32)


def second_step_kernel(rows, total, table, order, total0, out0, out, matrix):
    ncoarse = matrix.shape[0]
    inverse_from(table, rows, matrix)
    rhs = total[:ncoarse]
    sol = permuted(order[...], jnp.dot(matrix[...], rhs, precision=HIGHEST))
    dot11, rho1, dot10 = (total[ncoarse + row : ncoarse + row + 1] for row in range(3))
    minus_step0, rho0, dot00 = (out0[ncoarse + row : ncoarse + row + 1] for row in range(3))
    rho1 = 0.5 * rho1
    beta = rho1 / rho0
    coarse = jnp.sum((rhs + beta * total0[:ncoarse]) * (sol + beta * out0[:ncoarse]), axis=0, keepdims=True)
    step1 = rho1 / (dot11 + 2.0 * beta * dot10 + beta * beta * dot00 + coarse)
    out[:ncoarse] = sol
    out[ncoarse : ncoarse + 1] = -step1
    out[ncoarse + 1 : ncoarse + 2] = -step1 * beta
    out[ncoarse + 2 : ncoarse + 3] = step1 * beta - minus_step0
    out[ncoarse + 3 : ncoarse + 4] = step1
    out[ncoarse + 4 :] = jnp.zeros((out.shape[0] - ncoarse - 4, out.shape[1]), F32)


def stored(values, out, sems):
    size = values.shape[1]
    return [
        pltpu.make_async_copy(values.at[f], out.at[pl.ds(f * size, size)], sems.at[f]) for f in range(4)
    ]


def tail_kernel(*refs):
    (flags,), owns, nears, residuals, images, (select, lift, sol, steps, out, values, sems) = take(
        refs, 1, 4, 4, 4, 4
    )
    stores = stored(values, out, sems)
    parts = split(sol[...])
    size = values.shape[1]
    owns = faces_of(flags, [own[:size] for own in owns])
    nears = faces_of(flags, [near[:size] for near in nears])
    for f in range(4):
        image = owns[f] - permuted(select[f], nears[f]) + product(lift[f * size : (f + 1) * size], *parts)
        values[f] = residuals[f][...] + steps[0:1] * image + steps[1:2] * images[f][...]
        stores[f].start()
    for copy in stores:
        copy.wait()


def weighted_kernel(*refs):
    firsts, seconds, (steps, out, values, sems) = take(refs, 4, 4)
    stores = stored(values, out, sems)
    for f in range(4):
        values[f] = steps[2:3] * firsts[f][...] + steps[3:4] * seconds[f][...]
        stores[f].start()
    for copy in stores:
        copy.wait()


VMEM_SPEC = pl.BlockSpec(memory_space=pltpu.VMEM)
SMEM_SPEC = pl.BlockSpec(memory_space=pltpu.SMEM)
ANY_SPEC = pl.BlockSpec(memory_space=pl.ANY)


def call(kernel, operands, shapes, scratch=(), smem=0, anywhere=(), out_spec=VMEM_SPEC, flops=1024, limit=LIMIT):
    return pl.pallas_call(
        kernel,
        in_specs=[SMEM_SPEC if i < smem else ANY_SPEC if i in anywhere else VMEM_SPEC for i in range(len(operands))],
        out_specs=[out_spec] * len(shapes),
        out_shape=[jax.ShapeDtypeStruct(s, F32) for s in shapes],
        scratch_shapes=list(scratch),
        compiler_params=pltpu.CompilerParams(vmem_limit_bytes=limit),
        cost_estimate=pl.CostEstimate(flops=flops, bytes_accessed=1024, transcendentals=0),
    )(*operands)


def shards(loads, schur_flex, dirichlet, coupling, corner_index, face_lists, coarse_inverse):
    flex_mat = schur_flex[0, 0]
    prec_mat = dirichlet[0, 0]
    coupling_mat = coupling[0, 0]
    corners = corner_index[0, 0]
    face_index = face_lists[0, 0]
    load = loads[0, 0]
    ncoarse = coarse_inverse.shape[1]
    ncl, ni = coupling_mat.shape
    width = load.shape[1]
    face, half = ni // 4, ni // 2
    n_sx, n_sy = lax.axis_size("sx"), lax.axis_size("sy")
    at_x, at_y = lax.axis_index("sx"), lax.axis_index("sy")
    count = n_sx * n_sy

    has = jnp.stack([at_x > 0, at_x < n_sx - 1, at_y > 0, at_y < n_sy - 1])
    even = jnp.stack([at_x, at_y]) % 2 == 0
    flags = jnp.concatenate([jnp.where(has, 2.0, 1.0), jnp.where(even, 1.0, 0.0)]).astype(F32)
    select = (face_index[:, :, None] == jnp.arange(face, dtype=jnp.int32)).astype(BF16)
    coarse_ids = jnp.arange(ncoarse, dtype=jnp.int32)
    block = coarse_ids // (ncoarse // (n_sx * n_sy))
    origin = jnp.zeros_like(block)
    for at, (axis, bit) in enumerate(steps_of()):
        weight = bit * n_sy if axis == "sx" else bit
        origin = origin + ((block >> at) & 1) * weight
    origin = origin ^ (at_x * n_sy + at_y)
    within = coarse_ids % (ncoarse // (n_sx * n_sy))
    order = (origin * (ncoarse // (n_sx * n_sy)) + within)[None, :] == coarse_ids[:, None]
    order = order.astype(BF16)
    one_face, far_face = (face, width), (face + FAR_ROWS, width)
    parts = [pltpu.VMEM((half, width), BF16)] * 2
    one, select, order, flags = lax.optimization_barrier((jnp.ones((1, width), F32), select, order, flags))
    half_one = jnp.full((1, width), 0.5, F32)

    def early(matrix, owns, nears, coef, bases, lifts):
        operands = [flags, matrix, *owns, *nears, select, coef, *bases, *lifts]
        shapes = [one_face] * (4 if lifts else 2) + [(ni, width)]
        kernel = functools.partial(early_kernel, bool(bases), bool(lifts))
        *fields, partial = call(kernel, operands, shapes, parts, smem=1)
        return fields[:2], fields[2:], partial

    def crit(matrix, owns, nears, coef, partial, bases, lifts):
        operands = [flags, matrix, *owns, *nears, select, coef, partial, *bases, *lifts]
        shapes = [one_face] * (4 if lifts else 2) + [far_face] * 2
        kernel = functools.partial(crit_kernel, bool(bases), bool(lifts))
        *fields, a2, a3 = call(kernel, operands, shapes, parts, smem=1, flops=CRIT_FLOPS)
        return fields[:2], fields[2:], (a2, a3)

    def fields_of(matrix, owns, nears, coef, bases=(), lifts=(), beside=None):
        v01, q01, partial = early(matrix, owns[:2], nears[:2], coef, bases[:2], lifts)
        if beside is not None:
            partial, coef, made = beside(partial, coef)
        v23, q23, a23 = crit(matrix, owns[2:], nears[2:], coef, partial, bases[2:], lifts)
        fields = (*v01, *v23), (*q01, *q23), a23, partial
        return fields if beside is None else (*fields, made)

    def prec_late(values, a23, partial):
        operands = [flags, prec_mat, *values, *a23, partial]
        a0, a1, dots = call(prec_late_kernel, operands, [one_face, one_face, (1, width)], parts, smem=1)
        return (a0, a1, *a23), dots

    def flex_late(values, a23, partial, carried, other=()):
        operands = [flags, flex_mat, *values, *a23, *other, partial, coupling_mat, carried]
        kernel = functools.partial(flex_late_kernel, int(bool(other)))
        a0, a1, sums = call(kernel, operands, [one_face, one_face, (ncl + 8, width)], parts, smem=1)
        return (a0, a1, *a23), sums

    def solved(kernel, sums, faces, more):
        other, *far = lax.optimization_barrier((swapped(sums, "sy", 1), *faces[2:]))
        far = exchanged(far, "sy")
        close = faces[:2]
        parts, origins = [sums, other], [0, 1]
        for bit in bits_of("sy")[:0:-1]:
            rows = stacked_rows(parts)
            other, *close = lax.optimization_barrier((swapped(rows, "sy", bit), *close))
            parts = [rows, other]
            origins = origins + [at ^ bit for at in origins]
        origins = [block_of(at) for at in origins]
        spread = functools.partial(spread_kernel, ncl, table_rows, origins)
        (total,) = call(spread, [table, *parts], [step_shape])
        for bit in bits_of("sx"):
            total = total + swapped(total, "sx", bit)
        scratch = [pltpu.VMEM((ncoarse, ncoarse), F32)]
        kernel = functools.partial(kernel, table_rows)
        (result,) = call(kernel, [total, table, order, *more], [step_shape], scratch)
        return (*exchanged(close, "sx"), *far), total, result

    step_shape = (ncoarse + 8, width)
    extra = -(-face // width) * ncl
    copies = 4 * (1 + -(-face // width))
    sent = call(
        pack_kernel,
        [corners, load, coupling_mat],
        [(face + extra, width)] * 2 + [(face + extra + FAR_ROWS, width)] * 2,
        [pltpu.SemaphoreType.DMA((copies,))],
        smem=1,
        anywhere=(1, 2),
        limit=7 * LIMIT,
    )
    near = (*exchanged(sent[:2], "sx"), *exchanged(sent[2:], "sy"))

    own = coarse_inverse.shape[0]
    table_rows = own + 8
    inverse, flags, order, _ = lax.optimization_barrier((coarse_inverse, flags, order, sent[0]))
    (own_rows,) = call(rows_kernel, [corners, inverse], [(table_rows, ncoarse)], smem=1, flops=CRIT_FLOPS)

    def gather(partial, coef):
        rows, coef = lax.optimization_barrier((doubled(own_rows, steps_of()[:-1]), coef))
        return partial, coef, rows

    residual0, _, a23, partial, rows = fields_of(prec_mat, sent, near, one, beside=gather)
    applied0, rho0 = prec_late(residual0, a23, partial)
    (lift,) = call(
        lift_kernel, [flags, *near, select, coupling_mat, sent[0]], [(ni, ncoarse)], smem=1
    )
    table, half_one = lax.optimization_barrier((doubled(rows, steps_of()[-1:]), half_one))
    near = (*exchanged(applied0[:2], "sx"), *exchanged(applied0[2:], "sy"))

    direction0, _, a23, partial = fields_of(flex_mat, applied0, near, half_one)
    fine0, sums = flex_late(direction0, a23, partial, rho0)
    near, total0, result0 = solved(first_step_kernel, sums, fine0, [])
    lifts = (lift, result0[:ncoarse])
    residual1, image0, a23, partial = fields_of(prec_mat, fine0, near, result0[ncoarse:], residual0, lifts)
    applied1, rho1 = prec_late(residual1, a23, partial)
    near = (*exchanged(applied1[:2], "sx"), *exchanged(applied1[2:], "sy"))

    precond, _, a23, partial = fields_of(flex_mat, applied1, near, half_one)
    fine1, sums = flex_late(precond, a23, partial, rho1, fine0)
    near, _, result1 = solved(second_step_kernel, sums, fine1, [total0, result0])
    sol1, steps1 = result1[:ncoarse], result1[ncoarse:]

    def final(kernel, operands, smem=0):
        ends = [pltpu.VMEM((4, face, width), F32), pltpu.SemaphoreType.DMA((4,))]
        return call(kernel, operands, [(ni, width)], ends, smem=smem, out_spec=ANY_SPEC)[0]

    multipliers = final(weighted_kernel, [*direction0, *precond, steps1])
    operands = [flags, *fine1, *near, *residual1, *image0, select, lift, sol1, steps1]
    residual2 = final(tail_kernel, operands, smem=1)
    return multipliers[None, None], residual2[None, None]


def solution(mesh):
    return jax.shard_map(
        shards,
        mesh=mesh,
        in_specs=(
            P("sx", "sy", None, None),
            P("sx", "sy", None, None),
            P("sx", "sy", None, None),
            P("sx", "sy", None, None),
            P("sx", "sy", None),
            P("sx", "sy", None, None),
            P(("sx", "sy"), None),
        ),
        out_specs=(P("sx", "sy", None, None), P("sx", "sy", None, None)),
        check_vma=False,
    )
```

```python
import functools

import jax
import jax.numpy as jnp
from jax import lax
from jax.experimental import pallas as pl
from jax.experimental.pallas import tpu as pltpu
from jax.sharding import PartitionSpec as P

HIGHEST = lax.Precision.HIGHEST
F32 = jnp.float32
BF16 = jnp.bfloat16
LIMIT = 8 * 1024 * 1024
CRIT_FLOPS = 8 * 10**9
FAR_ROWS = 8


def swapped(block, axis, bit):
    return lax.ppermute(block, axis, [(i, i ^ bit) for i in range(lax.axis_size(axis))])


def swapped_between(block, axis):
    route = []
    for i in range(1, lax.axis_size(axis) - 1, 2):
        route += [(i, i + 1), (i + 1, i)]
    return lax.ppermute(block, axis, route)


def exchanged(slots, axis):
    between = swapped_between(slots[1], axis)
    return swapped(slots[0], axis, 1), between


def bits_of(axis):
    return [1 << i for i in range((lax.axis_size(axis) - 1).bit_length())]


def steps_of():
    return [("sy", 1)] + [("sx", bit) for bit in bits_of("sx")[::-1]] + [("sy", bit) for bit in bits_of("sy")[:0:-1]]


def stacked_rows(parts):
    count = parts[0].shape[0]
    total = count * len(parts)
    return sum(jnp.pad(p, ((at * count, total - (at + 1) * count), (0, 0))) for at, p in enumerate(parts))


def doubled(rows, steps):
    for axis, bit in steps:
        rows = stacked_rows([rows, swapped(rows, axis, bit)])
    return rows


def block_of(other):
    return sum(1 << at for at, (axis, bit) in enumerate(steps_of()) if axis == "sy" and other & bit)


def split(x):
    high = x.astype(BF16)
    return high, (x - high.astype(F32)).astype(BF16)


def dot(a, b):
    return jnp.dot(a, b, preferred_element_type=F32)


def product(a, b_high, b_low):
    a_high, a_low = split(a)
    return dot(a_high, b_high) + (dot(a_high, b_low) + dot(a_low, b_high))


def thirds(x):
    high = x.astype(BF16)
    rest = x - high.astype(F32)
    mid = rest.astype(BF16)
    return high, mid, (rest - mid.astype(F32)).astype(BF16)


def permuted(select, rows):
    high, mid, low = thirds(rows)
    return dot(select, high) + (dot(select, mid) + dot(select, low))


def pair(flag, first, second):
    return jnp.where(flag == 1.0, second, first), jnp.where(flag == 1.0, first, second)


def faces_of(flags, slots):
    return (*pair(flags[4], slots[0], slots[1]), *pair(flags[5], slots[2], slots[3]))


def pack_kernel(corners, load, coupling, *refs):
    outs, sems = refs[:4], refs[4]
    face = load.shape[0] // 4
    width = load.shape[1]
    ncl = coupling.shape[0]
    even = [1 - lax.axis_index("sx") % 2, 1 - lax.axis_index("sy") % 2]
    faces = [even[0], 1 - even[0], 2 + even[1], 3 - even[1]]
    copies = []

    def copy(source, target):
        copies.append(pltpu.make_async_copy(source, target, sems.at[len(copies)]))
        copies[-1].start()

    for slot in (3, 2, 0, 1):
        first = pl.multiple_of(faces[slot] * face, 128)
        out = outs[slot]
        copy(load.at[pl.ds(first, face)], out.at[pl.ds(0, face)])
        for block, at in enumerate(range(0, face, width)):
            wide = min(width, face - at)
            source = coupling.at[:, pl.ds(pl.multiple_of(first + at, 128), wide)]
            copy(source, out.at[pl.ds(face + block * ncl, ncl), pl.ds(0, wide)])
    start = face + (face // width) * ncl
    for out in outs:
        for k in range(ncl):
            listed = jnp.full((1, width - face % width), corners[k].astype(F32))
            out[start + k : start + k + 1, face % width :] = listed
        if out.shape[0] > start + ncl:
            out[start + ncl :] = jnp.zeros((out.shape[0] - start - ncl, width), F32)
    for started in copies:
        started.wait()


def rows_kernel(corners, inverse, out):
    own = inverse.shape[0]
    out[:own] = inverse[...]
    out[own:] = jnp.zeros((out.shape[0] - own, out.shape[1]), F32)
    columns = lax.broadcasted_iota(jnp.int32, (1, out.shape[1]), 1)
    listed = jnp.zeros((1, out.shape[1]), F32)
    for k in range(corners.shape[0]):
        listed = jnp.where(columns == k, corners[k].astype(F32), listed)
    out[own : own + 1] = listed


def lift_kernel(flags, near0, near1, near2, near3, select, coupling, sent, out):
    face = out.shape[0] // 4
    ncoarse = out.shape[1]
    ncl = coupling.shape[0]
    ids = lax.broadcasted_iota(jnp.int32, (ncl, ncoarse), 1).astype(F32)
    own_pick = (sent[sent.shape[0] - ncl :, sent.shape[1] - 1 :] == ids).astype(F32)
    end = near0.shape[0]
    nears = faces_of(flags, [near[face:end] for near in (near0, near1, near2, near3)])
    for f, near in enumerate(nears):
        columns = jnp.concatenate([near[at : at + ncl] for at in range(0, near.shape[0], ncl)], axis=1)
        near_pick = (columns[:, columns.shape[1] - 1 :] == ids).astype(F32)
        own = jnp.dot(coupling[:, f * face : (f + 1) * face].T, own_pick, precision=HIGHEST)
        theirs = jnp.dot(columns[:, :face].T, near_pick, precision=HIGHEST)
        out[f * face : (f + 1) * face] = own - permuted(select[f], theirs)


def field_into(at, owns, nears, select, flags, coef, bases, lifts, outs, images, high, low):
    size = outs[0].shape[0]
    if lifts:
        lift, sol = lifts
        corrections = product(lift[at * size : (at + 2) * size], *split(sol[...]))
    owns = pair(flags[4 + at // 2], *(own[:size] for own in owns))
    nears = pair(flags[4 + at // 2], *(near[:size] for near in nears))
    for f in range(2):
        image = owns[f] - permuted(select[at + f], nears[f])
        rows = slice(f * size, (f + 1) * size)
        if lifts:
            image = image + corrections[rows]
        if images:
            images[f][...] = image
        value = coef[0:1] * image
        if bases:
            value = bases[f][...] + value
        outs[f][...] = value
        high[rows], low[rows] = split(flags[at + f] * value)


def take(refs, *counts):
    groups = []
    for count in counts:
        groups.append(refs[:count])
        refs = refs[count:]
    return (*groups, refs)


def early_kernel(based, lifted, *refs):
    (flags, mat), owns, nears, (select, coef), bases, lifts, outs, images, rest = take(
        refs, 2, 2, 2, 2, 2 * based, 2 * lifted, 2, 2 * lifted
    )
    partial, high, low = rest
    field_into(0, owns, nears, select, flags, coef, bases, lifts, outs, images, high, low)
    half = high.shape[0]
    for rows in (slice(0, half), slice(half, 2 * half)):
        partial[rows] = product(mat[rows, :half], high[...], low[...])


def crit_kernel(based, lifted, *refs):
    (flags, mat), owns, nears, (select, coef, partial), bases, lifts, outs, images, rest = take(
        refs, 2, 2, 2, 3, 2 * based, 2 * lifted, 2, 2 * lifted
    )
    slot2, slot3, high, low = rest
    field_into(2, owns, nears, select, flags, coef, bases, lifts, outs, images, high, low)
    half = high.shape[0]
    size = half // 2
    value = partial[half:] + product(mat[half:, half:], high[...], low[...])
    slot3[:size], slot2[:size] = pair(flags[5], value[size:], value[:size])
    for slot in (slot2, slot3):
        slot[size:] = jnp.zeros((slot.shape[0] - size, slot.shape[1]), F32)


def late_rows(flags, mat, values, partial, high, low, slots):
    size = values[0].shape[0]
    for f in (2, 3):
        rows = slice((f - 2) * size, (f - 1) * size)
        high[rows], low[rows] = split(flags[f] * values[f][...])
    value = partial[: 2 * size] + product(mat[: 2 * size, 2 * size :], high[...], low[...])
    slots[1][:size], slots[0][...] = pair(flags[4], value[size:], value[:size])
    rest = slots[1].shape[0] - size
    if rest:
        slots[1][size:] = jnp.zeros((rest, slots[1].shape[1]), F32)
    return faces_of(flags, [slot[:size] for slot in slots])


def inner(flags, values, others):
    return sum(jnp.sum(flags[f] * values[f][...] * others[f], axis=0, keepdims=True) for f in range(4))


def prec_late_kernel(*refs):
    (flags, mat), values, applied, (partial, slot0, slot1, dots, high, low) = take(refs, 2, 4, 2)
    dots[...] = inner(flags, values, late_rows(flags, mat, values, partial, high, low, (slot0, slot1, *applied)))


def flex_late_kernel(others, *refs):
    (flags, mat), values, applied, other, rest = take(refs, 2, 4, 2, 4 * others)
    partial, coupling, carried, slot0, slot1, sums, high, low = rest
    size = slot0.shape[0]
    ncl = coupling.shape[0]
    coarse = None
    for f in range(4):
        term = product(coupling[:, f * size : (f + 1) * size], *split(flags[f] * values[f][...]))
        coarse = term if coarse is None else coarse + term
    faces = late_rows(flags, mat, values, partial, high, low, (slot0, slot1, *applied))
    rows = [inner(flags, values, faces), carried[...]]
    if others:
        rows.append(inner(flags, values, faces_of(flags, [slot[:size] for slot in other])))
    sums[:ncl] = coarse
    for at, row in enumerate(rows):
        sums[ncl + at : ncl + at + 1] = row
    end = ncl + len(rows)
    sums[end:] = jnp.zeros((sums.shape[0] - end, sums.shape[1]), F32)


def spread_kernel(ncl, rows, origins, table, *refs):
    parts, out = refs[:-1], refs[-1]
    ncoarse = out.shape[0] - 8
    ids = lax.broadcasted_iota(jnp.int32, (ncoarse, ncl), 0).astype(F32)
    size = ncl + 8
    each = parts[0].shape[0] // size
    coarse, dots = None, None
    for at, origin in enumerate(origins):
        start = origin * rows + rows - 8
        pick = (ids == table[start : start + 1, :ncl]).astype(BF16)
        values = parts[at // each][at % each * size : (at % each + 1) * size]
        term = permuted(pick, values[:ncl])
        coarse = term if coarse is None else coarse + term
        dots = values[ncl:] if dots is None else dots + values[ncl:]
    out[:ncoarse] = coarse
    out[ncoarse:] = dots


def inverse_from(table, rows, matrix):
    own = rows - 8
    for at in range(table.shape[0] // rows):
        matrix[at * own : (at + 1) * own] = table[at * rows : at * rows + own]


def first_step_kernel(rows, total, table, order, out, matrix):
    ncoarse = matrix.shape[0]
    inverse_from(table, rows, matrix)
    rhs = total[:ncoarse]
    sol = permuted(order[...], jnp.dot(matrix[...], rhs, precision=HIGHEST))
    fine_dot = total[ncoarse : ncoarse + 1]
    rho = 0.5 * total[ncoarse + 1 : ncoarse + 2]
    curve = fine_dot + jnp.sum(rhs * sol, axis=0, keepdims=True)
    out[:ncoarse] = sol
    out[ncoarse : ncoarse + 1] = -rho / curve
    out[ncoarse + 1 : ncoarse + 2] = rho
    out[ncoarse + 2 : ncoarse + 3] = fine_dot
    out[ncoarse + 3 :] = jnp.zeros((out.shape[0] - ncoarse - 3, out.shape[1]), F32)


def second_step_kernel(rows, total, table, order, total0, out0, out, matrix):
    ncoarse = matrix.shape[0]
    inverse_from(table, rows, matrix)
    rhs = total[:ncoarse]
    sol = permuted(order[...], jnp.dot(matrix[...], rhs, precision=HIGHEST))
    dot11, rho1, dot10 = (total[ncoarse + row : ncoarse + row + 1] for row in range(3))
    minus_step0, rho0, dot00 = (out0[ncoarse + row : ncoarse + row + 1] for row in range(3))
    rho1 = 0.5 * rho1
    beta = rho1 / rho0
    coarse = jnp.sum((rhs + beta * total0[:ncoarse]) * (sol + beta * out0[:ncoarse]), axis=0, keepdims=True)
    step1 = rho1 / (dot11 + 2.0 * beta * dot10 + beta * beta * dot00 + coarse)
    out[:ncoarse] = sol
    out[ncoarse : ncoarse + 1] = -step1
    out[ncoarse + 1 : ncoarse + 2] = -step1 * beta
    out[ncoarse + 2 : ncoarse + 3] = step1 * beta - minus_step0
    out[ncoarse + 3 : ncoarse + 4] = step1
    out[ncoarse + 4 :] = jnp.zeros((out.shape[0] - ncoarse - 4, out.shape[1]), F32)


def stored(values, out, sems):
    size = values.shape[1]
    return [
        pltpu.make_async_copy(values.at[f], out.at[pl.ds(f * size, size)], sems.at[f]) for f in range(4)
    ]


def tail_kernel(*refs):
    (flags,), owns, nears, residuals, images, (select, lift, sol, steps, out, values, sems) = take(
        refs, 1, 4, 4, 4, 4
    )
    stores = stored(values, out, sems)
    parts = split(sol[...])
    size = values.shape[1]
    owns = faces_of(flags, [own[:size] for own in owns])
    nears = faces_of(flags, [near[:size] for near in nears])
    for f in range(4):
        image = owns[f] - permuted(select[f], nears[f]) + product(lift[f * size : (f + 1) * size], *parts)
        values[f] = residuals[f][...] + steps[0:1] * image + steps[1:2] * images[f][...]
        stores[f].start()
    for copy in stores:
        copy.wait()


def weighted_kernel(*refs):
    firsts, seconds, (steps, out, values, sems) = take(refs, 4, 4)
    stores = stored(values, out, sems)
    for f in range(4):
        values[f] = steps[2:3] * firsts[f][...] + steps[3:4] * seconds[f][...]
        stores[f].start()
    for copy in stores:
        copy.wait()


VMEM_SPEC = pl.BlockSpec(memory_space=pltpu.VMEM)
SMEM_SPEC = pl.BlockSpec(memory_space=pltpu.SMEM)
ANY_SPEC = pl.BlockSpec(memory_space=pl.ANY)


def call(kernel, operands, shapes, scratch=(), smem=0, anywhere=(), out_spec=VMEM_SPEC, flops=1024, limit=LIMIT):
    return pl.pallas_call(
        kernel,
        in_specs=[SMEM_SPEC if i < smem else ANY_SPEC if i in anywhere else VMEM_SPEC for i in range(len(operands))],
        out_specs=[out_spec] * len(shapes),
        out_shape=[jax.ShapeDtypeStruct(s, F32) for s in shapes],
        scratch_shapes=list(scratch),
        compiler_params=pltpu.CompilerParams(vmem_limit_bytes=limit),
        cost_estimate=pl.CostEstimate(flops=flops, bytes_accessed=1024, transcendentals=0),
    )(*operands)


def shards(loads, schur_flex, dirichlet, coupling, corner_index, face_lists, coarse_inverse):
    flex_mat = schur_flex[0, 0]
    prec_mat = dirichlet[0, 0]
    coupling_mat = coupling[0, 0]
    corners = corner_index[0, 0]
    face_index = face_lists[0, 0]
    load = loads[0, 0]
    ncoarse = coarse_inverse.shape[1]
    ncl, ni = coupling_mat.shape
    width = load.shape[1]
    face, half = ni // 4, ni // 2
    n_sx, n_sy = lax.axis_size("sx"), lax.axis_size("sy")
    at_x, at_y = lax.axis_index("sx"), lax.axis_index("sy")
    count = n_sx * n_sy

    has = jnp.stack([at_x > 0, at_x < n_sx - 1, at_y > 0, at_y < n_sy - 1])
    even = jnp.stack([at_x, at_y]) % 2 == 0
    flags = jnp.concatenate([jnp.where(has, 2.0, 1.0), jnp.where(even, 1.0, 0.0)]).astype(F32)
    select = (face_index[:, :, None] == jnp.arange(face, dtype=jnp.int32)).astype(BF16)
    coarse_ids = jnp.arange(ncoarse, dtype=jnp.int32)
    block = coarse_ids // (ncoarse // (n_sx * n_sy))
    origin = jnp.zeros_like(block)
    for at, (axis, bit) in enumerate(steps_of()):
        weight = bit * n_sy if axis == "sx" else bit
        origin = origin + ((block >> at) & 1) * weight
    origin = origin ^ (at_x * n_sy + at_y)
    within = coarse_ids % (ncoarse // (n_sx * n_sy))
    order = (origin * (ncoarse // (n_sx * n_sy)) + within)[None, :] == coarse_ids[:, None]
    order = order.astype(BF16)
    one_face = (face, width)
    parts = [pltpu.VMEM((half, width), BF16)] * 2
    one, select, order, flags = lax.optimization_barrier((jnp.ones((1, width), F32), select, order, flags))
    half_one = jnp.full((1, width), 0.5, F32)

    def early(matrix, owns, nears, coef, bases, lifts):
        operands = [flags, matrix, *owns, *nears, select, coef, *bases, *lifts]
        shapes = [one_face] * (4 if lifts else 2) + [(ni, width)]
        kernel = functools.partial(early_kernel, bool(bases), bool(lifts))
        *fields, partial = call(kernel, operands, shapes, parts, smem=1)
        return fields[:2], fields[2:], partial

    def crit(matrix, owns, nears, coef, partial, bases, lifts):
        far_face = (face + (2 if matrix is flex_mat else 1) * FAR_ROWS, width)
        operands = [flags, matrix, *owns, *nears, select, coef, partial, *bases, *lifts]
        shapes = [one_face] * (4 if lifts else 2) + [far_face] * 2
        kernel = functools.partial(crit_kernel, bool(bases), bool(lifts))
        *fields, a2, a3 = call(kernel, operands, shapes, parts, smem=1, flops=CRIT_FLOPS)
        return fields[:2], fields[2:], (a2, a3)

    def fields_of(matrix, owns, nears, coef, bases=(), lifts=(), beside=None):
        v01, q01, partial = early(matrix, owns[:2], nears[:2], coef, bases[:2], lifts)
        if beside is not None:
            partial, coef, made = beside(partial, coef)
        v23, q23, a23 = crit(matrix, owns[2:], nears[2:], coef, partial, bases[2:], lifts)
        fields = (*v01, *v23), (*q01, *q23), a23, partial
        return fields if beside is None else (*fields, made)

    def prec_late(values, a23, partial):
        operands = [flags, prec_mat, *values, *a23, partial]
        a0, a1, dots = call(prec_late_kernel, operands, [one_face, one_face, (1, width)], parts, smem=1)
        return (a0, a1, *a23), dots

    def flex_late(values, a23, partial, carried, other=()):
        operands = [flags, flex_mat, *values, *a23, *other, partial, coupling_mat, carried]
        kernel = functools.partial(flex_late_kernel, int(bool(other)))
        a0, a1, sums = call(kernel, operands, [one_face, (face + FAR_ROWS, width), (ncl + 8, width)], parts, smem=1)
        return (a0, a1, *a23), sums

    def solved(kernel, sums, faces, more):
        other, *far = lax.optimization_barrier((swapped(sums, "sy", 1), *faces[2:]))
        far = exchanged(far, "sy")
        close = faces[:2]
        parts, origins = [sums, other], [0, 1]
        for bit in bits_of("sy")[:0:-1]:
            rows = stacked_rows(parts)
            other, *close = lax.optimization_barrier((swapped(rows, "sy", bit), *close))
            parts = [rows, other]
            origins = origins + [at ^ bit for at in origins]
        origins = [block_of(at) for at in origins]
        spread = functools.partial(spread_kernel, ncl, table_rows, origins)
        (total,) = call(spread, [table, *parts], [step_shape])
        for bit in bits_of("sx"):
            total = total + swapped(total, "sx", bit)
        scratch = [pltpu.VMEM((ncoarse, ncoarse), F32)]
        kernel = functools.partial(kernel, table_rows)
        (result,) = call(kernel, [total, table, order, *more], [step_shape], scratch)
        return (*exchanged(close, "sx"), *far), total, result

    step_shape = (ncoarse + 8, width)
    extra = -(-face // width) * ncl
    copies = 4 * (1 + -(-face // width))
    sent = call(
        pack_kernel,
        [corners, load, coupling_mat],
        [(face + extra, width)] * 2 + [(face + extra + FAR_ROWS, width)] * 2,
        [pltpu.SemaphoreType.DMA((copies,))],
        smem=1,
        anywhere=(1, 2),
        limit=7 * LIMIT,
    )
    near = (*exchanged(sent[:2], "sx"), *exchanged(sent[2:], "sy"))

    own = coarse_inverse.shape[0]
    table_rows = own + 8
    inverse, flags, order, _ = lax.optimization_barrier((coarse_inverse, flags, order, sent[0]))
    (own_rows,) = call(rows_kernel, [corners, inverse], [(table_rows, ncoarse)], smem=1, flops=CRIT_FLOPS)

    def gather(partial, coef):
        rows, coef = lax.optimization_barrier((doubled(own_rows, steps_of()[:-1]), coef))
        return partial, coef, rows

    residual0, _, a23, partial, rows = fields_of(prec_mat, sent, near, one, beside=gather)
    applied0, rho0 = prec_late(residual0, a23, partial)
    (lift,) = call(
        lift_kernel, [flags, *near, select, coupling_mat, sent[0]], [(ni, ncoarse)], smem=1
    )
    table, half_one = lax.optimization_barrier((doubled(rows, steps_of()[-1:]), half_one))
    near = (*exchanged(applied0[:2], "sx"), *exchanged(applied0[2:], "sy"))

    direction0, _, a23, partial = fields_of(flex_mat, applied0, near, half_one)
    fine0, sums = flex_late(direction0, a23, partial, rho0)
    near, total0, result0 = solved(first_step_kernel, sums, fine0, [])
    lifts = (lift, result0[:ncoarse])
    residual1, image0, a23, partial = fields_of(prec_mat, fine0, near, result0[ncoarse:], residual0, lifts)
    applied1, rho1 = prec_late(residual1, a23, partial)
    near = (*exchanged(applied1[:2], "sx"), *exchanged(applied1[2:], "sy"))

    precond, _, a23, partial = fields_of(flex_mat, applied1, near, half_one)
    fine1, sums = flex_late(precond, a23, partial, rho1, fine0)
    near, _, result1 = solved(second_step_kernel, sums, fine1, [total0, result0])
    sol1, steps1 = result1[:ncoarse], result1[ncoarse:]

    def final(kernel, operands, smem=0):
        ends = [pltpu.VMEM((4, face, width), F32), pltpu.SemaphoreType.DMA((4,))]
        return call(kernel, operands, [(ni, width)], ends, smem=smem, out_spec=ANY_SPEC)[0]

    multipliers = final(weighted_kernel, [*direction0, *precond, steps1])
    operands = [flags, *fine1, *near, *residual1, *image0, select, lift, sol1, steps1]
    residual2 = final(tail_kernel, operands, smem=1)
    return multipliers[None, None], residual2[None, None]


def solution(mesh):
    return jax.shard_map(
        shards,
        mesh=mesh,
        in_specs=(
            P("sx", "sy", None, None),
            P("sx", "sy", None, None),
            P("sx", "sy", None, None),
            P("sx", "sy", None, None),
            P("sx", "sy", None),
            P("sx", "sy", None, None),
            P(("sx", "sy"), None),
        ),
        out_specs=(P("sx", "sy", None, None), P("sx", "sy", None, None)),
        check_vma=False,
    )
```

```python
import functools

import jax
import jax.numpy as jnp
from jax import lax
from jax.experimental import pallas as pl
from jax.experimental.pallas import tpu as pltpu
from jax.sharding import PartitionSpec as P

HIGHEST = lax.Precision.HIGHEST
F32 = jnp.float32
BF16 = jnp.bfloat16
LIMIT = 8 * 1024 * 1024
CRIT_FLOPS = 8 * 10**9
FAR_ROWS = 8


def swapped(block, axis, bit):
    return lax.ppermute(block, axis, [(i, i ^ bit) for i in range(lax.axis_size(axis))])


def swapped_between(block, axis):
    route = []
    for i in range(1, lax.axis_size(axis) - 1, 2):
        route += [(i, i + 1), (i + 1, i)]
    return lax.ppermute(block, axis, route)


def exchanged(slots, axis):
    between = swapped_between(slots[1], axis)
    return swapped(slots[0], axis, 1), between


def bits_of(axis):
    return [1 << i for i in range((lax.axis_size(axis) - 1).bit_length())]


def steps_of():
    return [("sy", 1)] + [("sx", bit) for bit in bits_of("sx")[::-1]] + [("sy", bit) for bit in bits_of("sy")[:0:-1]]


def stacked_rows(parts):
    count = parts[0].shape[0]
    total = count * len(parts)
    return sum(jnp.pad(p, ((at * count, total - (at + 1) * count), (0, 0))) for at, p in enumerate(parts))


def doubled(rows, steps):
    for axis, bit in steps:
        rows = stacked_rows([rows, swapped(rows, axis, bit)])
    return rows


def block_of(other):
    return sum(1 << at for at, (axis, bit) in enumerate(steps_of()) if axis == "sy" and other & bit)


def split(x):
    high = x.astype(BF16)
    return high, (x - high.astype(F32)).astype(BF16)


def dot(a, b):
    return jnp.dot(a, b, preferred_element_type=F32)


def product(a, b_high, b_low):
    a_high, a_low = split(a)
    return dot(a_high, b_high) + (dot(a_high, b_low) + dot(a_low, b_high))


def thirds(x):
    high = x.astype(BF16)
    rest = x - high.astype(F32)
    mid = rest.astype(BF16)
    return high, mid, (rest - mid.astype(F32)).astype(BF16)


def permuted(select, rows):
    high, mid, low = thirds(rows)
    return dot(select, high) + (dot(select, mid) + dot(select, low))


def pair(flag, first, second):
    return jnp.where(flag == 1.0, second, first), jnp.where(flag == 1.0, first, second)


def faces_of(flags, slots):
    return (*pair(flags[4], slots[0], slots[1]), *pair(flags[5], slots[2], slots[3]))


def pack_kernel(corners, load, coupling, *refs):
    outs, sems = refs[:4], refs[4]
    face = load.shape[0] // 4
    width = load.shape[1]
    ncl = coupling.shape[0]
    even = [1 - lax.axis_index("sx") % 2, 1 - lax.axis_index("sy") % 2]
    faces = [even[0], 1 - even[0], 2 + even[1], 3 - even[1]]
    copies = []

    def copy(source, target):
        copies.append(pltpu.make_async_copy(source, target, sems.at[len(copies)]))
        copies[-1].start()

    for slot in (3, 2, 0, 1):
        first = pl.multiple_of(faces[slot] * face, 128)
        out = outs[slot]
        copy(load.at[pl.ds(first, face)], out.at[pl.ds(0, face)])
        for block, at in enumerate(range(0, face, width)):
            wide = min(width, face - at)
            source = coupling.at[:, pl.ds(pl.multiple_of(first + at, 128), wide)]
            copy(source, out.at[pl.ds(face + block * ncl, ncl), pl.ds(0, wide)])
    start = face + (face // width) * ncl
    for out in outs:
        for k in range(ncl):
            listed = jnp.full((1, width - face % width), corners[k].astype(F32))
            out[start + k : start + k + 1, face % width :] = listed
        if out.shape[0] > start + ncl:
            out[start + ncl :] = jnp.zeros((out.shape[0] - start - ncl, width), F32)
    for started in copies:
        started.wait()


def rows_kernel(corners, inverse, out):
    own = inverse.shape[0]
    out[:own] = inverse[...]
    out[own:] = jnp.zeros((out.shape[0] - own, out.shape[1]), F32)
    columns = lax.broadcasted_iota(jnp.int32, (1, out.shape[1]), 1)
    listed = jnp.zeros((1, out.shape[1]), F32)
    for k in range(corners.shape[0]):
        listed = jnp.where(columns == k, corners[k].astype(F32), listed)
    out[own : own + 1] = listed


def lift_kernel(flags, near0, near1, near2, near3, select, coupling, sent, out):
    face = out.shape[0] // 4
    ncoarse = out.shape[1]
    ncl = coupling.shape[0]
    ids = lax.broadcasted_iota(jnp.int32, (ncl, ncoarse), 1).astype(F32)
    own_pick = (sent[sent.shape[0] - ncl :, sent.shape[1] - 1 :] == ids).astype(F32)
    end = near0.shape[0]
    nears = faces_of(flags, [near[face:end] for near in (near0, near1, near2, near3)])
    for f, near in enumerate(nears):
        columns = jnp.concatenate([near[at : at + ncl] for at in range(0, near.shape[0], ncl)], axis=1)
        near_pick = (columns[:, columns.shape[1] - 1 :] == ids).astype(F32)
        own = jnp.dot(coupling[:, f * face : (f + 1) * face].T, own_pick, precision=HIGHEST)
        theirs = jnp.dot(columns[:, :face].T, near_pick, precision=HIGHEST)
        out[f * face : (f + 1) * face] = own - permuted(select[f], theirs)


def field_into(at, owns, nears, select, flags, coef, bases, lifts, outs, images, high, low):
    size = outs[0].shape[0]
    if lifts:
        lift, sol = lifts
        corrections = product(lift[at * size : (at + 2) * size], *split(sol[...]))
    owns = pair(flags[4 + at // 2], *(own[:size] for own in owns))
    nears = pair(flags[4 + at // 2], *(near[:size] for near in nears))
    for f in range(2):
        image = owns[f] - permuted(select[at + f], nears[f])
        rows = slice(f * size, (f + 1) * size)
        if lifts:
            image = image + corrections[rows]
        if images:
            images[f][...] = image
        value = coef[0:1] * image
        if bases:
            value = bases[f][...] + value
        outs[f][...] = value
        high[rows], low[rows] = split(flags[at + f] * value)


def take(refs, *counts):
    groups = []
    for count in counts:
        groups.append(refs[:count])
        refs = refs[count:]
    return (*groups, refs)


def early_kernel(based, lifted, *refs):
    (flags, mat), owns, nears, (select, coef), bases, lifts, outs, images, rest = take(
        refs, 2, 2, 2, 2, 2 * based, 2 * lifted, 2, 2 * lifted
    )
    partial, high, low = rest
    field_into(0, owns, nears, select, flags, coef, bases, lifts, outs, images, high, low)
    half = high.shape[0]
    for rows in (slice(0, half), slice(half, 2 * half)):
        partial[rows] = product(mat[rows, :half], high[...], low[...])


def crit_kernel(based, lifted, *refs):
    (flags, mat), owns, nears, (select, coef, partial), bases, lifts, outs, images, rest = take(
        refs, 2, 2, 2, 3, 2 * based, 2 * lifted, 2, 2 * lifted
    )
    slot2, slot3, high, low = rest
    field_into(2, owns, nears, select, flags, coef, bases, lifts, outs, images, high, low)
    half = high.shape[0]
    size = half // 2
    value = partial[half:] + product(mat[half:, half:], high[...], low[...])
    slot3[:size], slot2[:size] = pair(flags[5], value[size:], value[:size])
    for slot in (slot2, slot3):
        slot[size:] = jnp.zeros((slot.shape[0] - size, slot.shape[1]), F32)


def late_rows(flags, mat, values, partial, high, low, slots):
    size = values[0].shape[0]
    for f in (2, 3):
        rows = slice((f - 2) * size, (f - 1) * size)
        high[rows], low[rows] = split(flags[f] * values[f][...])
    value = partial[: 2 * size] + product(mat[: 2 * size, 2 * size :], high[...], low[...])
    slots[1][:size], slots[0][...] = pair(flags[4], value[size:], value[:size])
    rest = slots[1].shape[0] - size
    if rest:
        slots[1][size:] = jnp.zeros((rest, slots[1].shape[1]), F32)
    return faces_of(flags, [slot[:size] for slot in slots])


def inner(flags, values, others):
    return sum(jnp.sum(flags[f] * values[f][...] * others[f], axis=0, keepdims=True) for f in range(4))


def prec_late_kernel(*refs):
    (flags, mat), values, applied, (partial, slot0, slot1, dots, high, low) = take(refs, 2, 4, 2)
    dots[...] = inner(flags, values, late_rows(flags, mat, values, partial, high, low, (slot0, slot1, *applied)))


def flex_late_kernel(others, *refs):
    (flags, mat), values, applied, other, rest = take(refs, 2, 4, 2, 4 * others)
    partial, coupling, carried, slot0, slot1, sums, high, low = rest
    size = slot0.shape[0]
    ncl = coupling.shape[0]
    coarse = None
    for f in range(4):
        term = product(coupling[:, f * size : (f + 1) * size], *split(flags[f] * values[f][...]))
        coarse = term if coarse is None else coarse + term
    faces = late_rows(flags, mat, values, partial, high, low, (slot0, slot1, *applied))
    rows = [inner(flags, values, faces), carried[...]]
    if others:
        rows.append(inner(flags, values, faces_of(flags, [slot[:size] for slot in other])))
    sums[:ncl] = coarse
    for at, row in enumerate(rows):
        sums[ncl + at : ncl + at + 1] = row
    end = ncl + len(rows)
    sums[end:] = jnp.zeros((sums.shape[0] - end, sums.shape[1]), F32)


def spread_kernel(ncl, rows, origins, table, *refs):
    parts, out = refs[:-1], refs[-1]
    ncoarse = out.shape[0] - 8
    ids = lax.broadcasted_iota(jnp.int32, (ncoarse, ncl), 0).astype(F32)
    size = ncl + 8
    each = parts[0].shape[0] // size
    coarse, dots = None, None
    for at, origin in enumerate(origins):
        start = origin * rows + rows - 8
        pick = (ids == table[start : start + 1, :ncl]).astype(BF16)
        values = parts[at // each][at % each * size : (at % each + 1) * size]
        term = permuted(pick, values[:ncl])
        coarse = term if coarse is None else coarse + term
        dots = values[ncl:] if dots is None else dots + values[ncl:]
    out[:ncoarse] = coarse
    out[ncoarse:] = dots


def inverse_from(table, rows, matrix):
    own = rows - 8
    for at in range(table.shape[0] // rows):
        matrix[at * own : (at + 1) * own] = table[at * rows : at * rows + own]


def first_step_kernel(rows, total, table, order, out, matrix):
    ncoarse = matrix.shape[0]
    inverse_from(table, rows, matrix)
    rhs = total[:ncoarse]
    sol = permuted(order[...], jnp.dot(matrix[...], rhs, precision=HIGHEST))
    fine_dot = total[ncoarse : ncoarse + 1]
    rho = 0.5 * total[ncoarse + 1 : ncoarse + 2]
    curve = fine_dot + jnp.sum(rhs * sol, axis=0, keepdims=True)
    out[:ncoarse] = sol
    out[ncoarse : ncoarse + 1] = -rho / curve
    out[ncoarse + 1 : ncoarse + 2] = rho
    out[ncoarse + 2 : ncoarse + 3] = fine_dot
    out[ncoarse + 3 :] = jnp.zeros((out.shape[0] - ncoarse - 3, out.shape[1]), F32)


def second_step_kernel(rows, total, table, order, total0, out0, out, matrix):
    ncoarse = matrix.shape[0]
    inverse_from(table, rows, matrix)
    rhs = total[:ncoarse]
    sol = permuted(order[...], jnp.dot(matrix[...], rhs, precision=HIGHEST))
    dot11, rho1, dot10 = (total[ncoarse + row : ncoarse + row + 1] for row in range(3))
    minus_step0, rho0, dot00 = (out0[ncoarse + row : ncoarse + row + 1] for row in range(3))
    rho1 = 0.5 * rho1
    beta = rho1 / rho0
    coarse = jnp.sum((rhs + beta * total0[:ncoarse]) * (sol + beta * out0[:ncoarse]), axis=0, keepdims=True)
    step1 = rho1 / (dot11 + 2.0 * beta * dot10 + beta * beta * dot00 + coarse)
    out[:ncoarse] = sol
    out[ncoarse : ncoarse + 1] = -step1
    out[ncoarse + 1 : ncoarse + 2] = -step1 * beta
    out[ncoarse + 2 : ncoarse + 3] = step1 * beta - minus_step0
    out[ncoarse + 3 : ncoarse + 4] = step1
    out[ncoarse + 4 :] = jnp.zeros((out.shape[0] - ncoarse - 4, out.shape[1]), F32)


def stored(values, out, sems):
    size = values.shape[1]
    return [
        pltpu.make_async_copy(values.at[f], out.at[pl.ds(f * size, size)], sems.at[f]) for f in range(4)
    ]


def tail_kernel(*refs):
    (flags,), owns, nears, residuals, images, firsts, seconds, rest = take(refs, 1, 4, 4, 4, 4, 4, 4)
    select, lift, sol, steps, weighted_out, out, weighted, values, weighted_sems, sems = rest
    weighted_stores = stored(weighted, weighted_out, weighted_sems)
    stores = stored(values, out, sems)
    for f in range(4):
        weighted[f] = steps[2:3] * firsts[f][...] + steps[3:4] * seconds[f][...]
        weighted_stores[f].start()
    parts = split(sol[...])
    size = values.shape[1]
    owns = faces_of(flags, [own[:size] for own in owns])
    nears = faces_of(flags, [near[:size] for near in nears])
    for f in range(4):
        image = owns[f] - permuted(select[f], nears[f]) + product(lift[f * size : (f + 1) * size], *parts)
        values[f] = residuals[f][...] + steps[0:1] * image + steps[1:2] * images[f][...]
        stores[f].start()
    for copy in weighted_stores + stores:
        copy.wait()


VMEM_SPEC = pl.BlockSpec(memory_space=pltpu.VMEM)
SMEM_SPEC = pl.BlockSpec(memory_space=pltpu.SMEM)
ANY_SPEC = pl.BlockSpec(memory_space=pl.ANY)


def call(kernel, operands, shapes, scratch=(), smem=0, anywhere=(), out_spec=VMEM_SPEC, flops=1024, limit=LIMIT):
    return pl.pallas_call(
        kernel,
        in_specs=[SMEM_SPEC if i < smem else ANY_SPEC if i in anywhere else VMEM_SPEC for i in range(len(operands))],
        out_specs=[out_spec] * len(shapes),
        out_shape=[jax.ShapeDtypeStruct(s, F32) for s in shapes],
        scratch_shapes=list(scratch),
        compiler_params=pltpu.CompilerParams(vmem_limit_bytes=limit),
        cost_estimate=pl.CostEstimate(flops=flops, bytes_accessed=1024, transcendentals=0),
    )(*operands)


def shards(loads, schur_flex, dirichlet, coupling, corner_index, face_lists, coarse_inverse):
    flex_mat = schur_flex[0, 0]
    prec_mat = dirichlet[0, 0]
    coupling_mat = coupling[0, 0]
    corners = corner_index[0, 0]
    face_index = face_lists[0, 0]
    load = loads[0, 0]
    ncoarse = coarse_inverse.shape[1]
    ncl, ni = coupling_mat.shape
    width = load.shape[1]
    face, half = ni // 4, ni // 2
    n_sx, n_sy = lax.axis_size("sx"), lax.axis_size("sy")
    at_x, at_y = lax.axis_index("sx"), lax.axis_index("sy")
    count = n_sx * n_sy

    has = jnp.stack([at_x > 0, at_x < n_sx - 1, at_y > 0, at_y < n_sy - 1])
    even = jnp.stack([at_x, at_y]) % 2 == 0
    flags = jnp.concatenate([jnp.where(has, 2.0, 1.0), jnp.where(even, 1.0, 0.0)]).astype(F32)
    select = (face_index[:, :, None] == jnp.arange(face, dtype=jnp.int32)).astype(BF16)
    coarse_ids = jnp.arange(ncoarse, dtype=jnp.int32)
    block = coarse_ids // (ncoarse // (n_sx * n_sy))
    origin = jnp.zeros_like(block)
    for at, (axis, bit) in enumerate(steps_of()):
        weight = bit * n_sy if axis == "sx" else bit
        origin = origin + ((block >> at) & 1) * weight
    origin = origin ^ (at_x * n_sy + at_y)
    within = coarse_ids % (ncoarse // (n_sx * n_sy))
    order = (origin * (ncoarse // (n_sx * n_sy)) + within)[None, :] == coarse_ids[:, None]
    order = order.astype(BF16)
    one_face = (face, width)
    parts = [pltpu.VMEM((half, width), BF16)] * 2
    one, select, order, flags = lax.optimization_barrier((jnp.ones((1, width), F32), select, order, flags))
    half_one = jnp.full((1, width), 0.5, F32)

    def early(matrix, owns, nears, coef, bases, lifts):
        operands = [flags, matrix, *owns, *nears, select, coef, *bases, *lifts]
        shapes = [one_face] * (4 if lifts else 2) + [(ni, width)]
        kernel = functools.partial(early_kernel, bool(bases), bool(lifts))
        *fields, partial = call(kernel, operands, shapes, parts, smem=1)
        return fields[:2], fields[2:], partial

    def crit(matrix, owns, nears, coef, partial, bases, lifts):
        far_face = (face + (2 if matrix is flex_mat else 1) * FAR_ROWS, width)
        operands = [flags, matrix, *owns, *nears, select, coef, partial, *bases, *lifts]
        shapes = [one_face] * (4 if lifts else 2) + [far_face] * 2
        kernel = functools.partial(crit_kernel, bool(bases), bool(lifts))
        *fields, a2, a3 = call(kernel, operands, shapes, parts, smem=1, flops=CRIT_FLOPS)
        return fields[:2], fields[2:], (a2, a3)

    def fields_of(matrix, owns, nears, coef, bases=(), lifts=(), beside=None):
        v01, q01, partial = early(matrix, owns[:2], nears[:2], coef, bases[:2], lifts)
        if beside is not None:
            partial, coef, made = beside(partial, coef)
        v23, q23, a23 = crit(matrix, owns[2:], nears[2:], coef, partial, bases[2:], lifts)
        fields = (*v01, *v23), (*q01, *q23), a23, partial
        return fields if beside is None else (*fields, made)

    def prec_late(values, a23, partial):
        operands = [flags, prec_mat, *values, *a23, partial]
        a0, a1, dots = call(prec_late_kernel, operands, [one_face, one_face, (1, width)], parts, smem=1)
        return (a0, a1, *a23), dots

    def flex_late(values, a23, partial, carried, other=()):
        operands = [flags, flex_mat, *values, *a23, *other, partial, coupling_mat, carried]
        kernel = functools.partial(flex_late_kernel, int(bool(other)))
        a0, a1, sums = call(kernel, operands, [one_face, (face + FAR_ROWS, width), (ncl + 8, width)], parts, smem=1)
        return (a0, a1, *a23), sums

    def solved(kernel, sums, faces, more):
        other, *far = lax.optimization_barrier((swapped(sums, "sy", 1), *faces[2:]))
        far = exchanged(far, "sy")
        close = faces[:2]
        parts, origins = [sums, other], [0, 1]
        for bit in bits_of("sy")[:0:-1]:
            rows = stacked_rows(parts)
            other, *close = lax.optimization_barrier((swapped(rows, "sy", bit), *close))
            parts = [rows, other]
            origins = origins + [at ^ bit for at in origins]
        origins = [block_of(at) for at in origins]
        spread = functools.partial(spread_kernel, ncl, table_rows, origins)
        (total,) = call(spread, [table, *parts], [step_shape])
        for bit in bits_of("sx"):
            total = total + swapped(total, "sx", bit)
        scratch = [pltpu.VMEM((ncoarse, ncoarse), F32)]
        kernel = functools.partial(kernel, table_rows)
        (result,) = call(kernel, [total, table, order, *more], [step_shape], scratch)
        return (*exchanged(close, "sx"), *far), total, result

    step_shape = (ncoarse + 8, width)
    extra = -(-face // width) * ncl
    copies = 4 * (1 + -(-face // width))
    sent = call(
        pack_kernel,
        [corners, load, coupling_mat],
        [(face + extra, width)] * 2 + [(face + extra + FAR_ROWS, width)] * 2,
        [pltpu.SemaphoreType.DMA((copies,))],
        smem=1,
        anywhere=(1, 2),
        limit=7 * LIMIT,
    )
    near = (*exchanged(sent[:2], "sx"), *exchanged(sent[2:], "sy"))

    own = coarse_inverse.shape[0]
    table_rows = own + 8
    inverse, flags, order, _ = lax.optimization_barrier((coarse_inverse, flags, order, sent[0]))
    (own_rows,) = call(rows_kernel, [corners, inverse], [(table_rows, ncoarse)], smem=1, flops=CRIT_FLOPS)

    def gather(partial, coef):
        rows, coef = lax.optimization_barrier((doubled(own_rows, steps_of()[:-1]), coef))
        return partial, coef, rows

    residual0, _, a23, partial, rows = fields_of(prec_mat, sent, near, one, beside=gather)
    applied0, rho0 = prec_late(residual0, a23, partial)
    (lift,) = call(
        lift_kernel, [flags, *near, select, coupling_mat, sent[0]], [(ni, ncoarse)], smem=1
    )
    table, half_one = lax.optimization_barrier((doubled(rows, steps_of()[-1:]), half_one))
    near = (*exchanged(applied0[:2], "sx"), *exchanged(applied0[2:], "sy"))

    direction0, _, a23, partial = fields_of(flex_mat, applied0, near, half_one)
    fine0, sums = flex_late(direction0, a23, partial, rho0)
    near, total0, result0 = solved(first_step_kernel, sums, fine0, [])
    lifts = (lift, result0[:ncoarse])
    residual1, image0, a23, partial = fields_of(prec_mat, fine0, near, result0[ncoarse:], residual0, lifts)
    applied1, rho1 = prec_late(residual1, a23, partial)
    near = (*exchanged(applied1[:2], "sx"), *exchanged(applied1[2:], "sy"))

    precond, _, a23, partial = fields_of(flex_mat, applied1, near, half_one)
    fine1, sums = flex_late(precond, a23, partial, rho1, fine0)
    near, _, result1 = solved(second_step_kernel, sums, fine1, [total0, result0])
    sol1, steps1 = result1[:ncoarse], result1[ncoarse:]

    ends = [pltpu.VMEM((4, face, width), F32)] * 2 + [pltpu.SemaphoreType.DMA((4,))] * 2
    operands = [flags, *fine1, *near, *residual1, *image0, *direction0, *precond, select, lift, sol1, steps1]
    multipliers, residual2 = call(tail_kernel, operands, [(ni, width)] * 2, ends, smem=1, out_spec=ANY_SPEC)
    return multipliers[None, None], residual2[None, None]


def solution(mesh):
    return jax.shard_map(
        shards,
        mesh=mesh,
        in_specs=(
            P("sx", "sy", None, None),
            P("sx", "sy", None, None),
            P("sx", "sy", None, None),
            P("sx", "sy", None, None),
            P("sx", "sy", None),
            P("sx", "sy", None, None),
            P(("sx", "sy"), None),
        ),
        out_specs=(P("sx", "sy", None, None), P("sx", "sy", None, None)),
        check_vma=False,
    )
```
